32 devices in a mesh: groups: 2 (over x), fsdp: 16 (over z, y, core).
Axes of the slice: x: 2, y: 2, z: 4, core: 2. Of those that a mesh axis runs over, the one named last changes fastest.
Arguments:
- token_ids: int32 [768], P('groups'), parts along dimension 0, may hold values from 0 to 9599
- key_value_of_block: int32 [8], replicated, may hold values from 0 to 7, each once
- vocab_table: bfloat16 [9600, 5120], P('fsdp'), may hold values from -50 to 50, as said below
- in_gain: float32 [5120], replicated, may hold values from 0.25 to 1.75
- q_gain: float32 [128], replicated, may hold values from 0.25 to 1.75
- k_gain: float32 [128], replicated, may hold values from 0.25 to 1.75
- wq_codes: bfloat16 [5120, 8192], P('fsdp'), may hold values from -0.078125 to 0.078125
- wq_scale: float32 [40, 64], replicated, may hold values from 0.5 to 2
- key_value_codes: bfloat16 [5120, 2048], P('fsdp'), may hold values from -0.078125 to 0.078125
- key_value_scale: float32 [40, 16], replicated, may hold values from 0.5 to 2
- wo_codes: bfloat16 [8192, 5120], P(None, 'fsdp'), may hold values from -0.75 to 0.75
- wo_scale: float32 [64, 40], replicated, may hold values from 0.5 to 2
Outputs:
- attn_out: bfloat16 [768, 5120], P(('groups', 'fsdp')), parts along dimension 0
- synced_keys: bfloat16 [32, 5120, 128], P(('groups', 'fsdp')), parts along dimension 0
The draws below stay inside these ranges and needn't reach their ends.
There are 2 independent parts, one for each index of `groups`. The reference program is written for one: setup_inputs(seed, part) draws one part's arguments, and reference() takes and returns one part's arrays. A program takes and returns all parts, laid end to end along the dimension named above; an argument that names none is the same for every part. Nothing has to cross between parts.
Inputs may be any that keep to these rules, and one draw needn't show every extreme that they name: `key_value_of_block`: each of the 8 key-value heads appears exactly once. `vocab_table`: rows of very different sizes.
All inputs are finite; a program needn't handle non-finite values.
Results may differ from the reference program's by a relative error of at most 0.0095.
Values may be sent and summed in bfloat16 or wider, within the bound.
No kernel may reach another device: no remote copies, remote signals or barrier semaphores. Data moves between devices by JAX's collectives and lax.ppermute only.
A program may use at most 128 MiB of HBM per device.

```python
import math
import jax
import jax.numpy as jnp
import numpy as np
from jax import lax

MODEL_WIDTH = 5120
QUERY_HEADS = 64
KEY_VALUE_HEADS = 8
HEAD_SIZE = 128
TILE_SIDE = 128
LEN = 384
PROMPTS = 1
TOKEN_TOTAL = 384
VOCAB = 9600
DUP = 2


def draw_vocab_table(key, part):
    key = jax.random.fold_in(key, 11)
    row_key, value_key = jax.random.split(key)
    scales = jnp.exp(jax.random.uniform(row_key, (VOCAB, 1), jnp.float32, 0.0, math.log(10.0)))
    values = jnp.clip(jax.random.normal(value_key, (VOCAB, MODEL_WIDTH), jnp.float32), -5.0, 5.0)
    return (values * scales).astype(jnp.bfloat16)


def set_ends(entries, stream_key, smallest, top_value):
    place = [jax.random.randint(jax.random.fold_in(stream_key, axis), (), 0, length) for axis, length in enumerate(entries.shape)]
    widest = entries.shape.index(max(entries.shape))
    neighbour = place[:widest] + [(place[widest] + 1) % entries.shape[widest]] + place[widest + 1:]
    return entries.at[tuple(place)].set(smallest).at[tuple(neighbour)].set(top_value)


def level_of(key, dims, shards, smallest, high):
    gain, own = 1.0, jax.random.fold_in(key, 6)
    for axis_at, blocks in shards:
        heights = jnp.exp(jax.random.uniform(jax.random.fold_in(own, axis_at), (blocks,), jnp.float32, smallest / len(shards), high / len(shards)))
        gain = gain * jnp.repeat(heights, dims[axis_at] // blocks).reshape([-1 if axis == axis_at else 1 for axis in range(len(dims))])
    return gain


def rank_bounds(number_of, slope):
    weights = [(1 << 20) // math.isqrt(rank ** slope) + 1 for rank in range(1, number_of + 1)]
    spread = 1 + sum(weights) // (1 << 30)
    return np.cumsum(np.array([max(1, weight // spread) for weight in weights]))


def ranked_ids(rng, dims, amount, skew):
    listing = rank_bounds(amount, skew)
    lot = jax.random.randint(jax.random.fold_in(rng, 1), dims, 0, int(listing[amount - 1]))
    rank = jnp.searchsorted(jnp.asarray(listing, jnp.int32), lot, side="right")
    return jax.random.permutation(jax.random.fold_in(rng, 2), amount)[rank].astype(jnp.int32)


def noise(own_key, shape, width, limit, cuts=(), held_as=jnp.bfloat16):
    gain = level_of(own_key, shape, cuts, -0.22, 0.18) if cuts else 1.0
    values = jax.random.normal(own_key, shape, jnp.float32) * width * gain
    return jnp.minimum(jnp.maximum(values, -limit), limit).astype(held_as)


def setup_inputs(seed: int = 0, part: int = 0) -> dict:
    key_list = jax.random.split(jax.random.key(seed), 13)
    part_keys = jax.random.split(jax.random.fold_in(key_list[12], part), 13)
    token_ids = set_ends(ranked_ids(part_keys[0], (TOKEN_TOTAL,), VOCAB, 2), jax.random.fold_in(part_keys[0], 3), 0, VOCAB - 1).astype(jnp.int32)
    key_value_of_block = jax.random.permutation(key_list[1], KEY_VALUE_HEADS).astype(jnp.int32)
    vocab_table = draw_vocab_table(jax.random.fold_in(key_list[12], 71), part)
    in_gain = jnp.clip(1.0 + 0.15 * jax.random.normal(key_list[3], (MODEL_WIDTH,), jnp.float32), 0.25, 1.75)
    q_gain = jnp.clip(1.0 + 0.15 * jax.random.normal(key_list[4], (HEAD_SIZE,), jnp.float32), 0.25, 1.75)
    k_gain = jnp.clip(1.0 + 0.15 * jax.random.normal(key_list[5], (HEAD_SIZE,), jnp.float32), 0.25, 1.75)
    wq_codes = noise(key_list[6], (MODEL_WIDTH, QUERY_HEADS * HEAD_SIZE), MODEL_WIDTH ** -0.5, 0.078125, ((0, 16),))
    wq_scale = jnp.clip(jnp.exp(jax.random.uniform(key_list[7], (MODEL_WIDTH // TILE_SIDE, QUERY_HEADS * HEAD_SIZE // TILE_SIDE), jnp.float32, math.log(0.5), math.log(2.0))), 0.5, 2.0)
    key_value_codes = noise(key_list[8], (MODEL_WIDTH, 2 * KEY_VALUE_HEADS * HEAD_SIZE), MODEL_WIDTH ** -0.5, 0.078125, ((0, 16),))
    key_value_scale = jnp.clip(jnp.exp(jax.random.uniform(key_list[9], (MODEL_WIDTH // TILE_SIDE, 2 * KEY_VALUE_HEADS * HEAD_SIZE // TILE_SIDE), jnp.float32, math.log(0.5), math.log(2.0))), 0.5, 2.0)
    wo_codes = noise(key_list[10], (QUERY_HEADS * HEAD_SIZE, MODEL_WIDTH), QUERY_HEADS ** -0.5, 0.75, ((1, 16),))
    wo_scale = jnp.clip(jnp.exp(jax.random.uniform(key_list[11], (QUERY_HEADS * HEAD_SIZE // TILE_SIDE, MODEL_WIDTH // TILE_SIDE), jnp.float32, math.log(0.5), math.log(2.0))), 0.5, 2.0)
    return dict(token_ids=token_ids, key_value_of_block=key_value_of_block, vocab_table=vocab_table, in_gain=in_gain, q_gain=q_gain, k_gain=k_gain, wq_codes=wq_codes, wq_scale=wq_scale, key_value_codes=key_value_codes, key_value_scale=key_value_scale, wo_codes=wo_codes, wo_scale=wo_scale)


theta_base = 1000000.0
eps_norm = 1e-06

def rms_scale(values, norm_gain):
    mean_square = lax.optimization_barrier(jnp.mean(values * values, axis=-1, keepdims=True))
    return values * lax.rsqrt(mean_square + eps_norm) * norm_gain

def rotate(values, positions):
    half_width = values.shape[-1] // 2
    frequency = theta_base ** (-jnp.arange(half_width, dtype=jnp.float32) * 2.0 / values.shape[-1])
    angles = positions[:, None] * frequency[None, :]
    cosine = jnp.cos(angles)[:, None, :]
    sine_part = jnp.sin(angles)[:, None, :]
    lower_half = values[..., :half_width]
    upper_half = values[..., half_width:]
    return jnp.concatenate([lower_half * cosine - upper_half * sine_part, upper_half * cosine + lower_half * sine_part], axis=-1)

def dequantize(quantized, tile_scale):
    expanded = jnp.repeat(jnp.repeat(tile_scale, TILE_SIDE, axis=0), TILE_SIDE, axis=1)
    return (quantized.astype(jnp.float32) * expanded).astype(jnp.bfloat16)

def attend(queries, key_rows, value_rows, prompt_count):
    token_count, head_count, head_width = queries.shape
    length = token_count // prompt_count
    query_blocks = lax.optimization_barrier(queries).astype(jnp.float32).reshape(prompt_count, length, head_count, head_width)
    key_blocks = lax.optimization_barrier(key_rows).astype(jnp.float32).reshape(prompt_count, length, head_width)
    value_blocks = lax.optimization_barrier(value_rows).astype(jnp.float32).reshape(prompt_count, length, -1)
    scores = jnp.einsum('plhd,pmd->phlm', query_blocks, key_blocks) * head_width ** (-0.5)
    causal = jnp.arange(length)[:, None] >= jnp.arange(length)[None, :]
    weights = jnp.where(causal, jnp.exp(scores), 0.0)
    probabilities = (weights / lax.optimization_barrier(jnp.sum(weights, axis=-1, keepdims=True))).astype(jnp.bfloat16)
    probabilities = lax.optimization_barrier(probabilities).astype(jnp.float32)
    attended_rows = jnp.einsum('phlm,pmd->plhd', probabilities, value_blocks)
    return attended_rows.astype(jnp.bfloat16).reshape(token_count, head_count * value_blocks.shape[-1])

def reference(token_ids, key_value_of_block, vocab_table, in_gain, q_gain, k_gain, wq_codes, wq_scale, key_value_codes, key_value_scale, wo_codes, wo_scale):
    embedded = vocab_table[token_ids]
    normed = rms_scale(embedded.astype(jnp.float32), in_gain).astype(jnp.bfloat16)
    query_weight = dequantize(wq_codes, wq_scale)
    key_value_weight = dequantize(key_value_codes, key_value_scale)
    out_weight = dequantize(wo_codes, wo_scale)
    query_proj = jnp.dot(normed, query_weight, preferred_element_type=jnp.float32)
    key_value_projection = jnp.dot(normed, key_value_weight, preferred_element_type=jnp.float32)
    positions = (jnp.arange(TOKEN_TOTAL) % LEN).astype(jnp.float32)
    queries = rotate(rms_scale(query_proj.reshape(TOKEN_TOTAL, QUERY_HEADS, HEAD_SIZE), q_gain), positions).astype(jnp.bfloat16)
    key_value_heads = key_value_projection.reshape(TOKEN_TOTAL, KEY_VALUE_HEADS, 2, HEAD_SIZE)
    key_rows = rotate(rms_scale(key_value_heads[:, :, 0, :], k_gain), positions).astype(jnp.bfloat16)
    value_rows = key_value_heads[:, :, 1, :].astype(jnp.bfloat16)
    per_key_value = QUERY_HEADS // KEY_VALUE_HEADS

    def single_group(group_index):
        group_queries = lax.dynamic_slice_in_dim(queries, group_index * per_key_value, per_key_value, 1)
        group_keys = lax.dynamic_slice_in_dim(key_rows, group_index, 1, 1)[:, 0, :]
        group_values = lax.dynamic_slice_in_dim(value_rows, group_index, 1, 1)[:, 0, :]
        return attend(group_queries, group_keys, group_values, PROMPTS)
    attended_rows = lax.map(single_group, jnp.arange(KEY_VALUE_HEADS, dtype=jnp.int32))
    attended_rows = jnp.transpose(attended_rows, (1, 0, 2)).reshape(TOKEN_TOTAL, QUERY_HEADS * HEAD_SIZE)
    attn_out = jnp.dot(attended_rows, out_weight, preferred_element_type=jnp.float32).astype(jnp.bfloat16)
    key_matrix = jnp.transpose(key_value_weight.reshape(MODEL_WIDTH, KEY_VALUE_HEADS, 2, HEAD_SIZE)[:, :, 0, :], (1, 0, 2))
    synced_keys = jnp.take(key_matrix, jnp.repeat(key_value_of_block, DUP).astype(jnp.int32), axis=0)
    return (attn_out, synced_keys)
```

```python
import functools
import jax
import jax.numpy as jnp
from jax import lax
from jax.experimental import pallas as pl
from jax.experimental.pallas import tpu as pltpu
from jax.sharding import PartitionSpec as P
QUERY_HEADS = 64
KEY_VALUE_HEADS = 8
HEAD_SIZE = 128
TILE_SIDE = 128
LEN = 384


theta_base = 1000000.0
eps_norm = 1e-06


def rms_scale(values, norm_gain):
    mean_square = jnp.mean(values * values, axis=-1, keepdims=True)
    return values * lax.rsqrt(mean_square + eps_norm) * norm_gain


def rotate(values, positions):
    half_width = values.shape[-1] // 2
    frequency = theta_base ** (-jnp.arange(half_width, dtype=jnp.float32) * 2.0 / values.shape[-1])
    angles = positions[:, None] * frequency[None, :]
    cosine = jnp.cos(angles)[:, None, :]
    sine_part = jnp.sin(angles)[:, None, :]
    lower_half = values[..., :half_width]
    upper_half = values[..., half_width:]
    return jnp.concatenate(
        [
            lower_half * cosine - upper_half * sine_part,
            upper_half * cosine + lower_half * sine_part,
        ],
        axis=-1,
    )


def lookup_small(small_table, indices):
    matches = indices[..., None] == jnp.arange(small_table.shape[0], dtype=jnp.int32)
    return jnp.sum(jnp.where(matches, small_table, 0), axis=-1)


def column_scales(tile_scale, first_col, width_cols):
    per_column = jnp.repeat(tile_scale, TILE_SIDE, axis=1)
    picked = lax.dynamic_slice_in_dim(per_column, first_col, width_cols, 1)
    return jnp.repeat(picked, TILE_SIDE, axis=0)


def dequantize(quantized, scales):
    return (quantized.astype(jnp.float32) * scales).astype(jnp.bfloat16)


def attend(queries, key_rows, value_rows, prompt_count):
    token_count, head_count, head_width = queries.shape
    length = token_count // prompt_count
    query_blocks = queries.reshape(prompt_count, length, head_count, head_width)
    key_blocks = key_rows.reshape(prompt_count, length, head_width)
    value_blocks = value_rows.reshape(prompt_count, length, -1)
    scores = jnp.einsum(
        "plhd,pmd->phlm", query_blocks, key_blocks, preferred_element_type=jnp.float32
    ) * head_width ** (-0.5)
    causal = jnp.arange(length)[:, None] >= jnp.arange(length)[None, :]
    weights = jnp.where(causal, jnp.exp(scores), 0.0)
    probabilities = (weights / jnp.sum(weights, axis=-1, keepdims=True)).astype(jnp.bfloat16)
    attended_rows = jnp.einsum(
        "phlm,pmd->plhd", probabilities, value_blocks, preferred_element_type=jnp.float32
    )
    return attended_rows.astype(jnp.bfloat16).reshape(
        token_count, head_count * value_blocks.shape[-1]
    )


def general_plan(
    token_ids,
    key_value_of_block,
    vocab_table,
    in_gain,
    q_gain,
    k_gain,
    wq_codes,
    wq_scale,
    key_value_codes,
    key_value_scale,
    wo_codes,
    wo_scale,
):
    count_of_ranks = lax.axis_size("fsdp")
    my_rank = lax.axis_index("fsdp")
    duplicate_count = count_of_ranks // KEY_VALUE_HEADS
    per_key_value = QUERY_HEADS // KEY_VALUE_HEADS
    split_points = max(1, duplicate_count // per_key_value)
    heads_here = max(1, per_key_value // duplicate_count)
    value_columns = HEAD_SIZE // split_points
    query_width = heads_here * HEAD_SIZE
    local_rows = wq_codes.shape[0]
    token_count = token_ids.shape[0]
    targets = jnp.arange(count_of_ranks, dtype=jnp.int32)
    target_head = lookup_small(key_value_of_block, targets // duplicate_count)
    target_slot = targets % duplicate_count
    target_part = target_slot % split_points
    target_query = target_head * per_key_value + target_slot // split_points * heads_here
    my_head = lookup_small(key_value_of_block, my_rank // duplicate_count)
    my_slot = my_rank % duplicate_count
    my_part = my_slot % split_points
    my_query = my_head * per_key_value + my_slot // split_points * heads_here
    vocab_rows = vocab_table.shape[0]
    local_ids = token_ids - my_rank * vocab_rows
    inside = (local_ids >= 0) & (local_ids < vocab_rows)
    picked = jnp.take(vocab_table, jnp.clip(local_ids, 0, vocab_rows - 1), axis=0)
    terms = jnp.where(inside[:, None], picked, jnp.zeros_like(picked)).astype(jnp.float32)
    embedded = lax.psum(terms, "fsdp").astype(jnp.bfloat16)
    normed = rms_scale(embedded.astype(jnp.float32), in_gain).astype(jnp.bfloat16)
    query_groups = wq_codes.reshape(local_rows, QUERY_HEADS // heads_here, query_width)
    query_send = jnp.take(query_groups, target_query // heads_here, axis=1)
    key_value_heads = key_value_codes.reshape(local_rows, KEY_VALUE_HEADS, 2, HEAD_SIZE)
    key_send = jnp.take(key_value_heads[:, :, 0, :], target_head, axis=1)
    grouped_values = key_value_heads[:, :, 1, :].reshape(
        local_rows, KEY_VALUE_HEADS * split_points, value_columns
    )
    value_send = jnp.take(grouped_values, target_head * split_points + target_part, axis=1)
    both_send = jnp.concatenate([key_send, value_send], axis=2)
    query_got, kv_got = (
        lax.all_to_all(query_send, "fsdp", split_axis=1, concat_axis=0, tiled=True),
        lax.all_to_all(both_send, "fsdp", split_axis=1, concat_axis=0, tiled=True),
    )
    key_quant = kv_got[:, 0, :HEAD_SIZE]
    value_quant = kv_got[:, 0, HEAD_SIZE:]
    query_weight = dequantize(
        query_got[:, 0, :], column_scales(wq_scale, my_query * HEAD_SIZE, query_width)
    )
    key_matrix = dequantize(
        key_quant, column_scales(key_value_scale, my_head * 2 * HEAD_SIZE, HEAD_SIZE)
    )
    value_weight = dequantize(
        value_quant,
        column_scales(
            key_value_scale,
            my_head * 2 * HEAD_SIZE + HEAD_SIZE + my_part * value_columns,
            value_columns,
        ),
    )
    joined_weight = jnp.concatenate([query_weight, key_matrix, value_weight], axis=1)
    projected = jnp.dot(normed, joined_weight, preferred_element_type=jnp.float32)
    positions = (jnp.arange(token_count) % LEN).astype(jnp.float32)
    queries = rotate(
        rms_scale(projected[:, :query_width].reshape(token_count, heads_here, HEAD_SIZE), q_gain),
        positions,
    ).astype(jnp.bfloat16)
    keys_raw = projected[:, query_width : query_width + HEAD_SIZE].reshape(
        token_count, 1, HEAD_SIZE
    )
    key_rows = rotate(rms_scale(keys_raw, k_gain), positions).astype(jnp.bfloat16)[:, 0, :]
    value_rows = projected[:, query_width + HEAD_SIZE :].astype(jnp.bfloat16)
    attended_rows = attend(queries, key_rows, value_rows, token_count // LEN)
    cols_here = wo_codes.shape[1]
    local_weight = dequantize(wo_codes, column_scales(wo_scale, my_rank * cols_here, cols_here))
    ordered = jnp.take(
        local_weight.reshape(KEY_VALUE_HEADS, per_key_value * HEAD_SIZE, cols_here),
        key_value_of_block,
        axis=0,
    ).reshape(QUERY_HEADS * HEAD_SIZE, cols_here)
    columns = jnp.dot(
        lax.all_gather(attended_rows, "fsdp", axis=1, tiled=True),
        ordered,
        preferred_element_type=jnp.float32,
    )
    attn_out = lax.all_to_all(
        columns.astype(jnp.bfloat16), "fsdp", split_axis=0, concat_axis=1, tiled=True
    )
    return (attn_out, key_matrix.reshape(1, key_matrix.shape[0], HEAD_SIZE))


BF = jnp.bfloat16
F32 = jnp.float32
SLOTS = 32
GROUP_ROWS = 64
PARAMS = pltpu.CompilerParams(vmem_limit_bytes=48 << 20)
SMEM = pl.BlockSpec(memory_space=pltpu.SMEM)


def cost(flops, bytes_accessed):
    return pl.CostEstimate(flops=flops, bytes_accessed=bytes_accessed, transcendentals=0)


def owner_of(ids, vocab_rows, ranks):
    owner = jnp.zeros_like(ids)
    for rank in range(1, ranks):
        owner = owner + jnp.where(ids >= float(rank * vocab_rows), 1.0, 0.0)
    return owner


def iota(shape, axis):
    return lax.broadcasted_iota(jnp.int32, shape, axis).astype(F32)


def slot_kernel(ranks, vocab_rows, info, id_col, id_row, col_out, row_out, most_out):
    count = id_col.shape[0]
    ids_c, ids_r = id_col[...].astype(F32), id_row[...].astype(F32)
    at_r, at_c = iota((count, count), 0), iota((count, count), 1)
    same = ids_c == ids_r
    first_c = jnp.min(jnp.where(same, at_c, float(count)), axis=1, keepdims=True)
    first_r = jnp.min(jnp.where(same, at_r, float(count)), axis=0, keepdims=True)
    is_first_r = first_r == iota((1, count), 1)
    is_first_c = first_c == iota((count, 1), 0)
    owner_c, owner_r = owner_of(ids_c, vocab_rows, ranks), owner_of(ids_r, vocab_rows, ranks)
    peers = owner_c == owner_r
    slot_c = jnp.sum(
        jnp.where(peers & is_first_r & (at_c < first_c), 1.0, 0.0), axis=1, keepdims=True
    )
    slot_r = jnp.sum(
        jnp.where(peers & is_first_c & (at_r < first_r), 1.0, 0.0), axis=0, keepdims=True
    )
    lane = lax.broadcasted_iota(jnp.int32, (count, 128), 1)
    col_out[...] = jnp.where(lane == 0, owner_c, jnp.where(lane == 1, slot_c, 0.0))
    me = info[0].astype(F32)
    mine = is_first_r & (owner_r == me)
    row_out[...] = jnp.zeros_like(row_out)
    row_out[0:1, :] = jnp.where(mine, slot_r, -1.0)
    row_out[1:2, :] = ids_r - me * float(vocab_rows)
    most_out[...] = jnp.broadcast_to(jnp.max(slot_r, axis=1, keepdims=True) + 1.0, (8, 128))


def find_slots(token_ids, my_rank, ranks, vocab_rows):
    count = token_ids.shape[0]
    return pl.pallas_call(
        functools.partial(slot_kernel, ranks, vocab_rows),
        out_shape=(
            jax.ShapeDtypeStruct((count, 128), F32),
            jax.ShapeDtypeStruct((8, count), F32),
            jax.ShapeDtypeStruct((8, 128), F32),
        ),
        in_specs=[SMEM, pl.BlockSpec(memory_space=pltpu.VMEM), pl.BlockSpec(memory_space=pltpu.VMEM)],
        compiler_params=PARAMS,
        cost_estimate=cost(1000000, 1000000),
        name="find_slots",
    )(my_rank.reshape(1), token_ids.reshape(count, 1), token_ids.reshape(1, count))


def pick_kernel(width, base, rows, gain, table, out, picked, total):
    step = pl.program_id(0)
    slots = picked.shape[0]
    vocab_rows = table.shape[0]
    wanted = lax.broadcasted_iota(jnp.int32, (slots, 1), 0).astype(F32) + base[0].astype(F32)
    chosen = wanted == rows[0:1, :]
    index = jnp.sum(jnp.where(chosen, rows[1:2, :], 0.0), axis=1, keepdims=True)
    valid = jnp.sum(jnp.where(chosen, 1.0, 0.0), axis=1, keepdims=True)
    hot = (iota((slots, vocab_rows), 1) == index) & (valid > 0.5)
    block = jnp.dot(hot.astype(F32).astype(BF), table[...], preferred_element_type=F32)
    picked[:, pl.ds(pl.multiple_of(step * width, width), width)] = block

    @pl.when(step == 0)
    def _():
        total[...] = jnp.zeros_like(total)

    total[...] += jnp.sum(block * block, axis=1, keepdims=True)

    @pl.when(step == pl.num_programs(0) - 1)
    def _():
        features = picked.shape[1]
        inverse = lax.rsqrt(total[:, 0:1] * (1.0 / features) + eps_norm)
        for part in range(features // width):
            span = slice(part * width, (part + 1) * width)
            out[part] = (picked[:, span] * inverse * gain[:, span]).astype(BF)


def pick_rows(rows, base, in_gain, vocab_table, chips):
    vocab_rows, features = vocab_table.shape
    width = features // chips
    return pl.pallas_call(
        functools.partial(pick_kernel, width),
        grid=(chips,),
        out_shape=jax.ShapeDtypeStruct((chips, SLOTS, width), BF),
        in_specs=[
            SMEM,
            pl.BlockSpec(rows.shape, lambda i: (0, 0)),
            pl.BlockSpec((1, features), lambda i: (0, 0)),
            pl.BlockSpec((vocab_rows, width), lambda i: (0, i)),
        ],
        out_specs=pl.BlockSpec((chips, SLOTS, width), lambda i: (0, 0, 0)),
        scratch_shapes=[pltpu.VMEM((SLOTS, features), F32), pltpu.VMEM((SLOTS, 128), F32)],
        compiler_params=PARAMS,
        cost_estimate=cost(2 * SLOTS * vocab_rows * features, 2 * vocab_rows * features),
        name="pick_rows",
    )(base.reshape(1), rows, in_gain.reshape(1, features), vocab_table)


def place_kernel(chips, info, owners, own, other, out):
    count = owners.shape[0]
    core, base = info[0].astype(F32), info[1].astype(F32)
    owner, slot = owners[:, 0:1], owners[:, 1:2] - base
    chip = jnp.zeros_like(owner)
    for number in range(1, chips):
        chip = chip + jnp.where(owner >= 2.0 * number, 1.0, 0.0)
    owner_core = owner - 2.0 * chip
    fits = (slot >= 0.0) & (slot < float(SLOTS))
    column = iota((count, chips * SLOTS), 1)
    hit = (column == chip * float(SLOTS) + slot) & fits
    hot_own = jnp.where(hit & (owner_core == core), 1.0, 0.0).astype(BF)
    hot_other = jnp.where(hit & (owner_core != core), 1.0, 0.0).astype(BF)
    picked = jnp.dot(hot_own, own[...], preferred_element_type=F32)
    picked += jnp.dot(hot_other, other[...], preferred_element_type=F32)
    out[...] = picked.astype(BF)


def place_rows(owners, base, core, own, other, chips):
    count = owners.shape[0]
    width = own.shape[-1]
    vmem = pl.BlockSpec(memory_space=pltpu.VMEM)
    return pl.pallas_call(
        functools.partial(place_kernel, chips),
        out_shape=jax.ShapeDtypeStruct((count, width), BF),
        in_specs=[SMEM, vmem, vmem, vmem],
        compiler_params=PARAMS,
        cost_estimate=cost(4 * count * chips * SLOTS * width, 6 * chips * SLOTS * width),
        name="place_rows",
    )(
        jnp.stack([core, base]),
        owners,
        own.reshape(chips * SLOTS, width),
        other.reshape(chips * SLOTS, width),
    )


def weight_kernel(info, head_of, wq_scale, kv_scale, wq, kv, kv_key, own, send, key_out):
    block = pl.program_id(0)
    core, rank = info[0], info[1]
    rows = wq.shape[0]
    half = wq.shape[1] // 2
    key_head = head_of[block]
    for group in range(rows // GROUP_ROWS):
        tile_row = (rank * (rows // GROUP_ROWS) + group) // 2
        span = slice(group * GROUP_ROWS, (group + 1) * GROUP_ROWS)
        for side, target in ((core, own), (1 - core, send)):
            for tile in range(half // TILE_SIDE):
                scale = wq_scale[tile_row, (2 * block + side) * (half // TILE_SIDE) + tile]
                start = pl.multiple_of(side * half + tile * TILE_SIDE, TILE_SIDE)
                codes = wq[span, pl.ds(start, TILE_SIDE)].astype(F32)
                target[0, span, tile * TILE_SIDE : (tile + 1) * TILE_SIDE] = (codes * scale).astype(BF)
            scale = kv_scale[tile_row, 2 * block + side]
            start = pl.multiple_of(side * TILE_SIDE, TILE_SIDE)
            codes = kv[span, pl.ds(start, TILE_SIDE)].astype(F32)
            target[0, span, half : half + TILE_SIDE] = (codes * scale).astype(BF)
        scale = kv_scale[tile_row, 2 * key_head]
        key_out[0, span, :] = (kv_key[span, :].astype(F32) * scale).astype(BF)


def prepare_weights(core, my_rank, key_value_of_block, wq_codes, wq_scale, kv_codes, kv_scale, chips):
    rows = wq_codes.shape[0]
    half = wq_codes.shape[1] // (2 * chips)
    out = jax.ShapeDtypeStruct((chips, rows, half + TILE_SIDE), BF)
    out_spec = pl.BlockSpec((1, rows, half + TILE_SIDE), lambda b, *_: (b, 0, 0))
    return pl.pallas_call(
        weight_kernel,
        grid_spec=pltpu.PrefetchScalarGridSpec(
            num_scalar_prefetch=4,
            grid=(chips,),
            in_specs=[
                pl.BlockSpec((rows, 2 * half), lambda b, *_: (0, b)),
                pl.BlockSpec((rows, 2 * TILE_SIDE), lambda b, *_: (0, b)),
                pl.BlockSpec((rows, TILE_SIDE), lambda b, info, head_of, *_: (0, 2 * head_of[b])),
            ],
            out_specs=[out_spec, out_spec, pl.BlockSpec((1, rows, TILE_SIDE), lambda b, *_: (b, 0, 0))],
        ),
        out_shape=[out, out, jax.ShapeDtypeStruct((chips, rows, TILE_SIDE), BF)],
        compiler_params=PARAMS,
        cost_estimate=cost(rows * wq_codes.shape[1] * 8, rows * wq_codes.shape[1] * 6),
        name="prepare_weights",
    )(
        jnp.stack([core, my_rank]),
        key_value_of_block,
        wq_scale,
        kv_scale,
        wq_codes,
        kv_codes,
        kv_codes,
    )


def project_kernel(info, normed, own, other, out, weight):
    rows = own.shape[1]
    core = info[0]
    weight[pl.ds(pl.multiple_of(core * rows, GROUP_ROWS), rows), :] = own[0]
    weight[pl.ds(pl.multiple_of((1 - core) * rows, GROUP_ROWS), rows), :] = other[0]
    out[0] = jnp.dot(normed[...], weight[...], preferred_element_type=F32).astype(out.dtype)


def project(core, y_side, normed, own, other, out_type, z_count):
    count, width = normed.shape
    chips, rows, columns = own.shape
    weight_spec = pl.BlockSpec(
        (1, rows, columns), lambda z, info: (z * (chips // z_count) + info[1], 0, 0)
    )
    return pl.pallas_call(
        project_kernel,
        grid_spec=pltpu.PrefetchScalarGridSpec(
            num_scalar_prefetch=1,
            grid=(z_count,),
            in_specs=[
                pl.BlockSpec((count, width), lambda z, info: (0, 0)),
                weight_spec,
                weight_spec,
            ],
            out_specs=pl.BlockSpec((1, count, columns), lambda z, info: (z, 0, 0)),
            scratch_shapes=[pltpu.VMEM((width, columns), BF)],
        ),
        out_shape=jax.ShapeDtypeStruct((z_count, count, columns), out_type),
        compiler_params=PARAMS,
        cost_estimate=cost(
            2 * z_count * count * width * columns, 2 * z_count * columns * (width + count)
        ),
        name="project",
    )(jnp.stack([core, y_side]), normed, own, other)


def join_kernel(own, got, out):
    out[...] = (own[...] + got[...].astype(F32)).astype(BF)


def join_partials(own, got, start):
    blocks, rows, columns = got.shape
    return pl.pallas_call(
        join_kernel,
        grid=(blocks,),
        in_specs=[
            pl.BlockSpec((1, rows, columns), lambda z: (z, start // rows, 0)),
            pl.BlockSpec((1, rows, columns), lambda z: (z, 0, 0)),
        ],
        out_specs=pl.BlockSpec((1, rows, columns), lambda z: (z, 0, 0)),
        out_shape=jax.ShapeDtypeStruct(got.shape, BF),
        compiler_params=PARAMS,
        cost_estimate=cost(2 * blocks * rows * columns, 8 * blocks * rows * columns),
        name="join_partials",
    )(own, got)


def turn(values, cosine, sine):
    return values * cosine + pltpu.roll(values, HEAD_SIZE // 2, 1) * sine


def normalise(values, gain):
    mean_square = jnp.mean(values * values, axis=-1, keepdims=True)
    return values * lax.rsqrt(mean_square + eps_norm) * gain


def heads_kernel(info, parts, q_gain, k_gain, cosine, sine, q_out, kv_out):
    total = parts[0].astype(F32)
    for source in range(1, parts.shape[0]):
        total = total + parts[source].astype(F32)
    heads = q_out.shape[0]
    cos, sin = cosine[...], sine[...]
    last = total[:, heads * HEAD_SIZE :]

    @pl.when(info[0] == 0)
    def _():
        kv_out[...] = turn(normalise(last, k_gain[...]), cos, sin).astype(BF)

    @pl.when(info[0] == 1)
    def _():
        kv_out[...] = last.astype(BF)

    for head in range(heads):
        values = total[:, head * HEAD_SIZE : (head + 1) * HEAD_SIZE]
        q_out[head] = turn(normalise(values, q_gain[...]), cos, sin).astype(BF)


def make_heads(core, parts, q_gain, k_gain, cosine, sine):
    sources, count, columns = parts.shape
    heads = columns // HEAD_SIZE - 1
    vmem = pl.BlockSpec(memory_space=pltpu.VMEM)
    return pl.pallas_call(
        heads_kernel,
        out_shape=(
            jax.ShapeDtypeStruct((heads, count, HEAD_SIZE), BF),
            jax.ShapeDtypeStruct((count, HEAD_SIZE), BF),
        ),
        in_specs=[SMEM] + [vmem] * 5,
        compiler_params=PARAMS,
        cost_estimate=cost(20 * count * columns, 2 * parts.size + 2 * count * columns),
        name="make_heads",
    )(core.reshape(1), parts, q_gain.reshape(1, -1), k_gain.reshape(1, -1), cosine, sine)


def attend_kernel(length, info, queries, own, other, out):
    first = info[0] == 0
    keys = jnp.where(first, own[...], other[...])
    values = jnp.where(first, other[...], own[...])
    count = keys.shape[0]
    here = lax.broadcasted_iota(jnp.int32, (count, count), 0)
    there = lax.broadcasted_iota(jnp.int32, (count, count), 1)
    allowed = here >= there
    for prompt in range(1, count // length):
        allowed = allowed & ((here < prompt * length) | (there >= prompt * length))
    for head in range(queries.shape[0]):
        scores = lax.dot_general(
            queries[head], keys, (((1,), (1,)), ((), ())), preferred_element_type=F32
        ) * HEAD_SIZE ** (-0.5)
        weights = jnp.where(allowed, jnp.exp(scores), 0.0)
        probabilities = (weights / jnp.sum(weights, axis=-1, keepdims=True)).astype(BF)
        out[:, head * HEAD_SIZE : (head + 1) * HEAD_SIZE] = jnp.dot(
            probabilities, values, preferred_element_type=F32
        ).astype(BF)


def attend_heads(core, queries, own, other):
    heads, count, width = queries.shape
    vmem = pl.BlockSpec(memory_space=pltpu.VMEM)
    return pl.pallas_call(
        functools.partial(attend_kernel, LEN),
        out_shape=jax.ShapeDtypeStruct((count, heads * width), BF),
        in_specs=[SMEM, vmem, vmem, vmem],
        compiler_params=PARAMS,
        cost_estimate=cost(4 * heads * count * count * width, 4 * heads * count * width),
        name="attend",
    )(core.reshape(1), queries, own, other)


def out_weight_kernel(codes, scales, out):
    for tile in range(codes.shape[0] // TILE_SIDE):
        span = slice(tile * TILE_SIDE, (tile + 1) * TILE_SIDE)
        scale = scales[pl.ds(pl.program_id(0) * (codes.shape[0] // TILE_SIDE) + tile, 1), :]
        out[span, :] = (codes[span, :].astype(F32) * scale).astype(BF)


def prepare_out(wo_codes, scales, step_rows):
    rows, columns = wo_codes.shape
    return pl.pallas_call(
        out_weight_kernel,
        grid=(rows // step_rows,),
        in_specs=[
            pl.BlockSpec((step_rows, columns), lambda i: (i, 0)),
            pl.BlockSpec(scales.shape, lambda i: (0, 0)),
        ],
        out_specs=pl.BlockSpec((step_rows, columns), lambda i: (i, 0)),
        out_shape=jax.ShapeDtypeStruct(wo_codes.shape, BF),
        compiler_params=PARAMS,
        cost_estimate=cost(4 * rows * columns, 4 * rows * columns),
        name="prepare_out",
    )(wo_codes, scales)


def out_kernel(attended, weight, out, total):
    step = pl.program_id(0)

    @pl.when(step == 0)
    def _():
        total[...] = jnp.zeros_like(total)

    total[...] += jnp.dot(attended[0], weight[...], preferred_element_type=F32)

    @pl.when(step == pl.num_programs(0) - 1)
    def _():
        out[...] = total[...].astype(BF)


def out_project(attended, weight):
    ranks, count, width = attended.shape
    columns = weight.shape[1]
    return pl.pallas_call(
        out_kernel,
        grid=(ranks,),
        in_specs=[
            pl.BlockSpec((1, count, width), lambda i: (i, 0, 0)),
            pl.BlockSpec((width, columns), lambda i: (i, 0)),
        ],
        out_specs=pl.BlockSpec((count, columns), lambda i: (0, 0)),
        out_shape=jax.ShapeDtypeStruct((count, columns), BF),
        scratch_shapes=[pltpu.VMEM((count, columns), F32)],
        compiler_params=PARAMS,
        cost_estimate=cost(2 * ranks * count * width * columns, 2 * ranks * width * (count + columns)),
        name="out_project",
    )(attended, weight)


def rotation_tables(count):
    half_width = HEAD_SIZE // 2
    positions = (jnp.arange(count) % LEN).astype(F32)
    frequency = theta_base ** (-jnp.arange(half_width, dtype=F32) * 2.0 / HEAD_SIZE)
    angles = positions[:, None] * frequency[None, :]
    cosine, sine = jnp.cos(angles), jnp.sin(angles)
    return jnp.concatenate([cosine, cosine], axis=1), jnp.concatenate([-sine, sine], axis=1)


Z_COUNT = 4
TOKEN_PARTS = 2


def chip_plan(
    token_ids,
    key_value_of_block,
    vocab_table,
    in_gain,
    q_gain,
    k_gain,
    wq_codes,
    wq_scale,
    key_value_codes,
    key_value_scale,
    wo_codes,
    wo_scale,
):
    ranks = lax.axis_size("fsdp")
    chips = ranks // 2
    y_count = chips // Z_COUNT
    my_rank = lax.axis_index("fsdp").astype(jnp.int32)
    core = my_rank % 2
    my_y = my_rank // 2 % y_count
    count = token_ids.shape[0]
    vocab_rows = vocab_table.shape[0]
    same_core = [[2 * chip + side for chip in range(chips)] for side in range(2)]
    z_lines = [[2 * y_count * z + rest for z in range(Z_COUNT)] for rest in range(2 * y_count)]

    def swap(values, bit):
        return lax.ppermute(values, "fsdp", [(i, i ^ bit) for i in range(ranks)])

    owners, rows, most = find_slots(token_ids, my_rank, ranks, vocab_rows)
    most = jnp.maximum(most, lax.ppermute(most, "groups", [(0, 1), (1, 0)]))[0, 0]

    def exchange(base):
        sent = pick_rows(rows, base, in_gain, vocab_table, chips)
        own = lax.all_to_all(
            sent, "fsdp", split_axis=0, concat_axis=0, tiled=True, axis_index_groups=same_core
        )
        return place_rows(owners, base, core, own, swap(own, 1), chips)

    normed = exchange(jnp.int32(0))
    _, normed = lax.while_loop(
        lambda state: state[0].astype(F32) < most,
        lambda state: (state[0] + SLOTS, state[1] + exchange(state[0])),
        (jnp.int32(SLOTS), normed),
    )

    own_weight, sent_weight, sent_keys = prepare_weights(
        core, my_rank, key_value_of_block, wq_codes, wq_scale, key_value_codes, key_value_scale, chips
    )
    other_weight = swap(sent_weight, 1)
    own_keys = lax.all_to_all(
        sent_keys, "fsdp", split_axis=0, concat_axis=0, tiled=True, axis_index_groups=same_core
    )
    other_keys = swap(own_keys, 1)
    first = core == 0
    synced = jnp.stack(
        [jnp.where(first, own_keys, other_keys), jnp.where(first, other_keys, own_keys)], axis=1
    )

    away = project(core, 1 - my_y, normed, own_weight, other_weight, BF, Z_COUNT)
    step = count // TOKEN_PARTS
    got = [swap(away[:, part * step : (part + 1) * step], 2) for part in range(TOKEN_PARTS)]
    home = project(core, my_y, normed, own_weight, other_weight, F32, Z_COUNT)
    parts = [
        lax.all_to_all(
            join_partials(home, got[part], part * step),
            "fsdp",
            split_axis=0,
            concat_axis=0,
            tiled=True,
            axis_index_groups=z_lines,
        )
        for part in range(TOKEN_PARTS)
    ]
    parts = jnp.concatenate(parts, axis=1)
    cosine, sine = rotation_tables(count)
    queries, own_kv = make_heads(core, parts, q_gain, k_gain, cosine, sine)
    attended = attend_heads(core, queries, own_kv, swap(own_kv, 1))

    columns_here = wo_codes.shape[1]
    per_column = jnp.repeat(wo_scale, TILE_SIDE, axis=1)
    out_scales = lax.dynamic_slice_in_dim(per_column, my_rank * columns_here, columns_here, 1)
    out_weight = prepare_out(wo_codes, out_scales, attended.shape[1])
    columns = out_project(lax.all_gather(attended, "fsdp"), out_weight)
    attn_out = lax.all_to_all(columns, "fsdp", split_axis=0, concat_axis=1, tiled=True)
    return attn_out, synced.reshape(1, -1, HEAD_SIZE)


def solution(mesh):
    sizes = dict(mesh.shape)
    small = sizes["fsdp"] == 2 * KEY_VALUE_HEADS and sizes["groups"] == 2
    return jax.shard_map(
        chip_plan if small else general_plan,
        mesh=mesh,
        in_specs=(
            P("groups"),
            P(),
            P("fsdp", None),
            P(),
            P(),
            P(),
            P("fsdp", None),
            P(),
            P("fsdp", None),
            P(),
            P(None, "fsdp"),
            P(),
        ),
        out_specs=(P(("groups", "fsdp"), None), P(("groups", "fsdp"), None, None)),
        check_vma=False,
    )
```

```python
import functools
import jax
import jax.numpy as jnp
from jax import lax
from jax.experimental import pallas as pl
from jax.experimental.pallas import tpu as pltpu
from jax.sharding import PartitionSpec as P
QUERY_HEADS = 64
KEY_VALUE_HEADS = 8
HEAD_SIZE = 128
TILE_SIDE = 128
LEN = 384


theta_base = 1000000.0
eps_norm = 1e-06


def rms_scale(values, norm_gain):
    mean_square = jnp.mean(values * values, axis=-1, keepdims=True)
    return values * lax.rsqrt(mean_square + eps_norm) * norm_gain


def rotate(values, positions):
    half_width = values.shape[-1] // 2
    frequency = theta_base ** (-jnp.arange(half_width, dtype=jnp.float32) * 2.0 / values.shape[-1])
    angles = positions[:, None] * frequency[None, :]
    cosine = jnp.cos(angles)[:, None, :]
    sine_part = jnp.sin(angles)[:, None, :]
    lower_half = values[..., :half_width]
    upper_half = values[..., half_width:]
    return jnp.concatenate(
        [
            lower_half * cosine - upper_half * sine_part,
            upper_half * cosine + lower_half * sine_part,
        ],
        axis=-1,
    )


def lookup_small(small_table, indices):
    matches = indices[..., None] == jnp.arange(small_table.shape[0], dtype=jnp.int32)
    return jnp.sum(jnp.where(matches, small_table, 0), axis=-1)


def column_scales(tile_scale, first_col, width_cols):
    per_column = jnp.repeat(tile_scale, TILE_SIDE, axis=1)
    picked = lax.dynamic_slice_in_dim(per_column, first_col, width_cols, 1)
    return jnp.repeat(picked, TILE_SIDE, axis=0)


def dequantize(quantized, scales):
    return (quantized.astype(jnp.float32) * scales).astype(jnp.bfloat16)


def attend(queries, key_rows, value_rows, prompt_count):
    token_count, head_count, head_width = queries.shape
    length = token_count // prompt_count
    query_blocks = queries.reshape(prompt_count, length, head_count, head_width)
    key_blocks = key_rows.reshape(prompt_count, length, head_width)
    value_blocks = value_rows.reshape(prompt_count, length, -1)
    scores = jnp.einsum(
        "plhd,pmd->phlm", query_blocks, key_blocks, preferred_element_type=jnp.float32
    ) * head_width ** (-0.5)
    causal = jnp.arange(length)[:, None] >= jnp.arange(length)[None, :]
    weights = jnp.where(causal, jnp.exp(scores), 0.0)
    probabilities = (weights / jnp.sum(weights, axis=-1, keepdims=True)).astype(jnp.bfloat16)
    attended_rows = jnp.einsum(
        "phlm,pmd->plhd", probabilities, value_blocks, preferred_element_type=jnp.float32
    )
    return attended_rows.astype(jnp.bfloat16).reshape(
        token_count, head_count * value_blocks.shape[-1]
    )


def general_plan(
    token_ids,
    key_value_of_block,
    vocab_table,
    in_gain,
    q_gain,
    k_gain,
    wq_codes,
    wq_scale,
    key_value_codes,
    key_value_scale,
    wo_codes,
    wo_scale,
):
    count_of_ranks = lax.axis_size("fsdp")
    my_rank = lax.axis_index("fsdp")
    duplicate_count = count_of_ranks // KEY_VALUE_HEADS
    per_key_value = QUERY_HEADS // KEY_VALUE_HEADS
    split_points = max(1, duplicate_count // per_key_value)
    heads_here = max(1, per_key_value // duplicate_count)
    value_columns = HEAD_SIZE // split_points
    query_width = heads_here * HEAD_SIZE
    local_rows = wq_codes.shape[0]
    token_count = token_ids.shape[0]
    targets = jnp.arange(count_of_ranks, dtype=jnp.int32)
    target_head = lookup_small(key_value_of_block, targets // duplicate_count)
    target_slot = targets % duplicate_count
    target_part = target_slot % split_points
    target_query = target_head * per_key_value + target_slot // split_points * heads_here
    my_head = lookup_small(key_value_of_block, my_rank // duplicate_count)
    my_slot = my_rank % duplicate_count
    my_part = my_slot % split_points
    my_query = my_head * per_key_value + my_slot // split_points * heads_here
    vocab_rows = vocab_table.shape[0]
    local_ids = token_ids - my_rank * vocab_rows
    inside = (local_ids >= 0) & (local_ids < vocab_rows)
    picked = jnp.take(vocab_table, jnp.clip(local_ids, 0, vocab_rows - 1), axis=0)
    terms = jnp.where(inside[:, None], picked, jnp.zeros_like(picked)).astype(jnp.float32)
    embedded = lax.psum(terms, "fsdp").astype(jnp.bfloat16)
    normed = rms_scale(embedded.astype(jnp.float32), in_gain).astype(jnp.bfloat16)
    query_groups = wq_codes.reshape(local_rows, QUERY_HEADS // heads_here, query_width)
    query_send = jnp.take(query_groups, target_query // heads_here, axis=1)
    key_value_heads = key_value_codes.reshape(local_rows, KEY_VALUE_HEADS, 2, HEAD_SIZE)
    key_send = jnp.take(key_value_heads[:, :, 0, :], target_head, axis=1)
    grouped_values = key_value_heads[:, :, 1, :].reshape(
        local_rows, KEY_VALUE_HEADS * split_points, value_columns
    )
    value_send = jnp.take(grouped_values, target_head * split_points + target_part, axis=1)
    both_send = jnp.concatenate([key_send, value_send], axis=2)
    query_got, kv_got = (
        lax.all_to_all(query_send, "fsdp", split_axis=1, concat_axis=0, tiled=True),
        lax.all_to_all(both_send, "fsdp", split_axis=1, concat_axis=0, tiled=True),
    )
    key_quant = kv_got[:, 0, :HEAD_SIZE]
    value_quant = kv_got[:, 0, HEAD_SIZE:]
    query_weight = dequantize(
        query_got[:, 0, :], column_scales(wq_scale, my_query * HEAD_SIZE, query_width)
    )
    key_matrix = dequantize(
        key_quant, column_scales(key_value_scale, my_head * 2 * HEAD_SIZE, HEAD_SIZE)
    )
    value_weight = dequantize(
        value_quant,
        column_scales(
            key_value_scale,
            my_head * 2 * HEAD_SIZE + HEAD_SIZE + my_part * value_columns,
            value_columns,
        ),
    )
    joined_weight = jnp.concatenate([query_weight, key_matrix, value_weight], axis=1)
    projected = jnp.dot(normed, joined_weight, preferred_element_type=jnp.float32)
    positions = (jnp.arange(token_count) % LEN).astype(jnp.float32)
    queries = rotate(
        rms_scale(projected[:, :query_width].reshape(token_count, heads_here, HEAD_SIZE), q_gain),
        positions,
    ).astype(jnp.bfloat16)
    keys_raw = projected[:, query_width : query_width + HEAD_SIZE].reshape(
        token_count, 1, HEAD_SIZE
    )
    key_rows = rotate(rms_scale(keys_raw, k_gain), positions).astype(jnp.bfloat16)[:, 0, :]
    value_rows = projected[:, query_width + HEAD_SIZE :].astype(jnp.bfloat16)
    attended_rows = attend(queries, key_rows, value_rows, token_count // LEN)
    cols_here = wo_codes.shape[1]
    local_weight = dequantize(wo_codes, column_scales(wo_scale, my_rank * cols_here, cols_here))
    ordered = jnp.take(
        local_weight.reshape(KEY_VALUE_HEADS, per_key_value * HEAD_SIZE, cols_here),
        key_value_of_block,
        axis=0,
    ).reshape(QUERY_HEADS * HEAD_SIZE, cols_here)
    columns = jnp.dot(
        lax.all_gather(attended_rows, "fsdp", axis=1, tiled=True),
        ordered,
        preferred_element_type=jnp.float32,
    )
    attn_out = lax.all_to_all(
        columns.astype(jnp.bfloat16), "fsdp", split_axis=0, concat_axis=1, tiled=True
    )
    return (attn_out, key_matrix.reshape(1, key_matrix.shape[0], HEAD_SIZE))


BF = jnp.bfloat16
F32 = jnp.float32
SLOTS = 32
GROUP_ROWS = 64
PARAMS = pltpu.CompilerParams(vmem_limit_bytes=48 << 20)
SMEM = pl.BlockSpec(memory_space=pltpu.SMEM)


COST_SHARE = 1


def cost(flops, bytes_accessed):
    return pl.CostEstimate(
        flops=flops // COST_SHARE, bytes_accessed=bytes_accessed // COST_SHARE, transcendentals=0
    )


def owner_of(ids, vocab_rows, ranks):
    owner = jnp.zeros_like(ids)
    for rank in range(1, ranks):
        owner = owner + jnp.where(ids >= float(rank * vocab_rows), 1.0, 0.0)
    return owner


def iota(shape, axis):
    return lax.broadcasted_iota(jnp.int32, shape, axis).astype(F32)


def slot_kernel(ranks, vocab_rows, info, id_row, col_out, row_out, most_out):
    count = id_row.shape[1]
    ids_r = id_row[...].astype(F32)
    ids_c = jnp.transpose(jnp.broadcast_to(ids_r, (128, count)))[:, 0:1]
    at_r, at_c = iota((count, count), 0), iota((count, count), 1)
    same = ids_c == ids_r
    first_c = jnp.min(jnp.where(same, at_c, float(count)), axis=1, keepdims=True)
    first_r = jnp.min(jnp.where(same, at_r, float(count)), axis=0, keepdims=True)
    is_first_r = first_r == iota((1, count), 1)
    is_first_c = first_c == iota((count, 1), 0)
    owner_c, owner_r = owner_of(ids_c, vocab_rows, ranks), owner_of(ids_r, vocab_rows, ranks)
    peers = owner_c == owner_r
    slot_c = jnp.sum(
        jnp.where(peers & is_first_r & (at_c < first_c), 1.0, 0.0), axis=1, keepdims=True
    )
    slot_r = jnp.sum(
        jnp.where(peers & is_first_c & (at_r < first_r), 1.0, 0.0), axis=0, keepdims=True
    )
    lane = lax.broadcasted_iota(jnp.int32, (count, 128), 1)
    col_out[...] = jnp.where(lane == 0, owner_c, jnp.where(lane == 1, slot_c, 0.0))
    me = info[0].astype(F32)
    mine = is_first_r & (owner_r == me)
    row_out[...] = jnp.zeros_like(row_out)
    row_out[0:1, :] = jnp.where(mine, slot_r, -1.0)
    row_out[1:2, :] = ids_r - me * float(vocab_rows)
    most_out[...] = jnp.broadcast_to(jnp.max(slot_r, axis=1, keepdims=True) + 1.0, (8, 128))


def find_slots(token_ids, my_rank, ranks, vocab_rows):
    count = token_ids.shape[0]
    return pl.pallas_call(
        functools.partial(slot_kernel, ranks, vocab_rows),
        out_shape=(
            jax.ShapeDtypeStruct((count, 128), F32),
            jax.ShapeDtypeStruct((8, count), F32),
            jax.ShapeDtypeStruct((8, 128), F32),
        ),
        in_specs=[SMEM, pl.BlockSpec(memory_space=pltpu.VMEM)],
        compiler_params=PARAMS,
        cost_estimate=cost(1000000, 1000000),
        name="find_slots",
    )(my_rank.reshape(1), token_ids.reshape(1, count))


def pick_kernel(width, info, rows, gain, table, *refs):
    out, picked, total = refs
    step = pl.program_id(0)
    slots = picked.shape[0]
    vocab_rows = table.shape[0]
    wanted = lax.broadcasted_iota(jnp.int32, (slots, 1), 0).astype(F32) + info[0].astype(F32)
    chosen = wanted == rows[0:1, :]
    index = jnp.sum(jnp.where(chosen, rows[1:2, :], 0.0), axis=1, keepdims=True)
    valid = jnp.sum(jnp.where(chosen, 1.0, 0.0), axis=1, keepdims=True)
    hot = (iota((slots, vocab_rows), 1) == index) & (valid > 0.5)
    block = jnp.dot(hot.astype(F32).astype(BF), table[...], preferred_element_type=F32)
    picked[:, pl.ds(pl.multiple_of(step * width, width), width)] = block

    @pl.when(step == 0)
    def _():
        total[...] = jnp.zeros_like(total)

    total[...] += jnp.sum(block * block, axis=1, keepdims=True)

    @pl.when(step == pl.num_programs(0) - 1)
    def _():
        features = picked.shape[1]
        chips, _, chip_width = out.shape
        inverse = lax.rsqrt(total[:, 0:1] * (1.0 / features) + eps_norm)
        for chip in range(chips):
            span = slice(chip * chip_width, (chip + 1) * chip_width)
            out[chip] = (picked[:, span] * inverse * gain[:, span]).astype(BF)


def pick_rows(rows, base, in_gain, vocab_table, chips):
    vocab_rows, features = vocab_table.shape
    steps = 4
    width, chip_width = features // steps, features // chips
    return pl.pallas_call(
        functools.partial(pick_kernel, width),
        grid=(steps,),
        out_shape=jax.ShapeDtypeStruct((chips, SLOTS, chip_width), BF),
        in_specs=[
            SMEM,
            pl.BlockSpec(rows.shape, lambda i: (0, 0)),
            pl.BlockSpec((1, features), lambda i: (0, 0)),
            pl.BlockSpec((vocab_rows, width), lambda i: (0, i)),
        ],
        out_specs=pl.BlockSpec((chips, SLOTS, chip_width), lambda i: (0, 0, 0)),
        scratch_shapes=[pltpu.VMEM((SLOTS, features), F32), pltpu.VMEM((SLOTS, 128), F32)],
        compiler_params=PARAMS,
        cost_estimate=cost(2 * SLOTS * vocab_rows * features, 2 * vocab_rows * features),
        name="pick_rows",
    )(base.reshape(1), rows, in_gain.reshape(1, features), vocab_table)


def place_kernel(chips, info, owners, own, other, out):
    count = owners.shape[0]
    core, base = info[0], info[1].astype(F32)
    owner, slot = owners[:, 0:1].astype(jnp.int32), owners[:, 1:2] - base
    fits = (slot >= 0.0) & (slot < float(SLOTS))
    position = (owner >> 1) * SLOTS + slot.astype(jnp.int32)
    hit = (lax.broadcasted_iota(jnp.int32, (count, chips * SLOTS), 1) == position) & fits
    total = jnp.zeros(out.shape, F32)
    for side, received in enumerate((own, other)):
        hot = jnp.where(hit & ((owner & 1) == (core ^ side)), 1.0, 0.0).astype(BF)
        total = total + jnp.dot(hot, received[...], preferred_element_type=F32)
    out[...] = total.astype(BF)


def place_rows(owners, base, core, own, other):
    count = owners.shape[0]
    chips, _, width = own.shape
    vmem = pl.BlockSpec(memory_space=pltpu.VMEM)
    return pl.pallas_call(
        functools.partial(place_kernel, chips),
        out_shape=jax.ShapeDtypeStruct((count, width), BF),
        in_specs=[SMEM, vmem, vmem, vmem],
        compiler_params=PARAMS,
        cost_estimate=cost(4 * count * chips * SLOTS * width, 6 * chips * SLOTS * width),
        name="place_rows",
    )(
        jnp.stack([core, base]),
        owners,
        own.reshape(chips * SLOTS, width),
        other.reshape(chips * SLOTS, width),
    )


def weight_kernel(
    info, order, head_of, wq_scale, kv_scale, wq, kv, kv_key, own, first, second, key_out
):
    step = pl.program_id(0)
    block, key_head = order[step], head_of[step]
    core, rank = info[0], info[1]
    rows = wq.shape[0]
    half = wq.shape[1] // 2
    tiles = half // TILE_SIDE

    def fill(target, side):
        for group in range(rows // GROUP_ROWS):
            tile_row = (rank * (rows // GROUP_ROWS) + group) // 2
            span = slice(group * GROUP_ROWS, (group + 1) * GROUP_ROWS)
            for tile in range(tiles):
                scale = wq_scale[tile_row, (2 * block + side) * tiles + tile]
                start = pl.multiple_of(side * half + tile * TILE_SIDE, TILE_SIDE)
                codes = wq[span, pl.ds(start, TILE_SIDE)].astype(F32)
                target[0, span, tile * TILE_SIDE : (tile + 1) * TILE_SIDE] = (codes * scale).astype(BF)
            scale = kv_scale[tile_row, 2 * block + side]
            start = pl.multiple_of(side * TILE_SIDE, TILE_SIDE)
            codes = kv[span, pl.ds(start, TILE_SIDE)].astype(F32)
            target[0, span, half : half + TILE_SIDE] = (codes * scale).astype(BF)

    fill(own, core)

    @pl.when(step < pl.num_programs(0) // 2)
    def _():
        fill(first, 1 - core)

    @pl.when(step >= pl.num_programs(0) // 2)
    def _():
        fill(second, 1 - core)

    for group in range(rows // GROUP_ROWS):
        tile_row = (rank * (rows // GROUP_ROWS) + group) // 2
        span = slice(group * GROUP_ROWS, (group + 1) * GROUP_ROWS)
        scale = kv_scale[tile_row, 2 * key_head]
        key_out[0, span, :] = (kv_key[span, :].astype(F32) * scale).astype(BF)


def prepare_weights(core, my_rank, order, key_value_of_block, wq_codes, wq_scale, kv_codes, kv_scale):
    chips = order.shape[0]
    rows = wq_codes.shape[0]
    half = wq_codes.shape[1] // (2 * chips)
    middle = chips // 2
    block = (1, rows, half + TILE_SIDE)
    return pl.pallas_call(
        weight_kernel,
        grid_spec=pltpu.PrefetchScalarGridSpec(
            num_scalar_prefetch=5,
            grid=(chips,),
            in_specs=[
                pl.BlockSpec((rows, 2 * half), lambda i, info, order, *_: (0, order[i])),
                pl.BlockSpec((rows, 2 * TILE_SIDE), lambda i, info, order, *_: (0, order[i])),
                pl.BlockSpec(
                    (rows, TILE_SIDE), lambda i, info, order, head_of, *_: (0, 2 * head_of[i])
                ),
            ],
            out_specs=[
                pl.BlockSpec(block, lambda i, *_: (i, 0, 0)),
                pl.BlockSpec(block, lambda i, *_: (jnp.minimum(i, middle - 1), 0, 0)),
                pl.BlockSpec(block, lambda i, *_: (jnp.maximum(i - middle, 0), 0, 0)),
                pl.BlockSpec((1, rows, TILE_SIDE), lambda i, *_: (i, 0, 0)),
            ],
        ),
        out_shape=[
            jax.ShapeDtypeStruct((chips, *block[1:]), BF),
            jax.ShapeDtypeStruct((middle, *block[1:]), BF),
            jax.ShapeDtypeStruct((middle, *block[1:]), BF),
            jax.ShapeDtypeStruct((chips, rows, TILE_SIDE), BF),
        ],
        compiler_params=PARAMS,
        cost_estimate=cost(rows * wq_codes.shape[1] * 8, rows * wq_codes.shape[1] * 6),
        name="prepare_weights",
    )(
        jnp.stack([core, my_rank]),
        order,
        key_value_of_block,
        wq_scale,
        kv_scale,
        wq_codes,
        kv_codes,
        kv_codes,
    )


def project_kernel(info, normed, own, other, *refs):
    *outs, weight = refs
    rows = own.shape[1]
    core = info[0]
    weight[pl.ds(pl.multiple_of(core * rows, GROUP_ROWS), rows), :] = own[0]
    weight[pl.ds(pl.multiple_of((1 - core) * rows, GROUP_ROWS), rows), :] = other[0]
    product = jnp.dot(normed[...], weight[...], preferred_element_type=F32)
    start = 0
    for out in outs:
        out[0] = product[start : start + out.shape[1]].astype(out.dtype)
        start += out.shape[1]


def project(core, normed, own, first, other, out_type):
    count, width = normed.shape
    blocks, rows, columns = other.shape
    return pl.pallas_call(
        project_kernel,
        grid=(blocks,),
        in_specs=[
            SMEM,
            pl.BlockSpec((count, width), lambda k: (0, 0)),
            pl.BlockSpec((1, rows, columns), lambda k: (first + k, 0, 0)),
            pl.BlockSpec((1, rows, columns), lambda k: (k, 0, 0)),
        ],
        out_specs=[pl.BlockSpec((1, part, columns), lambda k: (k, 0, 0)) for part in PART_ROWS],
        scratch_shapes=[pltpu.VMEM((width, columns), BF)],
        out_shape=[jax.ShapeDtypeStruct((blocks, part, columns), out_type) for part in PART_ROWS],
        compiler_params=PARAMS,
        cost_estimate=cost(
            2 * blocks * count * width * columns, 2 * blocks * columns * (width + count)
        ),
        name="project",
    )(core.reshape(1), normed, own, other)


def join_kernel(own, got, kept, *sent):
    kept[...] = own[0] + got[0].astype(F32)
    for block, out in enumerate(sent):
        out[...] = (own[block + 1] + got[block + 1].astype(F32)).astype(BF)


def join_partials(own, got):
    blocks, rows, columns = got.shape
    vmem = pl.BlockSpec(memory_space=pltpu.VMEM)
    return pl.pallas_call(
        join_kernel,
        in_specs=[vmem, vmem],
        out_shape=[jax.ShapeDtypeStruct((rows, columns), F32)]
        + [jax.ShapeDtypeStruct((rows, columns), BF)] * (blocks - 1),
        compiler_params=PARAMS,
        cost_estimate=cost(2 * blocks * rows * columns, 8 * blocks * rows * columns),
        name="join_partials",
    )(own, got)


def turn(values, cosine, sine):
    return values * cosine + pltpu.roll(values, HEAD_SIZE // 2, 1) * sine


def normalise(values, gain):
    mean_square = jnp.mean(values * values, axis=-1, keepdims=True)
    return values * lax.rsqrt(mean_square + eps_norm) * gain


def heads_kernel(start, info, *refs):
    *parts, q_gain, k_gain, cosine, sine, q_out, kv_out = refs
    total = parts[0][...]
    for part in parts[1:]:
        total = total + part[...].astype(F32)
    heads, count, _ = q_out.shape
    cos, sin = cosine[start : start + count, :], sine[start : start + count, :]
    last = total[:, heads * HEAD_SIZE :]

    @pl.when(info[0] == 0)
    def _():
        kv_out[...] = turn(normalise(last, k_gain[...]), cos, sin).astype(BF)

    @pl.when(info[0] == 1)
    def _():
        kv_out[...] = last.astype(BF)

    for head in range(heads):
        values = total[:, head * HEAD_SIZE : (head + 1) * HEAD_SIZE]
        q_out[head] = turn(normalise(values, q_gain[...]), cos, sin).astype(BF)


def make_heads(core, parts, start, q_gain, k_gain, cosine, sine):
    count, columns = parts[0].shape
    heads = columns // HEAD_SIZE - 1
    vmem = pl.BlockSpec(memory_space=pltpu.VMEM)
    return pl.pallas_call(
        functools.partial(heads_kernel, start),
        out_shape=(
            jax.ShapeDtypeStruct((heads, count, HEAD_SIZE), BF),
            jax.ShapeDtypeStruct((count, HEAD_SIZE), BF),
        ),
        in_specs=[SMEM] + [vmem] * (len(parts) + 4),
        compiler_params=PARAMS,
        cost_estimate=cost(20 * count * columns, 14 * count * columns),
        name="make_heads",
    )(core.reshape(1), *parts, q_gain.reshape(1, -1), k_gain.reshape(1, -1), cosine, sine)


def attend_kernel(length, start, share, info, queries, *refs):
    *rows, kept, sent = refs
    parts = len(rows) // 2
    own = jnp.concatenate([ref[...] for ref in rows[:parts]], axis=0)
    other = jnp.concatenate([ref[...] for ref in rows[parts:]], axis=0)
    first = info[0] == 0
    keys, values = jnp.where(first, own, other), jnp.where(first, other, own)
    count = queries.shape[1]
    here = lax.broadcasted_iota(jnp.int32, (count, keys.shape[0]), 0) + start
    there = lax.broadcasted_iota(jnp.int32, (count, keys.shape[0]), 1)
    allowed = here >= there
    for prompt in range(1, (start + count + length - 1) // length):
        allowed = allowed & ((here < prompt * length) | (there >= prompt * length))
    for head in range(queries.shape[0]):
        scores = lax.dot_general(
            queries[head], keys, (((1,), (1,)), ((), ())), preferred_element_type=F32
        ) * HEAD_SIZE ** (-0.5)
        weights = jnp.where(allowed, jnp.exp(scores), 0.0)
        probabilities = (weights / jnp.sum(weights, axis=-1, keepdims=True)).astype(BF)
        result = jnp.dot(probabilities, values, preferred_element_type=F32)
        shares = [result[at : at + share] for at in range(0, count, share)]
        even = jnp.concatenate(shares[0::2], axis=0)
        odd = jnp.concatenate(shares[1::2], axis=0)
        span = slice(head * HEAD_SIZE, (head + 1) * HEAD_SIZE)
        kept[:, span] = jnp.where(first, even, odd).astype(BF)
        sent[:, span] = jnp.where(first, odd, even).astype(BF)


def attend_heads(core, queries, start, own, other, share):
    heads, count, width = queries.shape
    vmem = pl.BlockSpec(memory_space=pltpu.VMEM)
    return pl.pallas_call(
        functools.partial(attend_kernel, LEN, start, share),
        out_shape=[jax.ShapeDtypeStruct((count // 2, heads * width), BF)] * 2,
        in_specs=[SMEM] + [vmem] * (1 + len(own) + len(other)),
        compiler_params=PARAMS,
        cost_estimate=cost(4 * heads * count * (start + count) * width, 4 * heads * count * width),
        name="attend",
    )(core.reshape(1), queries, *own, *other)


def out_weight_kernel(info, scales, codes, out):
    step, rank = pl.program_id(0), info[0]
    blocks, rows, width = out.shape
    tiles = width // TILE_SIDE
    for group in range(rows // GROUP_ROWS):
        span = slice(group * GROUP_ROWS, (group + 1) * GROUP_ROWS)
        column = (rank * rows + group * GROUP_ROWS) // TILE_SIDE
        for tile in range(blocks * tiles):
            codes_here = codes[span, tile * TILE_SIDE : (tile + 1) * TILE_SIDE].astype(F32)
            lanes = slice(tile % tiles * TILE_SIDE, (tile % tiles + 1) * TILE_SIDE)
            scale = scales[step * blocks * tiles + tile, column]
            out[tile // tiles, span, lanes] = (codes_here * scale).astype(BF)


def prepare_out(rank, wo_rows, wo_scale, width):
    columns, rows = wo_rows.shape
    blocks = 4
    return pl.pallas_call(
        out_weight_kernel,
        grid_spec=pltpu.PrefetchScalarGridSpec(
            num_scalar_prefetch=2,
            grid=(rows // width // blocks,),
            in_specs=[pl.BlockSpec((columns, blocks * width), lambda i, *_: (0, i))],
            out_specs=pl.BlockSpec((blocks, columns, width), lambda i, *_: (i, 0, 0)),
        ),
        out_shape=jax.ShapeDtypeStruct((rows // width, columns, width), BF),
        compiler_params=PARAMS,
        cost_estimate=cost(4 * rows * columns, 4 * rows * columns),
        name="prepare_out",
    )(rank.reshape(1), wo_scale, wo_rows)


def out_kernel(blocks, has_start, last, info, *refs):
    attended = refs[:blocks]
    weights = refs[blocks : blocks + 2]
    out, held, arrived = refs[-3:]
    core = info[0]
    columns, width = held.shape[2:]
    halves = [(block, half) for block in range(blocks) for half in range(2)]
    copies = []
    for number, (block, half) in enumerate(halves):
        rank = 2 * info[1 + block] + (core ^ half)
        for side in range(2):
            copy = pltpu.make_async_copy(
                weights[side].at[rank], held.at[number, side], arrived.at[number, side]
            )
            copy.start()
            copies.append(copy)
    totals = [None, None]
    for number, (block, half) in enumerate(halves):
        rows = attended[block][:, half * width : (half + 1) * width]
        for side in range(2):
            copies[2 * number + side].wait()
            term = lax.dot_general(
                held[number, side], rows, (((1,), (1,)), ((), ())), preferred_element_type=F32
            )
            totals[side] = term if totals[side] is None else totals[side] + term
    if has_start:
        start = refs[blocks + 2]
        totals = [total + start[side] for side, total in enumerate(totals)]
    if last:
        first = core == 0
        both = jnp.concatenate(
            [jnp.where(first, totals[0], totals[1]), jnp.where(first, totals[1], totals[0])], axis=0
        )
        out[...] = both.T.astype(out.dtype)
    else:
        for side in range(2):
            out[side] = totals[side]


def out_project(core, attended, chips_of, weights, start, last):
    count, both = attended[0].shape
    blocks = len(attended)
    _, columns, width = weights[0].shape
    vmem = pl.BlockSpec(memory_space=pltpu.VMEM)
    extra = [] if start is None else [start]
    shape = (count, 2 * columns) if last else (2, columns, count)
    return pl.pallas_call(
        functools.partial(out_kernel, blocks, bool(extra), last),
        out_shape=jax.ShapeDtypeStruct(shape, BF if last else F32),
        in_specs=[SMEM]
        + [vmem] * blocks
        + [pl.BlockSpec(memory_space=pl.ANY)] * 2
        + [vmem] * len(extra),
        scratch_shapes=[
            pltpu.VMEM((2 * blocks, 2, columns, width), BF),
            pltpu.SemaphoreType.DMA((2 * blocks, 2)),
        ],
        compiler_params=PARAMS,
        cost_estimate=cost(4 * blocks * count * both * columns, 4 * blocks * both * columns),
        name="out_project",
    )(jnp.concatenate([core.reshape(1), chips_of]), *attended, *weights, *extra)


def rotation_tables(count):
    half_width = HEAD_SIZE // 2
    positions = (jnp.arange(count) % LEN).astype(F32)
    frequency = theta_base ** (-jnp.arange(half_width, dtype=F32) * 2.0 / HEAD_SIZE)
    angles = positions[:, None] * frequency[None, :]
    cosine, sine = jnp.cos(angles), jnp.sin(angles)
    return jnp.concatenate([cosine, cosine], axis=1), jnp.concatenate([-sine, sine], axis=1)


Z_COUNT = 4
PART_ROWS = (192, 192)
SPLIT_GATHER = False


def after(values, *earlier):
    return lax.optimization_barrier((values, *earlier))[0]


def chip_plan(
    token_ids,
    key_value_of_block,
    vocab_table,
    in_gain,
    q_gain,
    k_gain,
    wq_codes,
    wq_scale,
    key_value_codes,
    key_value_scale,
    wo_codes,
    wo_scale,
):
    ranks = lax.axis_size("fsdp")
    chips = ranks // 2
    y_count = chips // Z_COUNT
    my_rank = lax.axis_index("fsdp").astype(jnp.int32)
    core, chip = my_rank % 2, my_rank // 2
    count = token_ids.shape[0]
    vocab_rows = vocab_table.shape[0]
    same_core = [[2 * chip + side for chip in range(chips)] for side in range(2)]

    def swap(values, bits):
        return lax.ppermute(values, "fsdp", [(i, i ^ bits) for i in range(ranks)])

    def swap_groups(values):
        return lax.ppermute(values, "groups", [(0, 1), (1, 0)])

    def to_chips(values):
        return lax.all_to_all(
            values, "fsdp", split_axis=0, concat_axis=0, tiled=True, axis_index_groups=same_core
        )

    def exchange(sent):
        own = to_chips(sent)
        return own, swap(own, 1)

    owners, rows, most = find_slots(token_ids, my_rank, ranks, vocab_rows)
    sent = pick_rows(rows, jnp.int32(0), in_gain, vocab_table, chips)
    most = jnp.maximum(most, swap_groups(after(most, sent)))[0, 0]
    own, other = exchange(sent)
    normed = place_rows(owners, jnp.int32(0), core, own, other)

    def one_more(state):
        base, total = state
        more = exchange(pick_rows(rows, base, in_gain, vocab_table, chips))
        return base + SLOTS, total + place_rows(owners, base, core, *more)

    _, normed = lax.while_loop(
        lambda state: state[0].astype(F32) < most, one_more, (jnp.int32(SLOTS), normed)
    )

    near = jnp.arange(Z_COUNT, dtype=jnp.int32) * y_count
    order = after(chip, sent) ^ jnp.concatenate([near ^ 1, near])
    own_weight, away_weight, home_weight, sent_keys = prepare_weights(
        core, my_rank, order, key_value_of_block, wq_codes, wq_scale, key_value_codes, key_value_scale
    )
    away_weight = swap(after(away_weight, own), 1)
    home_weight = swap(after(home_weight, own), 1)

    half = sent_keys.shape[1] // 2
    group = lax.axis_index("groups")
    my_half = lax.dynamic_slice_in_dim(sent_keys, group * half, half, 1)
    my_z = chip // y_count

    def keys_for(z):
        return lax.dynamic_slice_in_dim(my_half, z * y_count, y_count, 0)

    by_z = [keys_for(my_z)] + [swap(keys_for(my_z ^ k), 2 * y_count * k) for k in range(1, Z_COUNT)]

    away = project(core, normed, own_weight, 0, away_weight, BF)
    got = [swap(part, 2) for part in away]
    home = project(after(core, *away), normed, own_weight, Z_COUNT, home_weight, F32)
    got[0], *by_z = lax.optimization_barrier((got[0], *by_z))

    cosine, sine = rotation_tables(count)
    heads_width = wq_codes.shape[1] // ranks
    own_kv, other_kv, held = [], [], []
    start, share = 0, count // ranks
    for part, part_rows in enumerate(PART_ROWS):
        kept, *sums = join_partials(home[part], got[part])
        sums = [swap(value, 4 * (k + 1)) for k, value in enumerate(sums)]
        queries, kv = make_heads(core, [kept, *sums], start, q_gain, k_gain, cosine, sine)
        own_kv.append(kv)
        other_kv.append(swap(kv, 1))
        kept, sent_rows = attend_heads(core, queries, start, own_kv, other_kv, share)
        held.append(jnp.concatenate([kept, swap(sent_rows, 1)], axis=1))
        start += part_rows
    wo_rows = wo_codes.T
    out_weights = [
        prepare_out(rank, codes, wo_scale, heads_width)
        for rank, codes in ((my_rank, wo_rows), (my_rank ^ 1, swap(wo_rows, 1)))
    ]

    by_z = jnp.stack(by_z)
    my_y = chip % y_count
    here = lax.dynamic_index_in_dim(by_z, my_y, 1, keepdims=False)
    there = swap(lax.dynamic_index_in_dim(by_z, 1 - my_y, 1, keepdims=False), 2)
    own_keys = jnp.stack([here, there], axis=1).reshape(chips, half, HEAD_SIZE)
    far_keys = swap_groups(own_keys)
    own_keys = (own_keys, far_keys)
    synced = collect_keys(
        jnp.stack([core, group, chip]), [*own_keys, *(swap(value, 1) for value in own_keys)]
    )

    if not SPLIT_GATHER:
        held = [jnp.concatenate(held, axis=0)]
    columns = []
    for block in held:
        blocks = gather_chips(block, chips, y_count)
        total = None
        for chosen in ((0, 1, 2, 3), (4, 6), (5, 7)):
            total = out_project(
                core,
                [blocks[bits] for bits in chosen],
                chip ^ jnp.array(chosen, jnp.int32),
                out_weights,
                total,
                chosen == (5, 7),
            )
        columns.append(total)
    columns = to_chips(jnp.concatenate(columns, axis=0).reshape(chips, share, -1))
    attn_out = jnp.transpose(columns, (1, 0, 2)).reshape(share, -1)
    return attn_out, synced


def collect_kernel(info, own, far, other, other_far, out):
    core, group = info[0], info[1]
    out[0, core, group] = own[0]
    out[0, core, 1 - group] = far[0]
    out[0, 1 - core, group] = other[0]
    out[0, 1 - core, 1 - group] = other_far[0]


def collect_keys(info, parts):
    chips, half, width = parts[0].shape
    part = pl.BlockSpec((1, half, width), lambda i, info: (i ^ info[2], 0, 0))
    out = pl.pallas_call(
        collect_kernel,
        grid_spec=pltpu.PrefetchScalarGridSpec(
            num_scalar_prefetch=1,
            grid=(chips,),
            in_specs=[part] * 4,
            out_specs=pl.BlockSpec((1, 2, 2, half, width), lambda i, info: (i, 0, 0, 0, 0)),
        ),
        out_shape=jax.ShapeDtypeStruct((chips, 2, 2, half, width), BF),
        compiler_params=PARAMS,
        cost_estimate=cost(0, 16 * chips * half * width),
        name="collect_keys",
    )(info, *parts)
    return out.reshape(1, -1, width)


def gather_chips(block, chips, y_count):
    ranks = 2 * chips
    along = 2 * y_count

    def swap(values, bits):
        return lax.ppermute(values, "fsdp", [(i, i ^ bits) for i in range(ranks)])

    def hop(values, pairs):
        return lax.ppermute(
            values,
            "fsdp",
            [(a * along + rest, b * along + rest) for a, b in pairs for rest in range(along)],
        )

    middle, outward = [(1, 2), (2, 1)], [(1, 0), (2, 3)]
    z_index = lax.axis_index("fsdp") // along
    at_end = (z_index == 0) | (z_index == Z_COUNT - 1)
    across = swap(block, 2)
    one = swap(block, along)
    inner = hop(block, middle)
    two_end = hop(inner, outward)
    two_inner = hop(one, middle)
    one_across = swap(one, 2)
    two = jnp.where(at_end, two_end, two_inner)
    three_end = hop(two, outward)
    two_across = swap(two, 2)
    three = jnp.where(at_end, three_end, inner)
    three_across = swap(three, 2)
    return {
        0: block,
        1: across,
        2: one,
        3: one_across,
        4: two,
        5: two_across,
        6: three,
        7: three_across,
    }


def solution(mesh):
    sizes = dict(mesh.shape)
    small = sizes["fsdp"] == 2 * KEY_VALUE_HEADS and sizes["groups"] == 2
    return jax.shard_map(
        chip_plan if small else general_plan,
        mesh=mesh,
        in_specs=(
            P("groups"),
            P(),
            P("fsdp", None),
            P(),
            P(),
            P(),
            P("fsdp", None),
            P(),
            P("fsdp", None),
            P(),
            P(None, "fsdp"),
            P(),
        ),
        out_specs=(P(("groups", "fsdp"), None), P(("groups", "fsdp"), None, None)),
        check_vma=False,
    )
```

```python
import functools
import jax
import jax.numpy as jnp
from jax import lax
from jax.experimental import pallas as pl
from jax.experimental.pallas import tpu as pltpu
from jax.sharding import PartitionSpec as P
QUERY_HEADS = 64
KEY_VALUE_HEADS = 8
HEAD_SIZE = 128
TILE_SIDE = 128
LEN = 384


theta_base = 1000000.0
eps_norm = 1e-06


def rms_scale(values, norm_gain):
    mean_square = jnp.mean(values * values, axis=-1, keepdims=True)
    return values * lax.rsqrt(mean_square + eps_norm) * norm_gain


def rotate(values, positions):
    half_width = values.shape[-1] // 2
    frequency = theta_base ** (-jnp.arange(half_width, dtype=jnp.float32) * 2.0 / values.shape[-1])
    angles = positions[:, None] * frequency[None, :]
    cosine = jnp.cos(angles)[:, None, :]
    sine_part = jnp.sin(angles)[:, None, :]
    lower_half = values[..., :half_width]
    upper_half = values[..., half_width:]
    return jnp.concatenate(
        [
            lower_half * cosine - upper_half * sine_part,
            upper_half * cosine + lower_half * sine_part,
        ],
        axis=-1,
    )


def lookup_small(small_table, indices):
    matches = indices[..., None] == jnp.arange(small_table.shape[0], dtype=jnp.int32)
    return jnp.sum(jnp.where(matches, small_table, 0), axis=-1)


def column_scales(tile_scale, first_col, width_cols):
    per_column = jnp.repeat(tile_scale, TILE_SIDE, axis=1)
    picked = lax.dynamic_slice_in_dim(per_column, first_col, width_cols, 1)
    return jnp.repeat(picked, TILE_SIDE, axis=0)


def dequantize(quantized, scales):
    return (quantized.astype(jnp.float32) * scales).astype(jnp.bfloat16)


def attend(queries, key_rows, value_rows, prompt_count):
    token_count, head_count, head_width = queries.shape
    length = token_count // prompt_count
    query_blocks = queries.reshape(prompt_count, length, head_count, head_width)
    key_blocks = key_rows.reshape(prompt_count, length, head_width)
    value_blocks = value_rows.reshape(prompt_count, length, -1)
    scores = jnp.einsum(
        "plhd,pmd->phlm", query_blocks, key_blocks, preferred_element_type=jnp.float32
    ) * head_width ** (-0.5)
    causal = jnp.arange(length)[:, None] >= jnp.arange(length)[None, :]
    weights = jnp.where(causal, jnp.exp(scores), 0.0)
    probabilities = (weights / jnp.sum(weights, axis=-1, keepdims=True)).astype(jnp.bfloat16)
    attended_rows = jnp.einsum(
        "phlm,pmd->plhd", probabilities, value_blocks, preferred_element_type=jnp.float32
    )
    return attended_rows.astype(jnp.bfloat16).reshape(
        token_count, head_count * value_blocks.shape[-1]
    )


def general_plan(
    token_ids,
    key_value_of_block,
    vocab_table,
    in_gain,
    q_gain,
    k_gain,
    wq_codes,
    wq_scale,
    key_value_codes,
    key_value_scale,
    wo_codes,
    wo_scale,
):
    count_of_ranks = lax.axis_size("fsdp")
    my_rank = lax.axis_index("fsdp")
    duplicate_count = count_of_ranks // KEY_VALUE_HEADS
    per_key_value = QUERY_HEADS // KEY_VALUE_HEADS
    split_points = max(1, duplicate_count // per_key_value)
    heads_here = max(1, per_key_value // duplicate_count)
    value_columns = HEAD_SIZE // split_points
    query_width = heads_here * HEAD_SIZE
    local_rows = wq_codes.shape[0]
    token_count = token_ids.shape[0]
    targets = jnp.arange(count_of_ranks, dtype=jnp.int32)
    target_head = lookup_small(key_value_of_block, targets // duplicate_count)
    target_slot = targets % duplicate_count
    target_part = target_slot % split_points
    target_query = target_head * per_key_value + target_slot // split_points * heads_here
    my_head = lookup_small(key_value_of_block, my_rank // duplicate_count)
    my_slot = my_rank % duplicate_count
    my_part = my_slot % split_points
    my_query = my_head * per_key_value + my_slot // split_points * heads_here
    vocab_rows = vocab_table.shape[0]
    local_ids = token_ids - my_rank * vocab_rows
    inside = (local_ids >= 0) & (local_ids < vocab_rows)
    picked = jnp.take(vocab_table, jnp.clip(local_ids, 0, vocab_rows - 1), axis=0)
    terms = jnp.where(inside[:, None], picked, jnp.zeros_like(picked)).astype(jnp.float32)
    embedded = lax.psum(terms, "fsdp").astype(jnp.bfloat16)
    normed = rms_scale(embedded.astype(jnp.float32), in_gain).astype(jnp.bfloat16)
    query_groups = wq_codes.reshape(local_rows, QUERY_HEADS // heads_here, query_width)
    query_send = jnp.take(query_groups, target_query // heads_here, axis=1)
    key_value_heads = key_value_codes.reshape(local_rows, KEY_VALUE_HEADS, 2, HEAD_SIZE)
    key_send = jnp.take(key_value_heads[:, :, 0, :], target_head, axis=1)
    grouped_values = key_value_heads[:, :, 1, :].reshape(
        local_rows, KEY_VALUE_HEADS * split_points, value_columns
    )
    value_send = jnp.take(grouped_values, target_head * split_points + target_part, axis=1)
    both_send = jnp.concatenate([key_send, value_send], axis=2)
    query_got, kv_got = (
        lax.all_to_all(query_send, "fsdp", split_axis=1, concat_axis=0, tiled=True),
        lax.all_to_all(both_send, "fsdp", split_axis=1, concat_axis=0, tiled=True),
    )
    key_quant = kv_got[:, 0, :HEAD_SIZE]
    value_quant = kv_got[:, 0, HEAD_SIZE:]
    query_weight = dequantize(
        query_got[:, 0, :], column_scales(wq_scale, my_query * HEAD_SIZE, query_width)
    )
    key_matrix = dequantize(
        key_quant, column_scales(key_value_scale, my_head * 2 * HEAD_SIZE, HEAD_SIZE)
    )
    value_weight = dequantize(
        value_quant,
        column_scales(
            key_value_scale,
            my_head * 2 * HEAD_SIZE + HEAD_SIZE + my_part * value_columns,
            value_columns,
        ),
    )
    joined_weight = jnp.concatenate([query_weight, key_matrix, value_weight], axis=1)
    projected = jnp.dot(normed, joined_weight, preferred_element_type=jnp.float32)
    positions = (jnp.arange(token_count) % LEN).astype(jnp.float32)
    queries = rotate(
        rms_scale(projected[:, :query_width].reshape(token_count, heads_here, HEAD_SIZE), q_gain),
        positions,
    ).astype(jnp.bfloat16)
    keys_raw = projected[:, query_width : query_width + HEAD_SIZE].reshape(
        token_count, 1, HEAD_SIZE
    )
    key_rows = rotate(rms_scale(keys_raw, k_gain), positions).astype(jnp.bfloat16)[:, 0, :]
    value_rows = projected[:, query_width + HEAD_SIZE :].astype(jnp.bfloat16)
    attended_rows = attend(queries, key_rows, value_rows, token_count // LEN)
    cols_here = wo_codes.shape[1]
    local_weight = dequantize(wo_codes, column_scales(wo_scale, my_rank * cols_here, cols_here))
    ordered = jnp.take(
        local_weight.reshape(KEY_VALUE_HEADS, per_key_value * HEAD_SIZE, cols_here),
        key_value_of_block,
        axis=0,
    ).reshape(QUERY_HEADS * HEAD_SIZE, cols_here)
    columns = jnp.dot(
        lax.all_gather(attended_rows, "fsdp", axis=1, tiled=True),
        ordered,
        preferred_element_type=jnp.float32,
    )
    attn_out = lax.all_to_all(
        columns.astype(jnp.bfloat16), "fsdp", split_axis=0, concat_axis=1, tiled=True
    )
    return (attn_out, key_matrix.reshape(1, key_matrix.shape[0], HEAD_SIZE))


BF = jnp.bfloat16
F32 = jnp.float32
SLOTS = 32
GROUP_ROWS = 64
PARAMS = pltpu.CompilerParams(vmem_limit_bytes=48 << 20)
SMEM = pl.BlockSpec(memory_space=pltpu.SMEM)


COST_SHARE = 1


def cost(flops, bytes_accessed):
    return pl.CostEstimate(
        flops=flops // COST_SHARE, bytes_accessed=bytes_accessed // COST_SHARE, transcendentals=0
    )


def owner_of(ids, vocab_rows, ranks):
    owner = jnp.zeros_like(ids)
    for rank in range(1, ranks):
        owner = owner + jnp.where(ids >= float(rank * vocab_rows), 1.0, 0.0)
    return owner


def iota(shape, axis):
    return lax.broadcasted_iota(jnp.int32, shape, axis).astype(F32)


def slot_kernel(ranks, vocab_rows, info, id_row, col_out, row_out, most_out):
    count = id_row.shape[1]
    ids_r = id_row[...].astype(F32)
    ids_c = jnp.transpose(jnp.broadcast_to(ids_r, (128, count)))[:, 0:1]
    at_r, at_c = iota((count, count), 0), iota((count, count), 1)
    same = ids_c == ids_r
    first_c = jnp.min(jnp.where(same, at_c, float(count)), axis=1, keepdims=True)
    first_r = jnp.min(jnp.where(same, at_r, float(count)), axis=0, keepdims=True)
    is_first_r = first_r == iota((1, count), 1)
    is_first_c = first_c == iota((count, 1), 0)
    owner_c, owner_r = owner_of(ids_c, vocab_rows, ranks), owner_of(ids_r, vocab_rows, ranks)
    peers = owner_c == owner_r
    slot_c = jnp.sum(
        jnp.where(peers & is_first_r & (at_c < first_c), 1.0, 0.0), axis=1, keepdims=True
    )
    slot_r = jnp.sum(
        jnp.where(peers & is_first_c & (at_r < first_r), 1.0, 0.0), axis=0, keepdims=True
    )
    lane = lax.broadcasted_iota(jnp.int32, (count, 128), 1)
    col_out[...] = jnp.where(lane == 0, owner_c, jnp.where(lane == 1, slot_c, 0.0))
    me = info[0].astype(F32)
    mine = is_first_r & (owner_r == me)
    row_out[...] = jnp.zeros_like(row_out)
    row_out[0:1, :] = jnp.where(mine, slot_r, -1.0)
    row_out[1:2, :] = ids_r - me * float(vocab_rows)
    most_out[...] = jnp.broadcast_to(jnp.max(slot_r, axis=1, keepdims=True) + 1.0, (8, 128))


def find_slots(token_ids, my_rank, ranks, vocab_rows):
    count = token_ids.shape[0]
    return pl.pallas_call(
        functools.partial(slot_kernel, ranks, vocab_rows),
        out_shape=(
            jax.ShapeDtypeStruct((count, 128), F32),
            jax.ShapeDtypeStruct((8, count), F32),
            jax.ShapeDtypeStruct((8, 128), F32),
        ),
        in_specs=[SMEM, pl.BlockSpec(memory_space=pltpu.VMEM)],
        compiler_params=PARAMS,
        cost_estimate=cost(1000000, 1000000),
        name="find_slots",
    )(my_rank.reshape(1), token_ids.reshape(1, count))


def pick_kernel(width, info, rows, gain, table, *refs):
    out, picked, total = refs
    step = pl.program_id(0)
    slots = picked.shape[0]
    vocab_rows = table.shape[0]
    wanted = lax.broadcasted_iota(jnp.int32, (slots, 1), 0).astype(F32) + info[0].astype(F32)
    chosen = wanted == rows[0:1, :]
    index = jnp.sum(jnp.where(chosen, rows[1:2, :], 0.0), axis=1, keepdims=True)
    valid = jnp.sum(jnp.where(chosen, 1.0, 0.0), axis=1, keepdims=True)
    hot = (iota((slots, vocab_rows), 1) == index) & (valid > 0.5)
    block = jnp.dot(hot.astype(F32).astype(BF), table[...], preferred_element_type=F32)
    picked[:, pl.ds(pl.multiple_of(step * width, width), width)] = block

    @pl.when(step == 0)
    def _():
        total[...] = jnp.zeros_like(total)

    total[...] += jnp.sum(block * block, axis=1, keepdims=True)

    @pl.when(step == pl.num_programs(0) - 1)
    def _():
        features = picked.shape[1]
        chips, _, chip_width = out.shape
        inverse = lax.rsqrt(total[:, 0:1] * (1.0 / features) + eps_norm)
        for chip in range(chips):
            span = slice(chip * chip_width, (chip + 1) * chip_width)
            out[chip] = (picked[:, span] * inverse * gain[:, span]).astype(BF)


def pick_rows(rows, base, in_gain, vocab_table, chips):
    vocab_rows, features = vocab_table.shape
    steps = 4
    width, chip_width = features // steps, features // chips
    return pl.pallas_call(
        functools.partial(pick_kernel, width),
        grid=(steps,),
        out_shape=jax.ShapeDtypeStruct((chips, SLOTS, chip_width), BF),
        in_specs=[
            SMEM,
            pl.BlockSpec(rows.shape, lambda i: (0, 0)),
            pl.BlockSpec((1, features), lambda i: (0, 0)),
            pl.BlockSpec((vocab_rows, width), lambda i: (0, i)),
        ],
        out_specs=pl.BlockSpec((chips, SLOTS, chip_width), lambda i: (0, 0, 0)),
        scratch_shapes=[pltpu.VMEM((SLOTS, features), F32), pltpu.VMEM((SLOTS, 128), F32)],
        compiler_params=PARAMS,
        cost_estimate=cost(2 * SLOTS * vocab_rows * features, 2 * vocab_rows * features),
        name="pick_rows",
    )(base.reshape(1), rows, in_gain.reshape(1, features), vocab_table)


def place_kernel(chips, info, owners, own, other, out):
    count = owners.shape[0]
    core, base = info[0], info[1].astype(F32)
    owner, slot = owners[:, 0:1].astype(jnp.int32), owners[:, 1:2] - base
    fits = (slot >= 0.0) & (slot < float(SLOTS))
    position = (owner >> 1) * SLOTS + slot.astype(jnp.int32)
    hit = (lax.broadcasted_iota(jnp.int32, (count, chips * SLOTS), 1) == position) & fits
    total = jnp.zeros(out.shape, F32)
    for side, received in enumerate((own, other)):
        hot = jnp.where(hit & ((owner & 1) == (core ^ side)), 1.0, 0.0).astype(BF)
        total = total + jnp.dot(hot, received[...], preferred_element_type=F32)
    out[...] = total.astype(BF)


def place_rows(owners, base, core, own, other):
    count = owners.shape[0]
    chips, _, width = own.shape
    vmem = pl.BlockSpec(memory_space=pltpu.VMEM)
    return pl.pallas_call(
        functools.partial(place_kernel, chips),
        out_shape=jax.ShapeDtypeStruct((count, width), BF),
        in_specs=[SMEM, vmem, vmem, vmem],
        compiler_params=PARAMS,
        cost_estimate=cost(4 * count * chips * SLOTS * width, 6 * chips * SLOTS * width),
        name="place_rows",
    )(
        jnp.stack([core, base]),
        owners,
        own.reshape(chips * SLOTS, width),
        other.reshape(chips * SLOTS, width),
    )


def weight_kernel(
    info, order, head_of, wq_scale, kv_scale, wq, kv, kv_key, own, first, second, key_out
):
    step = pl.program_id(0)
    block, key_head = order[step], head_of[step]
    core, rank = info[0], info[1]
    rows = wq.shape[0]
    half = wq.shape[1] // 2
    tiles = half // TILE_SIDE

    def fill(target, side):
        for group in range(rows // GROUP_ROWS):
            tile_row = (rank * (rows // GROUP_ROWS) + group) // 2
            span = slice(group * GROUP_ROWS, (group + 1) * GROUP_ROWS)
            for tile in range(tiles):
                scale = wq_scale[tile_row, (2 * block + side) * tiles + tile]
                start = pl.multiple_of(side * half + tile * TILE_SIDE, TILE_SIDE)
                codes = wq[span, pl.ds(start, TILE_SIDE)].astype(F32)
                target[0, span, tile * TILE_SIDE : (tile + 1) * TILE_SIDE] = (codes * scale).astype(BF)
            scale = kv_scale[tile_row, 2 * block + side]
            start = pl.multiple_of(side * TILE_SIDE, TILE_SIDE)
            codes = kv[span, pl.ds(start, TILE_SIDE)].astype(F32)
            target[0, span, half : half + TILE_SIDE] = (codes * scale).astype(BF)

    fill(own, core)

    @pl.when(step < pl.num_programs(0) // 2)
    def _():
        fill(first, 1 - core)

    @pl.when(step >= pl.num_programs(0) // 2)
    def _():
        fill(second, 1 - core)

    for group in range(rows // GROUP_ROWS):
        tile_row = (rank * (rows // GROUP_ROWS) + group) // 2
        span = slice(group * GROUP_ROWS, (group + 1) * GROUP_ROWS)
        scale = kv_scale[tile_row, 2 * key_head]
        key_out[0, span, :] = (kv_key[span, :].astype(F32) * scale).astype(BF)


def prepare_weights(core, my_rank, order, key_value_of_block, wq_codes, wq_scale, kv_codes, kv_scale):
    chips = order.shape[0]
    rows = wq_codes.shape[0]
    half = wq_codes.shape[1] // (2 * chips)
    middle = chips // 2
    block = (1, rows, half + TILE_SIDE)
    return pl.pallas_call(
        weight_kernel,
        grid_spec=pltpu.PrefetchScalarGridSpec(
            num_scalar_prefetch=5,
            grid=(chips,),
            in_specs=[
                pl.BlockSpec((rows, 2 * half), lambda i, info, order, *_: (0, order[i])),
                pl.BlockSpec((rows, 2 * TILE_SIDE), lambda i, info, order, *_: (0, order[i])),
                pl.BlockSpec(
                    (rows, TILE_SIDE), lambda i, info, order, head_of, *_: (0, 2 * head_of[i])
                ),
            ],
            out_specs=[
                pl.BlockSpec(block, lambda i, *_: (i, 0, 0)),
                pl.BlockSpec(block, lambda i, *_: (jnp.minimum(i, middle - 1), 0, 0)),
                pl.BlockSpec(block, lambda i, *_: (jnp.maximum(i - middle, 0), 0, 0)),
                pl.BlockSpec((1, rows, TILE_SIDE), lambda i, *_: (i, 0, 0)),
            ],
        ),
        out_shape=[
            jax.ShapeDtypeStruct((chips, *block[1:]), BF),
            jax.ShapeDtypeStruct((middle, *block[1:]), BF),
            jax.ShapeDtypeStruct((middle, *block[1:]), BF),
            jax.ShapeDtypeStruct((chips, rows, TILE_SIDE), BF),
        ],
        compiler_params=PARAMS,
        cost_estimate=cost(rows * wq_codes.shape[1] * 8, rows * wq_codes.shape[1] * 6),
        name="prepare_weights",
    )(
        jnp.stack([core, my_rank]),
        order,
        key_value_of_block,
        wq_scale,
        kv_scale,
        wq_codes,
        kv_codes,
        kv_codes,
    )


def project_kernel(info, normed, own, other, *refs):
    *outs, weight = refs
    rows = own.shape[1]
    core = info[0]
    weight[pl.ds(pl.multiple_of(core * rows, GROUP_ROWS), rows), :] = own[0]
    weight[pl.ds(pl.multiple_of((1 - core) * rows, GROUP_ROWS), rows), :] = other[0]
    product = jnp.dot(normed[...], weight[...], preferred_element_type=F32)
    start = 0
    for out in outs:
        out[0] = product[start : start + out.shape[1]].astype(out.dtype)
        start += out.shape[1]


def project(core, normed, own, first, other, out_type):
    count, width = normed.shape
    blocks, rows, columns = other.shape
    return pl.pallas_call(
        project_kernel,
        grid=(blocks,),
        in_specs=[
            SMEM,
            pl.BlockSpec((count, width), lambda k: (0, 0)),
            pl.BlockSpec((1, rows, columns), lambda k: (first + k, 0, 0)),
            pl.BlockSpec((1, rows, columns), lambda k: (k, 0, 0)),
        ],
        out_specs=[pl.BlockSpec((1, part, columns), lambda k: (k, 0, 0)) for part in PART_ROWS],
        scratch_shapes=[pltpu.VMEM((width, columns), BF)],
        out_shape=[jax.ShapeDtypeStruct((blocks, part, columns), out_type) for part in PART_ROWS],
        compiler_params=PARAMS,
        cost_estimate=cost(
            2 * blocks * count * width * columns, 2 * blocks * columns * (width + count)
        ),
        name="project",
    )(core.reshape(1), normed, own, other)


def join_kernel(own, got, kept, *sent):
    kept[...] = own[0] + got[0].astype(F32)
    for block, out in enumerate(sent):
        out[...] = (own[block + 1] + got[block + 1].astype(F32)).astype(BF)


def join_partials(own, got):
    blocks, rows, columns = got.shape
    vmem = pl.BlockSpec(memory_space=pltpu.VMEM)
    return pl.pallas_call(
        join_kernel,
        in_specs=[vmem, vmem],
        out_shape=[jax.ShapeDtypeStruct((rows, columns), F32)]
        + [jax.ShapeDtypeStruct((rows, columns), BF)] * (blocks - 1),
        compiler_params=PARAMS,
        cost_estimate=cost(2 * blocks * rows * columns, 8 * blocks * rows * columns),
        name="join_partials",
    )(own, got)


def turn(values, cosine, sine):
    return values * cosine + pltpu.roll(values, HEAD_SIZE // 2, 1) * sine


def normalise(values, gain):
    mean_square = jnp.mean(values * values, axis=-1, keepdims=True)
    return values * lax.rsqrt(mean_square + eps_norm) * gain


def heads_kernel(start, info, *refs):
    *parts, q_gain, k_gain, cosine, sine, q_out, kv_out = refs
    total = parts[0][...]
    for part in parts[1:]:
        total = total + part[...].astype(F32)
    heads, count, _ = q_out.shape
    cos, sin = cosine[start : start + count, :], sine[start : start + count, :]
    last = total[:, heads * HEAD_SIZE :]

    @pl.when(info[0] == 0)
    def _():
        kv_out[...] = turn(normalise(last, k_gain[...]), cos, sin).astype(BF)

    @pl.when(info[0] == 1)
    def _():
        kv_out[...] = last.astype(BF)

    for head in range(heads):
        values = total[:, head * HEAD_SIZE : (head + 1) * HEAD_SIZE]
        q_out[head] = turn(normalise(values, q_gain[...]), cos, sin).astype(BF)


def make_heads(core, parts, start, q_gain, k_gain, cosine, sine):
    count, columns = parts[0].shape
    heads = columns // HEAD_SIZE - 1
    vmem = pl.BlockSpec(memory_space=pltpu.VMEM)
    return pl.pallas_call(
        functools.partial(heads_kernel, start),
        out_shape=(
            jax.ShapeDtypeStruct((heads, count, HEAD_SIZE), BF),
            jax.ShapeDtypeStruct((count, HEAD_SIZE), BF),
        ),
        in_specs=[SMEM] + [vmem] * (len(parts) + 4),
        compiler_params=PARAMS,
        cost_estimate=cost(20 * count * columns, 14 * count * columns),
        name="make_heads",
    )(core.reshape(1), *parts, q_gain.reshape(1, -1), k_gain.reshape(1, -1), cosine, sine)


def attend_kernel(length, start, share, info, queries, *refs):
    *rows, kept, sent = refs
    parts = len(rows) // 2
    own = jnp.concatenate([ref[...] for ref in rows[:parts]], axis=0)
    other = jnp.concatenate([ref[...] for ref in rows[parts:]], axis=0)
    first = info[0] == 0
    keys, values = jnp.where(first, own, other), jnp.where(first, other, own)
    count = queries.shape[1]
    here = lax.broadcasted_iota(jnp.int32, (count, keys.shape[0]), 0) + start
    there = lax.broadcasted_iota(jnp.int32, (count, keys.shape[0]), 1)
    allowed = here >= there
    for prompt in range(1, (start + count + length - 1) // length):
        allowed = allowed & ((here < prompt * length) | (there >= prompt * length))
    for head in range(queries.shape[0]):
        scores = lax.dot_general(
            queries[head], keys, (((1,), (1,)), ((), ())), preferred_element_type=F32
        ) * HEAD_SIZE ** (-0.5)
        weights = jnp.where(allowed, jnp.exp(scores), 0.0)
        probabilities = (weights / jnp.sum(weights, axis=-1, keepdims=True)).astype(BF)
        result = jnp.dot(probabilities, values, preferred_element_type=F32)
        shares = [result[at : at + share] for at in range(0, count, share)]
        even = jnp.concatenate(shares[0::2], axis=0)
        odd = jnp.concatenate(shares[1::2], axis=0)
        span = slice(head * HEAD_SIZE, (head + 1) * HEAD_SIZE)
        kept[:, span] = jnp.where(first, even, odd).astype(BF)
        sent[:, span] = jnp.where(first, odd, even).astype(BF)


def attend_heads(core, queries, start, own, other, share):
    heads, count, width = queries.shape
    vmem = pl.BlockSpec(memory_space=pltpu.VMEM)
    return pl.pallas_call(
        functools.partial(attend_kernel, LEN, start, share),
        out_shape=[jax.ShapeDtypeStruct((count // 2, heads * width), BF)] * 2,
        in_specs=[SMEM] + [vmem] * (1 + len(own) + len(other)),
        compiler_params=PARAMS,
        cost_estimate=cost(4 * heads * count * (start + count) * width, 4 * heads * count * width),
        name="attend",
    )(core.reshape(1), queries, *own, *other)


def out_kernel(blocks, has_start, last, width, info, scales, *refs):
    attended = refs[:blocks]
    codes = refs[blocks : blocks + 2]
    out, held, arrived = refs[-3:]
    core, my_rank = info[0], info[1]
    columns = held.shape[1]
    tiles = width // TILE_SIDE
    pieces = [(block, half, side) for block in range(blocks) for half in range(2) for side in range(2)]
    copies = []
    for number, (block, half, side) in enumerate(pieces):
        start = (2 * info[2 + block] + (core ^ half)) * width
        copy = pltpu.make_async_copy(
            codes[side].at[:, pl.ds(pl.multiple_of(start, width), width)],
            held.at[number],
            arrived.at[number],
        )
        copy.start()
        copies.append(copy)
    totals = [None, None]
    for number, (block, half, side) in enumerate(pieces):
        rows = attended[block][:, half * width : (half + 1) * width]
        first_tile = (2 * info[2 + block] + (core ^ half)) * tiles
        copies[number].wait()
        weight = []
        for group in range(columns // GROUP_ROWS):
            column = ((my_rank ^ side) * columns + group * GROUP_ROWS) // TILE_SIDE
            span = slice(group * GROUP_ROWS, (group + 1) * GROUP_ROWS)
            weight.append(
                jnp.concatenate(
                    [
                        (
                            held[number, span, tile * TILE_SIDE : (tile + 1) * TILE_SIDE].astype(F32)
                            * scales[first_tile + tile, column]
                        ).astype(BF)
                        for tile in range(tiles)
                    ],
                    axis=1,
                )
            )
        term = lax.dot_general(
            jnp.concatenate(weight, axis=0),
            rows,
            (((1,), (1,)), ((), ())),
            preferred_element_type=F32,
        )
        totals[side] = term if totals[side] is None else totals[side] + term
    if has_start:
        start = refs[blocks + 2]
        totals = [total + start[side] for side, total in enumerate(totals)]
    if last:
        first = core == 0
        both = jnp.concatenate(
            [jnp.where(first, totals[0], totals[1]), jnp.where(first, totals[1], totals[0])], axis=0
        )
        out[...] = both.T.astype(out.dtype)
    else:
        for side in range(2):
            out[side] = totals[side]


def out_project(core, my_rank, attended, chips_of, codes, scales, start, last):
    count, both = attended[0].shape
    blocks = len(attended)
    columns = codes[0].shape[0]
    vmem = pl.BlockSpec(memory_space=pltpu.VMEM)
    extra = [] if start is None else [start]
    shape = (count, 2 * columns) if last else (2, columns, count)
    return pl.pallas_call(
        functools.partial(out_kernel, blocks, bool(extra), last, both // 2),
        out_shape=jax.ShapeDtypeStruct(shape, BF if last else F32),
        in_specs=[SMEM, SMEM]
        + [vmem] * blocks
        + [pl.BlockSpec(memory_space=pl.ANY)] * 2
        + [vmem] * len(extra),
        scratch_shapes=[
            pltpu.VMEM((4 * blocks, columns, both // 2), BF),
            pltpu.SemaphoreType.DMA((4 * blocks,)),
        ],
        compiler_params=PARAMS,
        cost_estimate=cost(4 * blocks * count * both * columns, 4 * blocks * both * columns),
        name="out_project",
    )(jnp.concatenate([jnp.stack([core, my_rank]), chips_of]), scales, *attended, *codes, *extra)


def rotation_tables(count):
    half_width = HEAD_SIZE // 2
    positions = (jnp.arange(count) % LEN).astype(F32)
    frequency = theta_base ** (-jnp.arange(half_width, dtype=F32) * 2.0 / HEAD_SIZE)
    angles = positions[:, None] * frequency[None, :]
    cosine, sine = jnp.cos(angles), jnp.sin(angles)
    return jnp.concatenate([cosine, cosine], axis=1), jnp.concatenate([-sine, sine], axis=1)


Z_COUNT = 4
PART_ROWS = (192, 192)
SPLIT_GATHER = False
TIE_SUMS = True
CALLS = ((0, 1, 2), (3, 4, 5, 6), (7,))


def after(values, *earlier):
    return lax.optimization_barrier((values, *earlier))[0]


def chip_plan(
    token_ids,
    key_value_of_block,
    vocab_table,
    in_gain,
    q_gain,
    k_gain,
    wq_codes,
    wq_scale,
    key_value_codes,
    key_value_scale,
    wo_codes,
    wo_scale,
):
    ranks = lax.axis_size("fsdp")
    chips = ranks // 2
    y_count = chips // Z_COUNT
    my_rank = lax.axis_index("fsdp").astype(jnp.int32)
    core, chip = my_rank % 2, my_rank // 2
    count = token_ids.shape[0]
    vocab_rows = vocab_table.shape[0]
    same_core = [[2 * chip + side for chip in range(chips)] for side in range(2)]

    def swap(values, bits):
        return lax.ppermute(values, "fsdp", [(i, i ^ bits) for i in range(ranks)])

    def swap_groups(values):
        return lax.ppermute(values, "groups", [(0, 1), (1, 0)])

    def to_chips(values):
        return lax.all_to_all(
            values, "fsdp", split_axis=0, concat_axis=0, tiled=True, axis_index_groups=same_core
        )

    def exchange(sent):
        own = to_chips(sent)
        return own, swap(own, 1)

    owners, rows, most = find_slots(token_ids, my_rank, ranks, vocab_rows)
    sent = pick_rows(rows, jnp.int32(0), in_gain, vocab_table, chips)
    most = jnp.maximum(most, swap_groups(after(most, sent)))[0, 0]
    own, other = exchange(sent)
    normed = place_rows(owners, jnp.int32(0), core, own, other)

    def one_more(state):
        base, total = state
        more = exchange(pick_rows(rows, base, in_gain, vocab_table, chips))
        return base + SLOTS, total + place_rows(owners, base, core, *more)

    _, normed = lax.while_loop(
        lambda state: state[0].astype(F32) < most, one_more, (jnp.int32(SLOTS), normed)
    )

    near = jnp.arange(Z_COUNT, dtype=jnp.int32) * y_count
    order = after(chip, sent) ^ jnp.concatenate([near ^ 1, near])
    own_weight, away_weight, home_weight, sent_keys = prepare_weights(
        core, my_rank, order, key_value_of_block, wq_codes, wq_scale, key_value_codes, key_value_scale
    )
    away_weight = swap(after(away_weight, own), 1)
    home_weight = swap(after(home_weight, own), 1)

    half = sent_keys.shape[1] // 2
    group = lax.axis_index("groups")
    my_half = lax.dynamic_slice_in_dim(sent_keys, group * half, half, 1)
    my_z = chip // y_count

    def keys_for(z):
        return lax.dynamic_slice_in_dim(my_half, z * y_count, y_count, 0)

    by_z = [keys_for(my_z)] + [swap(keys_for(my_z ^ k), 2 * y_count * k) for k in range(1, Z_COUNT)]

    away = project(core, normed, own_weight, 0, away_weight, BF)
    got = [swap(part, 2) for part in away]
    home = project(after(core, *away), normed, own_weight, Z_COUNT, home_weight, F32)
    got[0], *by_z = lax.optimization_barrier((got[0], *by_z))

    cosine, sine = rotation_tables(count)
    heads_width = wq_codes.shape[1] // ranks
    own_kv, other_kv, held = [], [], []
    start, share = 0, count // ranks
    for part, part_rows in enumerate(PART_ROWS):
        kept, *sums = join_partials(home[part], got[part])
        sums = [swap(value, 4 * (k + 1)) for k, value in enumerate(sums)]
        if TIE_SUMS and part + 1 < len(PART_ROWS):
            got[part + 1], *sums = lax.optimization_barrier((got[part + 1], *sums))
        queries, kv = make_heads(core, [kept, *sums], start, q_gain, k_gain, cosine, sine)
        own_kv.append(kv)
        other_kv.append(swap(kv, 1))
        kept, sent_rows = attend_heads(core, queries, start, own_kv, other_kv, share)
        held.append(jnp.concatenate([kept, swap(sent_rows, 1)], axis=1))
        start += part_rows
    wo_rows = wo_codes.T
    out_codes = [wo_rows, swap(wo_rows, 1)]

    by_z = jnp.stack(by_z)
    my_y = chip % y_count
    here = lax.dynamic_index_in_dim(by_z, my_y, 1, keepdims=False)
    there = swap(lax.dynamic_index_in_dim(by_z, 1 - my_y, 1, keepdims=False), 2)
    own_keys = jnp.stack([here, there], axis=1).reshape(chips, half, HEAD_SIZE)
    far_keys = swap_groups(own_keys)
    own_keys = (own_keys, far_keys)
    synced = collect_keys(
        jnp.stack([core, group, chip]), [*own_keys, *(swap(value, 1) for value in own_keys)]
    )

    if not SPLIT_GATHER:
        held = [jnp.concatenate(held, axis=0)]
    columns = []
    for block in held:
        blocks = gather_chips(block, chips, y_count)
        total = None
        for chosen in CALLS:
            total = out_project(
                core,
                my_rank,
                [blocks[bits] for bits in chosen],
                chip ^ jnp.array(chosen, jnp.int32),
                out_codes,
                wo_scale,
                total,
                chosen == CALLS[-1],
            )
        columns.append(total)
    columns = to_chips(jnp.concatenate(columns, axis=0).reshape(chips, share, -1))
    attn_out = jnp.transpose(columns, (1, 0, 2)).reshape(share, -1)
    return attn_out, synced


def collect_kernel(info, own, far, other, other_far, out):
    core, group = info[0], info[1]
    out[0, core, group] = own[0]
    out[0, core, 1 - group] = far[0]
    out[0, 1 - core, group] = other[0]
    out[0, 1 - core, 1 - group] = other_far[0]


def collect_keys(info, parts):
    chips, half, width = parts[0].shape
    part = pl.BlockSpec((1, half, width), lambda i, info: (i ^ info[2], 0, 0))
    out = pl.pallas_call(
        collect_kernel,
        grid_spec=pltpu.PrefetchScalarGridSpec(
            num_scalar_prefetch=1,
            grid=(chips,),
            in_specs=[part] * 4,
            out_specs=pl.BlockSpec((1, 2, 2, half, width), lambda i, info: (i, 0, 0, 0, 0)),
        ),
        out_shape=jax.ShapeDtypeStruct((chips, 2, 2, half, width), BF),
        compiler_params=PARAMS,
        cost_estimate=cost(0, 16 * chips * half * width),
        name="collect_keys",
    )(info, *parts)
    return out.reshape(1, -1, width)


def gather_chips(block, chips, y_count):
    ranks = 2 * chips
    along = 2 * y_count

    def swap(values, bits):
        return lax.ppermute(values, "fsdp", [(i, i ^ bits) for i in range(ranks)])

    def hop(values, pairs):
        return lax.ppermute(
            values,
            "fsdp",
            [(a * along + rest, b * along + rest) for a, b in pairs for rest in range(along)],
        )

    middle, outward = [(1, 2), (2, 1)], [(1, 0), (2, 3)]
    z_index = lax.axis_index("fsdp") // along
    at_end = (z_index == 0) | (z_index == Z_COUNT - 1)
    across = swap(block, 2)
    one = swap(block, along)
    inner = hop(block, middle)
    across, one, inner = lax.optimization_barrier((across, one, inner))
    two_end = hop(inner, outward)
    two_inner = hop(one, middle)
    one_across = swap(one, 2)
    two_end, two_inner, one_across = lax.optimization_barrier((two_end, two_inner, one_across))
    two = jnp.where(at_end, two_end, two_inner)
    three_end = hop(two, outward)
    two_across = swap(two, 2)
    three_end, two_across = lax.optimization_barrier((three_end, two_across))
    three = jnp.where(at_end, three_end, inner)
    three_across = swap(three, 2)
    return {
        0: block,
        1: across,
        2: one,
        3: one_across,
        4: two,
        5: two_across,
        6: three,
        7: three_across,
    }


def solution(mesh):
    sizes = dict(mesh.shape)
    small = sizes["fsdp"] == 2 * KEY_VALUE_HEADS and sizes["groups"] == 2
    return jax.shard_map(
        chip_plan if small else general_plan,
        mesh=mesh,
        in_specs=(
            P("groups"),
            P(),
            P("fsdp", None),
            P(),
            P(),
            P(),
            P("fsdp", None),
            P(),
            P("fsdp", None),
            P(),
            P(None, "fsdp"),
            P(),
        ),
        out_specs=(P(("groups", "fsdp"), None), P(("groups", "fsdp"), None, None)),
        check_vma=False,
    )
```

```python
import functools
import jax
import jax.numpy as jnp
from jax import lax
from jax.experimental import pallas as pl
from jax.experimental.pallas import tpu as pltpu
from jax.sharding import PartitionSpec as P
QUERY_HEADS = 64
KEY_VALUE_HEADS = 8
HEAD_SIZE = 128
TILE_SIDE = 128
LEN = 384


theta_base = 1000000.0
eps_norm = 1e-06


def rms_scale(values, norm_gain):
    mean_square = jnp.mean(values * values, axis=-1, keepdims=True)
    return values * lax.rsqrt(mean_square + eps_norm) * norm_gain


def rotate(values, positions):
    half_width = values.shape[-1] // 2
    frequency = theta_base ** (-jnp.arange(half_width, dtype=jnp.float32) * 2.0 / values.shape[-1])
    angles = positions[:, None] * frequency[None, :]
    cosine = jnp.cos(angles)[:, None, :]
    sine_part = jnp.sin(angles)[:, None, :]
    lower_half = values[..., :half_width]
    upper_half = values[..., half_width:]
    return jnp.concatenate(
        [
            lower_half * cosine - upper_half * sine_part,
            upper_half * cosine + lower_half * sine_part,
        ],
        axis=-1,
    )


def lookup_small(small_table, indices):
    matches = indices[..., None] == jnp.arange(small_table.shape[0], dtype=jnp.int32)
    return jnp.sum(jnp.where(matches, small_table, 0), axis=-1)


def column_scales(tile_scale, first_col, width_cols):
    per_column = jnp.repeat(tile_scale, TILE_SIDE, axis=1)
    picked = lax.dynamic_slice_in_dim(per_column, first_col, width_cols, 1)
    return jnp.repeat(picked, TILE_SIDE, axis=0)


def dequantize(quantized, scales):
    return (quantized.astype(jnp.float32) * scales).astype(jnp.bfloat16)


def attend(queries, key_rows, value_rows, prompt_count):
    token_count, head_count, head_width = queries.shape
    length = token_count // prompt_count
    query_blocks = queries.reshape(prompt_count, length, head_count, head_width)
    key_blocks = key_rows.reshape(prompt_count, length, head_width)
    value_blocks = value_rows.reshape(prompt_count, length, -1)
    scores = jnp.einsum(
        "plhd,pmd->phlm", query_blocks, key_blocks, preferred_element_type=jnp.float32
    ) * head_width ** (-0.5)
    causal = jnp.arange(length)[:, None] >= jnp.arange(length)[None, :]
    weights = jnp.where(causal, jnp.exp(scores), 0.0)
    probabilities = (weights / jnp.sum(weights, axis=-1, keepdims=True)).astype(jnp.bfloat16)
    attended_rows = jnp.einsum(
        "phlm,pmd->plhd", probabilities, value_blocks, preferred_element_type=jnp.float32
    )
    return attended_rows.astype(jnp.bfloat16).reshape(
        token_count, head_count * value_blocks.shape[-1]
    )


def general_plan(
    token_ids,
    key_value_of_block,
    vocab_table,
    in_gain,
    q_gain,
    k_gain,
    wq_codes,
    wq_scale,
    key_value_codes,
    key_value_scale,
    wo_codes,
    wo_scale,
):
    count_of_ranks = lax.axis_size("fsdp")
    my_rank = lax.axis_index("fsdp")
    duplicate_count = count_of_ranks // KEY_VALUE_HEADS
    per_key_value = QUERY_HEADS // KEY_VALUE_HEADS
    split_points = max(1, duplicate_count // per_key_value)
    heads_here = max(1, per_key_value // duplicate_count)
    value_columns = HEAD_SIZE // split_points
    query_width = heads_here * HEAD_SIZE
    local_rows = wq_codes.shape[0]
    token_count = token_ids.shape[0]
    targets = jnp.arange(count_of_ranks, dtype=jnp.int32)
    target_head = lookup_small(key_value_of_block, targets // duplicate_count)
    target_slot = targets % duplicate_count
    target_part = target_slot % split_points
    target_query = target_head * per_key_value + target_slot // split_points * heads_here
    my_head = lookup_small(key_value_of_block, my_rank // duplicate_count)
    my_slot = my_rank % duplicate_count
    my_part = my_slot % split_points
    my_query = my_head * per_key_value + my_slot // split_points * heads_here
    vocab_rows = vocab_table.shape[0]
    local_ids = token_ids - my_rank * vocab_rows
    inside = (local_ids >= 0) & (local_ids < vocab_rows)
    picked = jnp.take(vocab_table, jnp.clip(local_ids, 0, vocab_rows - 1), axis=0)
    terms = jnp.where(inside[:, None], picked, jnp.zeros_like(picked)).astype(jnp.float32)
    embedded = lax.psum(terms, "fsdp").astype(jnp.bfloat16)
    normed = rms_scale(embedded.astype(jnp.float32), in_gain).astype(jnp.bfloat16)
    query_groups = wq_codes.reshape(local_rows, QUERY_HEADS // heads_here, query_width)
    query_send = jnp.take(query_groups, target_query // heads_here, axis=1)
    key_value_heads = key_value_codes.reshape(local_rows, KEY_VALUE_HEADS, 2, HEAD_SIZE)
    key_send = jnp.take(key_value_heads[:, :, 0, :], target_head, axis=1)
    grouped_values = key_value_heads[:, :, 1, :].reshape(
        local_rows, KEY_VALUE_HEADS * split_points, value_columns
    )
    value_send = jnp.take(grouped_values, target_head * split_points + target_part, axis=1)
    both_send = jnp.concatenate([key_send, value_send], axis=2)
    query_got, kv_got = (
        lax.all_to_all(query_send, "fsdp", split_axis=1, concat_axis=0, tiled=True),
        lax.all_to_all(both_send, "fsdp", split_axis=1, concat_axis=0, tiled=True),
    )
    key_quant = kv_got[:, 0, :HEAD_SIZE]
    value_quant = kv_got[:, 0, HEAD_SIZE:]
    query_weight = dequantize(
        query_got[:, 0, :], column_scales(wq_scale, my_query * HEAD_SIZE, query_width)
    )
    key_matrix = dequantize(
        key_quant, column_scales(key_value_scale, my_head * 2 * HEAD_SIZE, HEAD_SIZE)
    )
    value_weight = dequantize(
        value_quant,
        column_scales(
            key_value_scale,
            my_head * 2 * HEAD_SIZE + HEAD_SIZE + my_part * value_columns,
            value_columns,
        ),
    )
    joined_weight = jnp.concatenate([query_weight, key_matrix, value_weight], axis=1)
    projected = jnp.dot(normed, joined_weight, preferred_element_type=jnp.float32)
    positions = (jnp.arange(token_count) % LEN).astype(jnp.float32)
    queries = rotate(
        rms_scale(projected[:, :query_width].reshape(token_count, heads_here, HEAD_SIZE), q_gain),
        positions,
    ).astype(jnp.bfloat16)
    keys_raw = projected[:, query_width : query_width + HEAD_SIZE].reshape(
        token_count, 1, HEAD_SIZE
    )
    key_rows = rotate(rms_scale(keys_raw, k_gain), positions).astype(jnp.bfloat16)[:, 0, :]
    value_rows = projected[:, query_width + HEAD_SIZE :].astype(jnp.bfloat16)
    attended_rows = attend(queries, key_rows, value_rows, token_count // LEN)
    cols_here = wo_codes.shape[1]
    local_weight = dequantize(wo_codes, column_scales(wo_scale, my_rank * cols_here, cols_here))
    ordered = jnp.take(
        local_weight.reshape(KEY_VALUE_HEADS, per_key_value * HEAD_SIZE, cols_here),
        key_value_of_block,
        axis=0,
    ).reshape(QUERY_HEADS * HEAD_SIZE, cols_here)
    columns = jnp.dot(
        lax.all_gather(attended_rows, "fsdp", axis=1, tiled=True),
        ordered,
        preferred_element_type=jnp.float32,
    )
    attn_out = lax.all_to_all(
        columns.astype(jnp.bfloat16), "fsdp", split_axis=0, concat_axis=1, tiled=True
    )
    return (attn_out, key_matrix.reshape(1, key_matrix.shape[0], HEAD_SIZE))


BF = jnp.bfloat16
F32 = jnp.float32
SLOTS = 32
GROUP_ROWS = 64
PARAMS = pltpu.CompilerParams(vmem_limit_bytes=48 << 20)
SMEM = pl.BlockSpec(memory_space=pltpu.SMEM)


COST_SHARE = 1


def cost(flops, bytes_accessed):
    return pl.CostEstimate(
        flops=flops // COST_SHARE, bytes_accessed=bytes_accessed // COST_SHARE, transcendentals=0
    )


def owner_of(ids, vocab_rows, ranks):
    owner = jnp.zeros_like(ids)
    for rank in range(1, ranks):
        owner = owner + jnp.where(ids >= float(rank * vocab_rows), 1.0, 0.0)
    return owner


def iota(shape, axis):
    return lax.broadcasted_iota(jnp.int32, shape, axis).astype(F32)


def slot_kernel(ranks, vocab_rows, info, id_row, col_out, row_out, most_out):
    count = id_row.shape[1]
    ids_r = id_row[...].astype(F32)
    ids_c = jnp.transpose(jnp.broadcast_to(ids_r, (128, count)))[:, 0:1]
    at_r, at_c = iota((count, count), 0), iota((count, count), 1)
    same = ids_c == ids_r
    first_c = jnp.min(jnp.where(same, at_c, float(count)), axis=1, keepdims=True)
    first_r = jnp.min(jnp.where(same, at_r, float(count)), axis=0, keepdims=True)
    is_first_r = first_r == iota((1, count), 1)
    is_first_c = first_c == iota((count, 1), 0)
    owner_c, owner_r = owner_of(ids_c, vocab_rows, ranks), owner_of(ids_r, vocab_rows, ranks)
    peers = owner_c == owner_r
    slot_c = jnp.sum(
        jnp.where(peers & is_first_r & (at_c < first_c), 1.0, 0.0), axis=1, keepdims=True
    )
    slot_r = jnp.sum(
        jnp.where(peers & is_first_c & (at_r < first_r), 1.0, 0.0), axis=0, keepdims=True
    )
    lane = lax.broadcasted_iota(jnp.int32, (count, 128), 1)
    col_out[...] = jnp.where(lane == 0, owner_c, jnp.where(lane == 1, slot_c, 0.0))
    me = info[0].astype(F32)
    mine = is_first_r & (owner_r == me)
    row_out[...] = jnp.zeros_like(row_out)
    row_out[0:1, :] = jnp.where(mine, slot_r, -1.0)
    row_out[1:2, :] = ids_r - me * float(vocab_rows)
    most_out[...] = jnp.broadcast_to(jnp.max(slot_r, axis=1, keepdims=True) + 1.0, (8, 128))


def find_slots(token_ids, my_rank, ranks, vocab_rows):
    count = token_ids.shape[0]
    return pl.pallas_call(
        functools.partial(slot_kernel, ranks, vocab_rows),
        out_shape=(
            jax.ShapeDtypeStruct((count, 128), F32),
            jax.ShapeDtypeStruct((8, count), F32),
            jax.ShapeDtypeStruct((8, 128), F32),
        ),
        in_specs=[SMEM, pl.BlockSpec(memory_space=pltpu.VMEM)],
        compiler_params=PARAMS,
        cost_estimate=cost(1000000, 1000000),
        name="find_slots",
    )(my_rank.reshape(1), token_ids.reshape(1, count))


def pick_kernel(width, info, rows, gain, table, *refs):
    out, picked, total = refs
    step = pl.program_id(0)
    slots = picked.shape[0]
    vocab_rows = table.shape[0]
    wanted = lax.broadcasted_iota(jnp.int32, (slots, 1), 0).astype(F32) + info[0].astype(F32)
    chosen = wanted == rows[0:1, :]
    index = jnp.sum(jnp.where(chosen, rows[1:2, :], 0.0), axis=1, keepdims=True)
    valid = jnp.sum(jnp.where(chosen, 1.0, 0.0), axis=1, keepdims=True)
    hot = (iota((slots, vocab_rows), 1) == index) & (valid > 0.5)
    block = jnp.dot(hot.astype(F32).astype(BF), table[...], preferred_element_type=F32)
    picked[:, pl.ds(pl.multiple_of(step * width, width), width)] = block

    @pl.when(step == 0)
    def _():
        total[...] = jnp.zeros_like(total)

    total[...] += jnp.sum(block * block, axis=1, keepdims=True)

    @pl.when(step == pl.num_programs(0) - 1)
    def _():
        features = picked.shape[1]
        chips, _, chip_width = out.shape
        inverse = lax.rsqrt(total[:, 0:1] * (1.0 / features) + eps_norm)
        for chip in range(chips):
            span = slice(chip * chip_width, (chip + 1) * chip_width)
            out[chip] = (picked[:, span] * inverse * gain[:, span]).astype(BF)


def pick_rows(rows, base, in_gain, vocab_table, chips):
    vocab_rows, features = vocab_table.shape
    steps = 4
    width, chip_width = features // steps, features // chips
    return pl.pallas_call(
        functools.partial(pick_kernel, width),
        grid=(steps,),
        out_shape=jax.ShapeDtypeStruct((chips, SLOTS, chip_width), BF),
        in_specs=[
            SMEM,
            pl.BlockSpec(rows.shape, lambda i: (0, 0)),
            pl.BlockSpec((1, features), lambda i: (0, 0)),
            pl.BlockSpec((vocab_rows, width), lambda i: (0, i)),
        ],
        out_specs=pl.BlockSpec((chips, SLOTS, chip_width), lambda i: (0, 0, 0)),
        scratch_shapes=[pltpu.VMEM((SLOTS, features), F32), pltpu.VMEM((SLOTS, 128), F32)],
        compiler_params=PARAMS,
        cost_estimate=cost(2 * SLOTS * vocab_rows * features, 2 * vocab_rows * features),
        name="pick_rows",
    )(base.reshape(1), rows, in_gain.reshape(1, features), vocab_table)


def place_kernel(chips, info, owners, own, other, out):
    count = owners.shape[0]
    core, base = info[0], info[1].astype(F32)
    owner, slot = owners[:, 0:1].astype(jnp.int32), owners[:, 1:2] - base
    fits = (slot >= 0.0) & (slot < float(SLOTS))
    position = (owner >> 1) * SLOTS + slot.astype(jnp.int32)
    hit = (lax.broadcasted_iota(jnp.int32, (count, chips * SLOTS), 1) == position) & fits
    total = jnp.zeros(out.shape, F32)
    for side, received in enumerate((own, other)):
        hot = jnp.where(hit & ((owner & 1) == (core ^ side)), 1.0, 0.0).astype(BF)
        total = total + jnp.dot(hot, received[...], preferred_element_type=F32)
    out[...] = total.astype(BF)


def place_rows(owners, base, core, own, other):
    count = owners.shape[0]
    chips, _, width = own.shape
    vmem = pl.BlockSpec(memory_space=pltpu.VMEM)
    return pl.pallas_call(
        functools.partial(place_kernel, chips),
        out_shape=jax.ShapeDtypeStruct((count, width), BF),
        in_specs=[SMEM, vmem, vmem, vmem],
        compiler_params=PARAMS,
        cost_estimate=cost(4 * count * chips * SLOTS * width, 6 * chips * SLOTS * width),
        name="place_rows",
    )(
        jnp.stack([core, base]),
        owners,
        own.reshape(chips * SLOTS, width),
        other.reshape(chips * SLOTS, width),
    )


def weight_kernel(
    info, order, head_of, wq_scale, kv_scale, wq, kv, kv_key, own, first, second, key_out
):
    step = pl.program_id(0)
    block, key_head = order[step], head_of[step]
    core, rank = info[0], info[1]
    rows = wq.shape[0]
    half = wq.shape[1] // 2
    tiles = half // TILE_SIDE

    def fill(target, side):
        for group in range(rows // GROUP_ROWS):
            tile_row = (rank * (rows // GROUP_ROWS) + group) // 2
            span = slice(group * GROUP_ROWS, (group + 1) * GROUP_ROWS)
            for tile in range(tiles):
                scale = wq_scale[tile_row, (2 * block + side) * tiles + tile]
                start = pl.multiple_of(side * half + tile * TILE_SIDE, TILE_SIDE)
                codes = wq[span, pl.ds(start, TILE_SIDE)].astype(F32)
                target[0, span, tile * TILE_SIDE : (tile + 1) * TILE_SIDE] = (codes * scale).astype(BF)
            scale = kv_scale[tile_row, 2 * block + side]
            start = pl.multiple_of(side * TILE_SIDE, TILE_SIDE)
            codes = kv[span, pl.ds(start, TILE_SIDE)].astype(F32)
            target[0, span, half : half + TILE_SIDE] = (codes * scale).astype(BF)

    fill(own, core)

    @pl.when(step < pl.num_programs(0) // 2)
    def _():
        fill(first, 1 - core)

    @pl.when(step >= pl.num_programs(0) // 2)
    def _():
        fill(second, 1 - core)

    for group in range(rows // GROUP_ROWS):
        tile_row = (rank * (rows // GROUP_ROWS) + group) // 2
        span = slice(group * GROUP_ROWS, (group + 1) * GROUP_ROWS)
        scale = kv_scale[tile_row, 2 * key_head]
        key_out[0, span, :] = (kv_key[span, :].astype(F32) * scale).astype(BF)


def prepare_weights(core, my_rank, order, key_value_of_block, wq_codes, wq_scale, kv_codes, kv_scale):
    chips = order.shape[0]
    rows = wq_codes.shape[0]
    half = wq_codes.shape[1] // (2 * chips)
    middle = chips // 2
    block = (1, rows, half + TILE_SIDE)
    return pl.pallas_call(
        weight_kernel,
        grid_spec=pltpu.PrefetchScalarGridSpec(
            num_scalar_prefetch=5,
            grid=(chips,),
            in_specs=[
                pl.BlockSpec((rows, 2 * half), lambda i, info, order, *_: (0, order[i])),
                pl.BlockSpec((rows, 2 * TILE_SIDE), lambda i, info, order, *_: (0, order[i])),
                pl.BlockSpec(
                    (rows, TILE_SIDE), lambda i, info, order, head_of, *_: (0, 2 * head_of[i])
                ),
            ],
            out_specs=[
                pl.BlockSpec(block, lambda i, *_: (i, 0, 0)),
                pl.BlockSpec(block, lambda i, *_: (jnp.minimum(i, middle - 1), 0, 0)),
                pl.BlockSpec(block, lambda i, *_: (jnp.maximum(i - middle, 0), 0, 0)),
                pl.BlockSpec((1, rows, TILE_SIDE), lambda i, *_: (i, 0, 0)),
            ],
        ),
        out_shape=[
            jax.ShapeDtypeStruct((chips, *block[1:]), BF),
            jax.ShapeDtypeStruct((middle, *block[1:]), BF),
            jax.ShapeDtypeStruct((middle, *block[1:]), BF),
            jax.ShapeDtypeStruct((chips, rows, TILE_SIDE), BF),
        ],
        compiler_params=PARAMS,
        cost_estimate=cost(rows * wq_codes.shape[1] * 8, rows * wq_codes.shape[1] * 6),
        name="prepare_weights",
    )(
        jnp.stack([core, my_rank]),
        order,
        key_value_of_block,
        wq_scale,
        kv_scale,
        wq_codes,
        kv_codes,
        kv_codes,
    )


def project_kernel(info, normed, own, other, *refs):
    *outs, weight = refs
    rows = own.shape[1]
    core = info[0]
    weight[pl.ds(pl.multiple_of(core * rows, GROUP_ROWS), rows), :] = own[0]
    weight[pl.ds(pl.multiple_of((1 - core) * rows, GROUP_ROWS), rows), :] = other[0]
    product = jnp.dot(normed[...], weight[...], preferred_element_type=F32)
    start = 0
    for out in outs:
        out[0] = product[start : start + out.shape[1]].astype(out.dtype)
        start += out.shape[1]


def project(core, normed, own, first, other, out_type):
    count, width = normed.shape
    blocks, rows, columns = other.shape
    return pl.pallas_call(
        project_kernel,
        grid=(blocks,),
        in_specs=[
            SMEM,
            pl.BlockSpec((count, width), lambda k: (0, 0)),
            pl.BlockSpec((1, rows, columns), lambda k: (first + k, 0, 0)),
            pl.BlockSpec((1, rows, columns), lambda k: (k, 0, 0)),
        ],
        out_specs=[pl.BlockSpec((1, part, columns), lambda k: (k, 0, 0)) for part in PART_ROWS],
        scratch_shapes=[pltpu.VMEM((width, columns), BF)],
        out_shape=[jax.ShapeDtypeStruct((blocks, part, columns), out_type) for part in PART_ROWS],
        compiler_params=PARAMS,
        cost_estimate=cost(
            2 * blocks * count * width * columns, 2 * blocks * columns * (width + count)
        ),
        name="project",
    )(core.reshape(1), normed, own, other)


def join_kernel(own, got, kept, *sent):
    kept[...] = own[0] + got[0].astype(F32)
    for block, out in enumerate(sent):
        out[...] = (own[block + 1] + got[block + 1].astype(F32)).astype(BF)


def join_partials(own, got):
    blocks, rows, columns = got.shape
    vmem = pl.BlockSpec(memory_space=pltpu.VMEM)
    return pl.pallas_call(
        join_kernel,
        in_specs=[vmem, vmem],
        out_shape=[jax.ShapeDtypeStruct((rows, columns), F32)]
        + [jax.ShapeDtypeStruct((rows, columns), BF)] * (blocks - 1),
        compiler_params=PARAMS,
        cost_estimate=cost(2 * blocks * rows * columns, 8 * blocks * rows * columns),
        name="join_partials",
    )(own, got)


def turn(values, cosine, sine):
    return values * cosine + pltpu.roll(values, HEAD_SIZE // 2, 1) * sine


def normalise(values, gain):
    mean_square = jnp.mean(values * values, axis=-1, keepdims=True)
    return values * lax.rsqrt(mean_square + eps_norm) * gain


def heads_kernel(start, info, *refs):
    *parts, q_gain, k_gain, cosine, sine, q_out, kv_out = refs
    total = parts[0][...]
    for part in parts[1:]:
        total = total + part[...].astype(F32)
    heads, count, _ = q_out.shape
    cos, sin = cosine[start : start + count, :], sine[start : start + count, :]
    last = total[:, heads * HEAD_SIZE :]

    @pl.when(info[0] == 0)
    def _():
        kv_out[...] = turn(normalise(last, k_gain[...]), cos, sin).astype(BF)

    @pl.when(info[0] == 1)
    def _():
        kv_out[...] = last.astype(BF)

    for head in range(heads):
        values = total[:, head * HEAD_SIZE : (head + 1) * HEAD_SIZE]
        q_out[head] = turn(normalise(values, q_gain[...]), cos, sin).astype(BF)


def make_heads(core, parts, start, q_gain, k_gain, cosine, sine):
    count, columns = parts[0].shape
    heads = columns // HEAD_SIZE - 1
    vmem = pl.BlockSpec(memory_space=pltpu.VMEM)
    return pl.pallas_call(
        functools.partial(heads_kernel, start),
        out_shape=(
            jax.ShapeDtypeStruct((heads, count, HEAD_SIZE), BF),
            jax.ShapeDtypeStruct((count, HEAD_SIZE), BF),
        ),
        in_specs=[SMEM] + [vmem] * (len(parts) + 4),
        compiler_params=PARAMS,
        cost_estimate=cost(20 * count * columns, 14 * count * columns),
        name="make_heads",
    )(core.reshape(1), *parts, q_gain.reshape(1, -1), k_gain.reshape(1, -1), cosine, sine)


def attend_kernel(length, start, share, info, queries, *refs):
    *rows, kept, sent = refs
    parts = len(rows) // 2
    own = jnp.concatenate([ref[...] for ref in rows[:parts]], axis=0)
    other = jnp.concatenate([ref[...] for ref in rows[parts:]], axis=0)
    first = info[0] == 0
    keys, values = jnp.where(first, own, other), jnp.where(first, other, own)
    count = queries.shape[1]
    here = lax.broadcasted_iota(jnp.int32, (count, keys.shape[0]), 0) + start
    there = lax.broadcasted_iota(jnp.int32, (count, keys.shape[0]), 1)
    allowed = here >= there
    for prompt in range(1, (start + count + length - 1) // length):
        allowed = allowed & ((here < prompt * length) | (there >= prompt * length))
    for head in range(queries.shape[0]):
        scores = lax.dot_general(
            queries[head], keys, (((1,), (1,)), ((), ())), preferred_element_type=F32
        ) * HEAD_SIZE ** (-0.5)
        weights = jnp.where(allowed, jnp.exp(scores), 0.0)
        probabilities = (weights / jnp.sum(weights, axis=-1, keepdims=True)).astype(BF)
        result = jnp.dot(probabilities, values, preferred_element_type=F32)
        shares = [result[at : at + share] for at in range(0, count, share)]
        even = jnp.concatenate(shares[0::2], axis=0)
        odd = jnp.concatenate(shares[1::2], axis=0)
        span = slice(head * HEAD_SIZE, (head + 1) * HEAD_SIZE)
        kept[:, span] = jnp.where(first, even, odd).astype(BF)
        sent[:, span] = jnp.where(first, odd, even).astype(BF)


def attend_heads(core, queries, start, own, other, share):
    heads, count, width = queries.shape
    vmem = pl.BlockSpec(memory_space=pltpu.VMEM)
    return pl.pallas_call(
        functools.partial(attend_kernel, LEN, start, share),
        out_shape=[jax.ShapeDtypeStruct((count // 2, heads * width), BF)] * 2,
        in_specs=[SMEM] + [vmem] * (1 + len(own) + len(other)),
        compiler_params=PARAMS,
        cost_estimate=cost(4 * heads * count * (start + count) * width, 4 * heads * count * width),
        name="attend",
    )(core.reshape(1), queries, *own, *other)


def out_kernel(blocks, has_start, last, width, info, scales, *refs):
    attended = refs[:blocks]
    codes = refs[blocks : blocks + 2]
    out, held, arrived = refs[-3:]
    core, my_rank = info[0], info[1]
    columns = held.shape[1]
    tiles = width // TILE_SIDE
    pieces = [(block, half, side) for block in range(blocks) for half in range(2) for side in range(2)]
    copies = []
    for number, (block, half, side) in enumerate(pieces):
        start = (2 * info[2 + block] + (core ^ half)) * width
        copy = pltpu.make_async_copy(
            codes[side].at[:, pl.ds(pl.multiple_of(start, width), width)],
            held.at[number],
            arrived.at[number],
        )
        copy.start()
        copies.append(copy)
    totals = [None, None]
    for number, (block, half, side) in enumerate(pieces):
        rows = attended[block][:, half * width : (half + 1) * width]
        first_tile = (2 * info[2 + block] + (core ^ half)) * tiles
        copies[number].wait()
        weight = []
        for group in range(columns // GROUP_ROWS):
            column = ((my_rank ^ side) * columns + group * GROUP_ROWS) // TILE_SIDE
            span = slice(group * GROUP_ROWS, (group + 1) * GROUP_ROWS)
            weight.append(
                jnp.concatenate(
                    [
                        (
                            held[number, span, tile * TILE_SIDE : (tile + 1) * TILE_SIDE].astype(F32)
                            * scales[first_tile + tile, column]
                        ).astype(BF)
                        for tile in range(tiles)
                    ],
                    axis=1,
                )
            )
        term = lax.dot_general(
            jnp.concatenate(weight, axis=0),
            rows,
            (((1,), (1,)), ((), ())),
            preferred_element_type=F32,
        )
        totals[side] = term if totals[side] is None else totals[side] + term
    if has_start:
        start = refs[blocks + 2]
        totals = [total + start[side] for side, total in enumerate(totals)]
    if last:
        first = core == 0
        both = jnp.concatenate(
            [jnp.where(first, totals[0], totals[1]), jnp.where(first, totals[1], totals[0])], axis=0
        )
        out[...] = both.T.astype(out.dtype)
    else:
        for side in range(2):
            out[side] = totals[side]


def out_project(core, my_rank, attended, chips_of, codes, scales, start, last):
    count, both = attended[0].shape
    blocks = len(attended)
    columns = codes[0].shape[0]
    vmem = pl.BlockSpec(memory_space=pltpu.VMEM)
    extra = [] if start is None else [start]
    shape = (count, 2 * columns) if last else (2, columns, count)
    return pl.pallas_call(
        functools.partial(out_kernel, blocks, bool(extra), last, both // 2),
        out_shape=jax.ShapeDtypeStruct(shape, BF if last else F32),
        in_specs=[SMEM, SMEM]
        + [vmem] * blocks
        + [pl.BlockSpec(memory_space=pl.ANY)] * 2
        + [vmem] * len(extra),
        scratch_shapes=[
            pltpu.VMEM((4 * blocks, columns, both // 2), BF),
            pltpu.SemaphoreType.DMA((4 * blocks,)),
        ],
        compiler_params=PARAMS,
        cost_estimate=cost(4 * blocks * count * both * columns, 4 * blocks * both * columns),
        name="out_project",
    )(jnp.concatenate([jnp.stack([core, my_rank]), chips_of]), scales, *attended, *codes, *extra)


def rotation_tables(count):
    half_width = HEAD_SIZE // 2
    positions = (jnp.arange(count) % LEN).astype(F32)
    frequency = theta_base ** (-jnp.arange(half_width, dtype=F32) * 2.0 / HEAD_SIZE)
    angles = positions[:, None] * frequency[None, :]
    cosine, sine = jnp.cos(angles), jnp.sin(angles)
    return jnp.concatenate([cosine, cosine], axis=1), jnp.concatenate([-sine, sine], axis=1)


Z_COUNT = 4
PART_ROWS = (192, 192)
TIE_FIRST = True
TIE_SECOND = False
TIE_KEYS = True


def after(values, *earlier):
    return lax.optimization_barrier((values, *earlier))[0]


def chip_plan(
    token_ids,
    key_value_of_block,
    vocab_table,
    in_gain,
    q_gain,
    k_gain,
    wq_codes,
    wq_scale,
    key_value_codes,
    key_value_scale,
    wo_codes,
    wo_scale,
):
    ranks = lax.axis_size("fsdp")
    chips = ranks // 2
    y_count = chips // Z_COUNT
    my_rank = lax.axis_index("fsdp").astype(jnp.int32)
    core, chip = my_rank % 2, my_rank // 2
    count = token_ids.shape[0]
    vocab_rows = vocab_table.shape[0]
    same_core = [[2 * chip + side for chip in range(chips)] for side in range(2)]

    def swap(values, bits):
        return lax.ppermute(values, "fsdp", [(i, i ^ bits) for i in range(ranks)])

    def swap_groups(values):
        return lax.ppermute(values, "groups", [(0, 1), (1, 0)])

    def to_chips(values):
        return lax.all_to_all(
            values, "fsdp", split_axis=0, concat_axis=0, tiled=True, axis_index_groups=same_core
        )

    def exchange(sent):
        own = to_chips(sent)
        return own, swap(own, 1)

    owners, rows, most = find_slots(token_ids, my_rank, ranks, vocab_rows)
    sent = pick_rows(rows, jnp.int32(0), in_gain, vocab_table, chips)
    most = jnp.maximum(most, swap_groups(after(most, sent)))[0, 0]
    own, other = exchange(sent)
    normed = place_rows(owners, jnp.int32(0), core, own, other)

    def one_more(state):
        base, total = state
        more = exchange(pick_rows(rows, base, in_gain, vocab_table, chips))
        return base + SLOTS, total + place_rows(owners, base, core, *more)

    _, normed = lax.while_loop(
        lambda state: state[0].astype(F32) < most, one_more, (jnp.int32(SLOTS), normed)
    )

    near = jnp.arange(Z_COUNT, dtype=jnp.int32) * y_count
    order = after(chip, sent) ^ jnp.concatenate([near ^ 1, near])
    own_weight, away_weight, home_weight, sent_keys = prepare_weights(
        core, my_rank, order, key_value_of_block, wq_codes, wq_scale, key_value_codes, key_value_scale
    )
    away_weight = swap(after(away_weight, own), 1)
    home_weight = swap(after(home_weight, own), 1)

    half = sent_keys.shape[1] // 2
    group = lax.axis_index("groups")
    my_half = lax.dynamic_slice_in_dim(sent_keys, group * half, half, 1)
    my_z = chip // y_count

    def keys_for(z):
        return lax.dynamic_slice_in_dim(my_half, z * y_count, y_count, 0)

    by_z = [keys_for(my_z)] + [swap(keys_for(my_z ^ k), 2 * y_count * k) for k in range(1, Z_COUNT)]

    away = project(core, normed, own_weight, 0, away_weight, BF)
    got = [swap(part, 2) for part in away]
    home = project(after(core, *away), normed, own_weight, Z_COUNT, home_weight, F32)
    got[0], *by_z = lax.optimization_barrier((got[0], *by_z))

    cosine, sine = rotation_tables(count)
    heads_width = wq_codes.shape[1] // ranks
    by_z = jnp.stack(by_z)
    my_y = chip % y_count
    here = lax.dynamic_index_in_dim(by_z, my_y, 1, keepdims=False)
    there = swap(lax.dynamic_index_in_dim(by_z, 1 - my_y, 1, keepdims=False), 2)
    own_kv, other_kv, held = [], [], []
    start, share = 0, count // ranks
    for part, part_rows in enumerate(PART_ROWS):
        kept, *sums = join_partials(home[part], got[part])
        sums = [swap(value, 4 * (k + 1)) for k, value in enumerate(sums)]
        if part + 1 < len(PART_ROWS):
            got[part + 1], *sums = lax.optimization_barrier((got[part + 1], *sums))
        if part == 1 and TIE_KEYS:
            kept, there = lax.optimization_barrier((kept, there))
        queries, kv = make_heads(core, [kept, *sums], start, q_gain, k_gain, cosine, sine)
        own_kv.append(kv)
        other_kv.append(swap(kv, 1))
        kept, sent_rows = attend_heads(core, queries, start, own_kv, other_kv, share)
        held.append(jnp.concatenate([kept, swap(sent_rows, 1)], axis=1))
        start += part_rows
    wo_rows = wo_codes.T
    out_codes = [wo_rows, swap(wo_rows, 1)]

    own_keys = jnp.stack([here, there], axis=1).reshape(chips, half, HEAD_SIZE)
    far_keys = swap_groups(own_keys)
    own_keys = (own_keys, far_keys)
    synced = collect_keys(
        jnp.stack([core, group, chip]), [*own_keys, *(swap(value, 1) for value in own_keys)]
    )

    def add_blocks(total, blocks, numbers, last=False):
        chips_of = chip ^ jnp.array(numbers, jnp.int32)
        return out_project(
            core, my_rank, blocks, chips_of, out_codes, wo_scale, total, last
        )

    total = gather_project(jnp.concatenate(held, axis=0), add_blocks, y_count)
    columns = to_chips(total.reshape(chips, share, -1))
    attn_out = jnp.transpose(columns, (1, 0, 2)).reshape(share, -1)
    return attn_out, synced


def collect_kernel(info, own, far, other, other_far, out):
    core, group = info[0], info[1]
    out[0, core, group] = own[0]
    out[0, core, 1 - group] = far[0]
    out[0, 1 - core, group] = other[0]
    out[0, 1 - core, 1 - group] = other_far[0]


def collect_keys(info, parts):
    chips, half, width = parts[0].shape
    part = pl.BlockSpec((1, half, width), lambda i, info: (i ^ info[2], 0, 0))
    out = pl.pallas_call(
        collect_kernel,
        grid_spec=pltpu.PrefetchScalarGridSpec(
            num_scalar_prefetch=1,
            grid=(chips,),
            in_specs=[part] * 4,
            out_specs=pl.BlockSpec((1, 2, 2, half, width), lambda i, info: (i, 0, 0, 0, 0)),
        ),
        out_shape=jax.ShapeDtypeStruct((chips, 2, 2, half, width), BF),
        compiler_params=PARAMS,
        cost_estimate=cost(0, 16 * chips * half * width),
        name="collect_keys",
    )(info, *parts)
    return out.reshape(1, -1, width)


def hop(values, pairs, along, ranks):
    moves = [(a * along + rest, b * along + rest) for a, b in pairs for rest in range(along)]
    return lax.ppermute(values, "fsdp", moves)


NEXT = [(0, 1), (1, 0), (2, 3), (3, 2)]
MIDDLE = [(1, 2), (2, 1)]
OUTWARD = [(1, 0), (2, 3)]


def gather_project(block, add_blocks, y_count):
    along = 2 * y_count
    ranks = Z_COUNT * along
    together = lax.optimization_barrier

    def swap_y(values):
        return lax.ppermute(values, "fsdp", [(i, i ^ 2) for i in range(ranks)])

    z_index = lax.axis_index("fsdp") // along
    at_end = (z_index == 0) | (z_index == Z_COUNT - 1)
    across, one, inner = together(
        (swap_y(block), hop(block, NEXT, along, ranks), hop(block, MIDDLE, along, ranks))
    )
    total = add_blocks(None, [block, across, one], (0, 1, 2))
    two_end, two_inner, one_across = (
        hop(inner, OUTWARD, along, ranks),
        hop(one, MIDDLE, along, ranks),
        swap_y(one),
    )
    if TIE_FIRST:
        two_end, two_inner, one_across, total = together((two_end, two_inner, one_across, total))
    else:
        two_end, two_inner, one_across = together((two_end, two_inner, one_across))
    two = jnp.where(at_end, two_end, two_inner)
    three_end, two_across = hop(two, OUTWARD, along, ranks), swap_y(two)
    if TIE_SECOND:
        total = add_blocks(total, [one_across, two], (3, 4))
        three_end, two_across, total = together((three_end, two_across, total))
        rest, numbers = [two_across], (5, 6)
    else:
        three_end, two_across = together((three_end, two_across))
        rest, numbers = [one_across, two, two_across], (3, 4, 5, 6)
    three = jnp.where(at_end, three_end, inner)
    three_across = swap_y(three)
    total = add_blocks(total, [*rest, three], numbers)
    return add_blocks(total, [three_across], (7,), True)


def solution(mesh):
    sizes = dict(mesh.shape)
    small = sizes["fsdp"] == 2 * KEY_VALUE_HEADS and sizes["groups"] == 2
    return jax.shard_map(
        chip_plan if small else general_plan,
        mesh=mesh,
        in_specs=(
            P("groups"),
            P(),
            P("fsdp", None),
            P(),
            P(),
            P(),
            P("fsdp", None),
            P(),
            P("fsdp", None),
            P(),
            P(None, "fsdp"),
            P(),
        ),
        out_specs=(P(("groups", "fsdp"), None), P(("groups", "fsdp"), None, None)),
        check_vma=False,
    )
```

```python
import functools
import jax
import jax.numpy as jnp
from jax import lax
from jax.experimental import pallas as pl
from jax.experimental.pallas import tpu as pltpu
from jax.sharding import PartitionSpec as P
QUERY_HEADS = 64
KEY_VALUE_HEADS = 8
HEAD_SIZE = 128
TILE_SIDE = 128
LEN = 384


theta_base = 1000000.0
eps_norm = 1e-06


def rms_scale(values, norm_gain):
    mean_square = jnp.mean(values * values, axis=-1, keepdims=True)
    return values * lax.rsqrt(mean_square + eps_norm) * norm_gain


def rotate(values, positions):
    half_width = values.shape[-1] // 2
    frequency = theta_base ** (-jnp.arange(half_width, dtype=jnp.float32) * 2.0 / values.shape[-1])
    angles = positions[:, None] * frequency[None, :]
    cosine = jnp.cos(angles)[:, None, :]
    sine_part = jnp.sin(angles)[:, None, :]
    lower_half = values[..., :half_width]
    upper_half = values[..., half_width:]
    return jnp.concatenate(
        [
            lower_half * cosine - upper_half * sine_part,
            upper_half * cosine + lower_half * sine_part,
        ],
        axis=-1,
    )


def lookup_small(small_table, indices):
    matches = indices[..., None] == jnp.arange(small_table.shape[0], dtype=jnp.int32)
    return jnp.sum(jnp.where(matches, small_table, 0), axis=-1)


def column_scales(tile_scale, first_col, width_cols):
    per_column = jnp.repeat(tile_scale, TILE_SIDE, axis=1)
    picked = lax.dynamic_slice_in_dim(per_column, first_col, width_cols, 1)
    return jnp.repeat(picked, TILE_SIDE, axis=0)


def dequantize(quantized, scales):
    return (quantized.astype(jnp.float32) * scales).astype(jnp.bfloat16)


def attend(queries, key_rows, value_rows, prompt_count):
    token_count, head_count, head_width = queries.shape
    length = token_count // prompt_count
    query_blocks = queries.reshape(prompt_count, length, head_count, head_width)
    key_blocks = key_rows.reshape(prompt_count, length, head_width)
    value_blocks = value_rows.reshape(prompt_count, length, -1)
    scores = jnp.einsum(
        "plhd,pmd->phlm", query_blocks, key_blocks, preferred_element_type=jnp.float32
    ) * head_width ** (-0.5)
    causal = jnp.arange(length)[:, None] >= jnp.arange(length)[None, :]
    weights = jnp.where(causal, jnp.exp(scores), 0.0)
    probabilities = (weights / jnp.sum(weights, axis=-1, keepdims=True)).astype(jnp.bfloat16)
    attended_rows = jnp.einsum(
        "phlm,pmd->plhd", probabilities, value_blocks, preferred_element_type=jnp.float32
    )
    return attended_rows.astype(jnp.bfloat16).reshape(
        token_count, head_count * value_blocks.shape[-1]
    )


def general_plan(
    token_ids,
    key_value_of_block,
    vocab_table,
    in_gain,
    q_gain,
    k_gain,
    wq_codes,
    wq_scale,
    key_value_codes,
    key_value_scale,
    wo_codes,
    wo_scale,
):
    count_of_ranks = lax.axis_size("fsdp")
    my_rank = lax.axis_index("fsdp")
    duplicate_count = count_of_ranks // KEY_VALUE_HEADS
    per_key_value = QUERY_HEADS // KEY_VALUE_HEADS
    split_points = max(1, duplicate_count // per_key_value)
    heads_here = max(1, per_key_value // duplicate_count)
    value_columns = HEAD_SIZE // split_points
    query_width = heads_here * HEAD_SIZE
    local_rows = wq_codes.shape[0]
    token_count = token_ids.shape[0]
    targets = jnp.arange(count_of_ranks, dtype=jnp.int32)
    target_head = lookup_small(key_value_of_block, targets // duplicate_count)
    target_slot = targets % duplicate_count
    target_part = target_slot % split_points
    target_query = target_head * per_key_value + target_slot // split_points * heads_here
    my_head = lookup_small(key_value_of_block, my_rank // duplicate_count)
    my_slot = my_rank % duplicate_count
    my_part = my_slot % split_points
    my_query = my_head * per_key_value + my_slot // split_points * heads_here
    vocab_rows = vocab_table.shape[0]
    local_ids = token_ids - my_rank * vocab_rows
    inside = (local_ids >= 0) & (local_ids < vocab_rows)
    picked = jnp.take(vocab_table, jnp.clip(local_ids, 0, vocab_rows - 1), axis=0)
    terms = jnp.where(inside[:, None], picked, jnp.zeros_like(picked)).astype(jnp.float32)
    embedded = lax.psum(terms, "fsdp").astype(jnp.bfloat16)
    normed = rms_scale(embedded.astype(jnp.float32), in_gain).astype(jnp.bfloat16)
    query_groups = wq_codes.reshape(local_rows, QUERY_HEADS // heads_here, query_width)
    query_send = jnp.take(query_groups, target_query // heads_here, axis=1)
    key_value_heads = key_value_codes.reshape(local_rows, KEY_VALUE_HEADS, 2, HEAD_SIZE)
    key_send = jnp.take(key_value_heads[:, :, 0, :], target_head, axis=1)
    grouped_values = key_value_heads[:, :, 1, :].reshape(
        local_rows, KEY_VALUE_HEADS * split_points, value_columns
    )
    value_send = jnp.take(grouped_values, target_head * split_points + target_part, axis=1)
    both_send = jnp.concatenate([key_send, value_send], axis=2)
    query_got, kv_got = (
        lax.all_to_all(query_send, "fsdp", split_axis=1, concat_axis=0, tiled=True),
        lax.all_to_all(both_send, "fsdp", split_axis=1, concat_axis=0, tiled=True),
    )
    key_quant = kv_got[:, 0, :HEAD_SIZE]
    value_quant = kv_got[:, 0, HEAD_SIZE:]
    query_weight = dequantize(
        query_got[:, 0, :], column_scales(wq_scale, my_query * HEAD_SIZE, query_width)
    )
    key_matrix = dequantize(
        key_quant, column_scales(key_value_scale, my_head * 2 * HEAD_SIZE, HEAD_SIZE)
    )
    value_weight = dequantize(
        value_quant,
        column_scales(
            key_value_scale,
            my_head * 2 * HEAD_SIZE + HEAD_SIZE + my_part * value_columns,
            value_columns,
        ),
    )
    joined_weight = jnp.concatenate([query_weight, key_matrix, value_weight], axis=1)
    projected = jnp.dot(normed, joined_weight, preferred_element_type=jnp.float32)
    positions = (jnp.arange(token_count) % LEN).astype(jnp.float32)
    queries = rotate(
        rms_scale(projected[:, :query_width].reshape(token_count, heads_here, HEAD_SIZE), q_gain),
        positions,
    ).astype(jnp.bfloat16)
    keys_raw = projected[:, query_width : query_width + HEAD_SIZE].reshape(
        token_count, 1, HEAD_SIZE
    )
    key_rows = rotate(rms_scale(keys_raw, k_gain), positions).astype(jnp.bfloat16)[:, 0, :]
    value_rows = projected[:, query_width + HEAD_SIZE :].astype(jnp.bfloat16)
    attended_rows = attend(queries, key_rows, value_rows, token_count // LEN)
    cols_here = wo_codes.shape[1]
    local_weight = dequantize(wo_codes, column_scales(wo_scale, my_rank * cols_here, cols_here))
    ordered = jnp.take(
        local_weight.reshape(KEY_VALUE_HEADS, per_key_value * HEAD_SIZE, cols_here),
        key_value_of_block,
        axis=0,
    ).reshape(QUERY_HEADS * HEAD_SIZE, cols_here)
    columns = jnp.dot(
        lax.all_gather(attended_rows, "fsdp", axis=1, tiled=True),
        ordered,
        preferred_element_type=jnp.float32,
    )
    attn_out = lax.all_to_all(
        columns.astype(jnp.bfloat16), "fsdp", split_axis=0, concat_axis=1, tiled=True
    )
    return (attn_out, key_matrix.reshape(1, key_matrix.shape[0], HEAD_SIZE))


BF = jnp.bfloat16
F32 = jnp.float32
SLOTS = 32
GROUP_ROWS = 64
PARAMS = pltpu.CompilerParams(vmem_limit_bytes=48 << 20)
SMEM = pl.BlockSpec(memory_space=pltpu.SMEM)


COST_SHARE = 1


def cost(flops, bytes_accessed):
    return pl.CostEstimate(
        flops=flops // COST_SHARE, bytes_accessed=bytes_accessed // COST_SHARE, transcendentals=0
    )


def owner_of(ids, vocab_rows, ranks):
    owner = jnp.zeros_like(ids)
    for rank in range(1, ranks):
        owner = owner + jnp.where(ids >= float(rank * vocab_rows), 1.0, 0.0)
    return owner


def iota(shape, axis):
    return lax.broadcasted_iota(jnp.int32, shape, axis).astype(F32)


def slot_kernel(ranks, vocab_rows, info, id_row, col_out, row_out, most_out):
    count = id_row.shape[1]
    ids_r = id_row[...].astype(F32)
    ids_c = jnp.transpose(jnp.broadcast_to(ids_r, (128, count)))[:, 0:1]
    at_r, at_c = iota((count, count), 0), iota((count, count), 1)
    same = ids_c == ids_r
    first_c = jnp.min(jnp.where(same, at_c, float(count)), axis=1, keepdims=True)
    first_r = jnp.min(jnp.where(same, at_r, float(count)), axis=0, keepdims=True)
    is_first_r = first_r == iota((1, count), 1)
    is_first_c = first_c == iota((count, 1), 0)
    owner_c, owner_r = owner_of(ids_c, vocab_rows, ranks), owner_of(ids_r, vocab_rows, ranks)
    peers = owner_c == owner_r
    slot_c = jnp.sum(
        jnp.where(peers & is_first_r & (at_c < first_c), 1.0, 0.0), axis=1, keepdims=True
    )
    slot_r = jnp.sum(
        jnp.where(peers & is_first_c & (at_r < first_r), 1.0, 0.0), axis=0, keepdims=True
    )
    lane = lax.broadcasted_iota(jnp.int32, (count, 128), 1)
    col_out[...] = jnp.where(lane == 0, owner_c, jnp.where(lane == 1, slot_c, 0.0))
    me = info[0].astype(F32)
    mine = is_first_r & (owner_r == me)
    row_out[...] = jnp.zeros_like(row_out)
    row_out[0:1, :] = jnp.where(mine, slot_r, -1.0)
    row_out[1:2, :] = ids_r - me * float(vocab_rows)
    most_out[...] = jnp.broadcast_to(jnp.max(slot_r, axis=1, keepdims=True) + 1.0, (8, 128))


def find_slots(token_ids, my_rank, ranks, vocab_rows):
    count = token_ids.shape[0]
    return pl.pallas_call(
        functools.partial(slot_kernel, ranks, vocab_rows),
        out_shape=(
            jax.ShapeDtypeStruct((count, 128), F32),
            jax.ShapeDtypeStruct((8, count), F32),
            jax.ShapeDtypeStruct((8, 128), F32),
        ),
        in_specs=[SMEM, pl.BlockSpec(memory_space=pltpu.VMEM)],
        compiler_params=PARAMS,
        cost_estimate=cost(1000000, 1000000),
        name="find_slots",
    )(my_rank.reshape(1), token_ids.reshape(1, count))


def pick_kernel(width, info, rows, gain, table, *refs):
    out, picked, total = refs
    step = pl.program_id(0)
    slots = picked.shape[0]
    vocab_rows = table.shape[0]
    wanted = lax.broadcasted_iota(jnp.int32, (slots, 1), 0).astype(F32) + info[0].astype(F32)
    chosen = wanted == rows[0:1, :]
    index = jnp.sum(jnp.where(chosen, rows[1:2, :], 0.0), axis=1, keepdims=True)
    valid = jnp.sum(jnp.where(chosen, 1.0, 0.0), axis=1, keepdims=True)
    hot = (iota((slots, vocab_rows), 1) == index) & (valid > 0.5)
    block = jnp.dot(hot.astype(F32).astype(BF), table[...], preferred_element_type=F32)
    picked[:, pl.ds(pl.multiple_of(step * width, width), width)] = block

    @pl.when(step == 0)
    def _():
        total[...] = jnp.zeros_like(total)

    total[...] += jnp.sum(block * block, axis=1, keepdims=True)

    @pl.when(step == pl.num_programs(0) - 1)
    def _():
        features = picked.shape[1]
        chips, _, chip_width = out.shape
        inverse = lax.rsqrt(total[:, 0:1] * (1.0 / features) + eps_norm)
        for chip in range(chips):
            span = slice(chip * chip_width, (chip + 1) * chip_width)
            out[chip] = (picked[:, span] * inverse * gain[:, span]).astype(BF)


def pick_rows(rows, base, in_gain, vocab_table, chips):
    vocab_rows, features = vocab_table.shape
    steps = 4
    width, chip_width = features // steps, features // chips
    return pl.pallas_call(
        functools.partial(pick_kernel, width),
        grid=(steps,),
        out_shape=jax.ShapeDtypeStruct((chips, SLOTS, chip_width), BF),
        in_specs=[
            SMEM,
            pl.BlockSpec(rows.shape, lambda i: (0, 0)),
            pl.BlockSpec((1, features), lambda i: (0, 0)),
            pl.BlockSpec((vocab_rows, width), lambda i: (0, i)),
        ],
        out_specs=pl.BlockSpec((chips, SLOTS, chip_width), lambda i: (0, 0, 0)),
        scratch_shapes=[pltpu.VMEM((SLOTS, features), F32), pltpu.VMEM((SLOTS, 128), F32)],
        compiler_params=PARAMS,
        cost_estimate=cost(2 * SLOTS * vocab_rows * features, 2 * vocab_rows * features),
        name="pick_rows",
    )(base.reshape(1), rows, in_gain.reshape(1, features), vocab_table)


def place_kernel(chips, info, owners, own, other, out):
    count = owners.shape[0]
    core, base = info[0], info[1].astype(F32)
    owner, slot = owners[:, 0:1].astype(jnp.int32), owners[:, 1:2] - base
    fits = (slot >= 0.0) & (slot < float(SLOTS))
    position = (owner >> 1) * SLOTS + slot.astype(jnp.int32)
    hit = (lax.broadcasted_iota(jnp.int32, (count, chips * SLOTS), 1) == position) & fits
    total = jnp.zeros(out.shape, F32)
    for side, received in enumerate((own, other)):
        hot = jnp.where(hit & ((owner & 1) == (core ^ side)), 1.0, 0.0).astype(BF)
        total = total + jnp.dot(hot, received[...], preferred_element_type=F32)
    out[...] = total.astype(BF)


def place_rows(owners, base, core, own, other):
    count = owners.shape[0]
    chips, _, width = own.shape
    vmem = pl.BlockSpec(memory_space=pltpu.VMEM)
    return pl.pallas_call(
        functools.partial(place_kernel, chips),
        out_shape=jax.ShapeDtypeStruct((count, width), BF),
        in_specs=[SMEM, vmem, vmem, vmem],
        compiler_params=PARAMS,
        cost_estimate=cost(4 * count * chips * SLOTS * width, 6 * chips * SLOTS * width),
        name="place_rows",
    )(
        jnp.stack([core, base]),
        owners,
        own.reshape(chips * SLOTS, width),
        other.reshape(chips * SLOTS, width),
    )


def weight_kernel(flips, info, order, wq_scale, kv_scale, wq, kv, *outs):
    block = order[pl.program_id(0)]
    core, rank = info[0], info[1]
    rows = wq.shape[0]
    half = wq.shape[1] // 2
    tiles = half // TILE_SIDE
    for flip, out in zip(flips, outs):
        side = core ^ flip
        for group in range(rows // GROUP_ROWS):
            tile_row = (rank * (rows // GROUP_ROWS) + group) // 2
            span = slice(group * GROUP_ROWS, (group + 1) * GROUP_ROWS)
            for tile in range(tiles):
                scale = wq_scale[tile_row, (2 * block + side) * tiles + tile]
                start = pl.multiple_of(side * half + tile * TILE_SIDE, TILE_SIDE)
                codes = wq[span, pl.ds(start, TILE_SIDE)].astype(F32)
                out[0, span, tile * TILE_SIDE : (tile + 1) * TILE_SIDE] = (codes * scale).astype(BF)
            scale = kv_scale[tile_row, 2 * block + side]
            start = pl.multiple_of(side * TILE_SIDE, TILE_SIDE)
            codes = kv[span, pl.ds(start, TILE_SIDE)].astype(F32)
            out[0, span, half : half + TILE_SIDE] = (codes * scale).astype(BF)


def prepare_weights(flips, core, my_rank, order, chips, wq_codes, wq_scale, kv_codes, kv_scale):
    rows = wq_codes.shape[0]
    half = wq_codes.shape[1] // (2 * chips)
    blocks = order.shape[0]
    block = (1, rows, half + TILE_SIDE)
    return pl.pallas_call(
        functools.partial(weight_kernel, flips),
        grid_spec=pltpu.PrefetchScalarGridSpec(
            num_scalar_prefetch=4,
            grid=(blocks,),
            in_specs=[
                pl.BlockSpec((rows, 2 * half), lambda i, info, order, *_: (0, order[i])),
                pl.BlockSpec((rows, 2 * TILE_SIDE), lambda i, info, order, *_: (0, order[i])),
            ],
            out_specs=[pl.BlockSpec(block, lambda i, *_: (i, 0, 0))] * len(flips),
        ),
        out_shape=[jax.ShapeDtypeStruct((blocks, *block[1:]), BF)] * len(flips),
        compiler_params=PARAMS,
        cost_estimate=cost(rows * wq_codes.shape[1] * 4, rows * wq_codes.shape[1] * 3),
        name="prepare_weights",
    )(jnp.stack([core, my_rank]), order, wq_scale, kv_scale, wq_codes, kv_codes)


def key_kernel(info, head_of, kv_scale, codes, out):
    step = pl.program_id(0)
    rows = codes.shape[0]
    for group in range(rows // GROUP_ROWS):
        tile_row = (info[0] * (rows // GROUP_ROWS) + group) // 2
        span = slice(group * GROUP_ROWS, (group + 1) * GROUP_ROWS)
        scale = kv_scale[tile_row, 2 * head_of[step]]
        out[0, span, :] = (codes[span, :].astype(F32) * scale).astype(BF)


def prepare_keys(my_rank, key_value_of_block, kv_codes, kv_scale):
    rows = kv_codes.shape[0]
    chips = key_value_of_block.shape[0]
    return pl.pallas_call(
        key_kernel,
        grid_spec=pltpu.PrefetchScalarGridSpec(
            num_scalar_prefetch=3,
            grid=(chips,),
            in_specs=[
                pl.BlockSpec((rows, TILE_SIDE), lambda i, info, head_of, *_: (0, 2 * head_of[i]))
            ],
            out_specs=pl.BlockSpec((1, rows, TILE_SIDE), lambda i, *_: (i, 0, 0)),
        ),
        out_shape=jax.ShapeDtypeStruct((chips, rows, TILE_SIDE), BF),
        compiler_params=PARAMS,
        cost_estimate=cost(2 * chips * rows * TILE_SIDE, 4 * chips * rows * TILE_SIDE),
        name="prepare_keys",
    )(my_rank.reshape(1), key_value_of_block, kv_scale, kv_codes)


def project_kernel(info, normed, own, other, first, sent, kept, weight):
    step = pl.program_id(0)
    rows = own.shape[1]
    core = info[0]
    weight[pl.ds(pl.multiple_of(core * rows, GROUP_ROWS), rows), :] = own[0]
    weight[pl.ds(pl.multiple_of((1 - core) * rows, GROUP_ROWS), rows), :] = other[0]
    product = jnp.dot(normed[...], weight[...], preferred_element_type=F32)
    first[0] = product[: first.shape[1]].astype(first.dtype)
    second = product[first.shape[1] :]

    @pl.when(step < 2)
    def _():
        sent[0] = second.astype(BF)

    @pl.when(step >= 2)
    def _():
        kept[0] = second


def project(core, normed, own, other, first_type):
    count, width = normed.shape
    blocks, rows, columns = other.shape
    first, second = PART_ROWS
    return pl.pallas_call(
        project_kernel,
        grid=(blocks,),
        in_specs=[
            SMEM,
            pl.BlockSpec((count, width), lambda k: (0, 0)),
            pl.BlockSpec((1, rows, columns), lambda k: (k, 0, 0)),
            pl.BlockSpec((1, rows, columns), lambda k: (k, 0, 0)),
        ],
        out_specs=[
            pl.BlockSpec((1, first, columns), lambda k: (k, 0, 0)),
            pl.BlockSpec((1, second, columns), lambda k: (jnp.minimum(k, 1), 0, 0)),
            pl.BlockSpec((1, second, columns), lambda k: (jnp.maximum(k - 2, 0), 0, 0)),
        ],
        scratch_shapes=[pltpu.VMEM((width, columns), BF)],
        out_shape=[
            jax.ShapeDtypeStruct((blocks, first, columns), first_type),
            jax.ShapeDtypeStruct((2, second, columns), BF),
            jax.ShapeDtypeStruct((2, second, columns), F32),
        ],
        compiler_params=PARAMS,
        cost_estimate=cost(
            2 * blocks * count * width * columns, 2 * blocks * columns * (width + count)
        ),
        name="project",
    )(core.reshape(1), normed, own, other)


def join_kernel(own, got, kept, near, far, middle):
    for block, out in enumerate((near, far, kept, middle)):
        out[...] = (own[block] + got[block].astype(F32)).astype(out.dtype)


def join_partials(own, got):
    _, rows, columns = got.shape
    vmem = pl.BlockSpec(memory_space=pltpu.VMEM)
    sent = jax.ShapeDtypeStruct((rows, columns), BF)
    kept, near, far, middle = pl.pallas_call(
        join_kernel,
        in_specs=[vmem, vmem],
        out_shape=[jax.ShapeDtypeStruct((rows, columns), F32), sent, sent, sent],
        compiler_params=PARAMS,
        cost_estimate=cost(8 * rows * columns, 32 * rows * columns),
        name="join_partials",
    )(own, got)
    return kept, near, middle, far


def pair_kernel(away, home, got_away, got_home, sent, kept):
    sent[...] = (away[...] + got_away[...].astype(F32)).astype(BF)
    kept[...] = home[...] + got_home[...].astype(F32)


def join_pair(away, home, got_away, got_home):
    vmem = pl.BlockSpec(memory_space=pltpu.VMEM)
    return pl.pallas_call(
        pair_kernel,
        in_specs=[vmem] * 4,
        out_shape=[jax.ShapeDtypeStruct(away.shape, BF), jax.ShapeDtypeStruct(home.shape, F32)],
        compiler_params=PARAMS,
        cost_estimate=cost(2 * home.size, 16 * home.size),
        name="join_pair",
    )(away, home, got_away, got_home)


def last_kernel(kept, got, own, sent):
    own[...] = kept[0] + got[0].astype(F32)
    sent[...] = (kept[1] + got[1].astype(F32)).astype(BF)


def join_last(kept, got):
    _, rows, columns = kept.shape
    vmem = pl.BlockSpec(memory_space=pltpu.VMEM)
    return pl.pallas_call(
        last_kernel,
        in_specs=[vmem, vmem],
        out_shape=[
            jax.ShapeDtypeStruct((rows, columns), F32),
            jax.ShapeDtypeStruct((rows, columns), BF),
        ],
        compiler_params=PARAMS,
        cost_estimate=cost(2 * kept.size, 8 * kept.size),
        name="join_last",
    )(kept, got)


def turn(values, cosine, sine):
    return values * cosine + pltpu.roll(values, HEAD_SIZE // 2, 1) * sine


def normalise(values, gain):
    mean_square = jnp.mean(values * values, axis=-1, keepdims=True)
    return values * lax.rsqrt(mean_square + eps_norm) * gain


def heads_kernel(start, info, *refs):
    *parts, q_gain, k_gain, cosine, sine, q_out, kv_out = refs
    total = parts[0][...]
    for part in parts[1:]:
        total = total + part[...].astype(F32)
    heads, count, _ = q_out.shape
    cos, sin = cosine[start : start + count, :], sine[start : start + count, :]
    last = total[:, heads * HEAD_SIZE :]

    @pl.when(info[0] == 0)
    def _():
        kv_out[...] = turn(normalise(last, k_gain[...]), cos, sin).astype(BF)

    @pl.when(info[0] == 1)
    def _():
        kv_out[...] = last.astype(BF)

    for head in range(heads):
        values = total[:, head * HEAD_SIZE : (head + 1) * HEAD_SIZE]
        q_out[head] = turn(normalise(values, q_gain[...]), cos, sin).astype(BF)


def make_heads(core, parts, start, q_gain, k_gain, cosine, sine):
    count, columns = parts[0].shape
    heads = columns // HEAD_SIZE - 1
    vmem = pl.BlockSpec(memory_space=pltpu.VMEM)
    return pl.pallas_call(
        functools.partial(heads_kernel, start),
        out_shape=(
            jax.ShapeDtypeStruct((heads, count, HEAD_SIZE), BF),
            jax.ShapeDtypeStruct((count, HEAD_SIZE), BF),
        ),
        in_specs=[SMEM] + [vmem] * (len(parts) + 4),
        compiler_params=PARAMS,
        cost_estimate=cost(20 * count * columns, 14 * count * columns),
        name="make_heads",
    )(core.reshape(1), *parts, q_gain.reshape(1, -1), k_gain.reshape(1, -1), cosine, sine)


def attend_kernel(length, start, share, info, queries, *refs):
    *rows, kept, sent = refs
    parts = len(rows) // 2
    own = jnp.concatenate([ref[...] for ref in rows[:parts]], axis=0)
    other = jnp.concatenate([ref[...] for ref in rows[parts:]], axis=0)
    first = info[0] == 0
    keys, values = jnp.where(first, own, other), jnp.where(first, other, own)
    count = queries.shape[1]
    here = lax.broadcasted_iota(jnp.int32, (count, keys.shape[0]), 0) + start
    there = lax.broadcasted_iota(jnp.int32, (count, keys.shape[0]), 1)
    allowed = here >= there
    for prompt in range(1, (start + count + length - 1) // length):
        allowed = allowed & ((here < prompt * length) | (there >= prompt * length))
    for head in range(queries.shape[0]):
        scores = lax.dot_general(
            queries[head], keys, (((1,), (1,)), ((), ())), preferred_element_type=F32
        ) * HEAD_SIZE ** (-0.5)
        weights = jnp.where(allowed, jnp.exp(scores), 0.0)
        probabilities = (weights / jnp.sum(weights, axis=-1, keepdims=True)).astype(BF)
        result = jnp.dot(probabilities, values, preferred_element_type=F32)
        shares = [result[at : at + share] for at in range(0, count, share)]
        even = jnp.concatenate(shares[0::2], axis=0)
        odd = jnp.concatenate(shares[1::2], axis=0)
        span = slice(head * HEAD_SIZE, (head + 1) * HEAD_SIZE)
        kept[:, span] = jnp.where(first, even, odd).astype(BF)
        sent[:, span] = jnp.where(first, odd, even).astype(BF)


def attend_heads(core, queries, start, own, other, share):
    heads, count, width = queries.shape
    vmem = pl.BlockSpec(memory_space=pltpu.VMEM)
    return pl.pallas_call(
        functools.partial(attend_kernel, LEN, start, share),
        out_shape=[jax.ShapeDtypeStruct((count // 2, heads * width), BF)] * 2,
        in_specs=[SMEM] + [vmem] * (1 + len(own) + len(other)),
        compiler_params=PARAMS,
        cost_estimate=cost(4 * heads * count * (start + count) * width, 4 * heads * count * width),
        name="attend",
    )(core.reshape(1), queries, *own, *other)


def out_kernel(blocks, has_start, last, width, info, scales, *refs):
    attended = refs[:blocks]
    codes = refs[blocks : blocks + 2]
    out, held, arrived = refs[-3:]
    core, my_rank = info[0], info[1]
    columns = held.shape[1]
    tiles = width // TILE_SIDE
    pieces = [(block, half, side) for block in range(blocks) for half in range(2) for side in range(2)]
    copies = []
    for number, (block, half, side) in enumerate(pieces):
        start = (2 * info[2 + block] + (core ^ half)) * width
        copy = pltpu.make_async_copy(
            codes[side].at[:, pl.ds(pl.multiple_of(start, width), width)],
            held.at[number],
            arrived.at[number],
        )
        copy.start()
        copies.append(copy)
    totals = [None, None]
    for number, (block, half, side) in enumerate(pieces):
        rows = attended[block][:, half * width : (half + 1) * width]
        first_tile = (2 * info[2 + block] + (core ^ half)) * tiles
        copies[number].wait()
        weight = []
        for group in range(columns // GROUP_ROWS):
            column = ((my_rank ^ side) * columns + group * GROUP_ROWS) // TILE_SIDE
            span = slice(group * GROUP_ROWS, (group + 1) * GROUP_ROWS)
            weight.append(
                jnp.concatenate(
                    [
                        (
                            held[number, span, tile * TILE_SIDE : (tile + 1) * TILE_SIDE].astype(F32)
                            * scales[first_tile + tile, column]
                        ).astype(BF)
                        for tile in range(tiles)
                    ],
                    axis=1,
                )
            )
        term = lax.dot_general(
            jnp.concatenate(weight, axis=0),
            rows,
            (((1,), (1,)), ((), ())),
            preferred_element_type=F32,
        )
        totals[side] = term if totals[side] is None else totals[side] + term
    if has_start:
        start = refs[blocks + 2]
        totals = [total + start[side] for side, total in enumerate(totals)]
    if last:
        first = core == 0
        both = jnp.concatenate(
            [jnp.where(first, totals[0], totals[1]), jnp.where(first, totals[1], totals[0])], axis=0
        )
        out[...] = both.T.astype(out.dtype)
    else:
        for side in range(2):
            out[side] = totals[side]


def out_project(core, my_rank, attended, chips_of, codes, scales, start, last):
    count, both = attended[0].shape
    blocks = len(attended)
    columns = codes[0].shape[0]
    vmem = pl.BlockSpec(memory_space=pltpu.VMEM)
    extra = [] if start is None else [start]
    shape = (count, 2 * columns) if last else (2, columns, count)
    return pl.pallas_call(
        functools.partial(out_kernel, blocks, bool(extra), last, both // 2),
        out_shape=jax.ShapeDtypeStruct(shape, BF if last else F32),
        in_specs=[SMEM, SMEM]
        + [vmem] * blocks
        + [pl.BlockSpec(memory_space=pl.ANY)] * 2
        + [vmem] * len(extra),
        scratch_shapes=[
            pltpu.VMEM((4 * blocks, columns, both // 2), BF),
            pltpu.SemaphoreType.DMA((4 * blocks,)),
        ],
        compiler_params=PARAMS,
        cost_estimate=cost(4 * blocks * count * both * columns, 4 * blocks * both * columns),
        name="out_project",
    )(jnp.concatenate([jnp.stack([core, my_rank]), chips_of]), scales, *attended, *codes, *extra)


def rotation_tables(count):
    half_width = HEAD_SIZE // 2
    positions = (jnp.arange(count) % LEN).astype(F32)
    frequency = theta_base ** (-jnp.arange(half_width, dtype=F32) * 2.0 / HEAD_SIZE)
    angles = positions[:, None] * frequency[None, :]
    cosine, sine = jnp.cos(angles), jnp.sin(angles)
    return jnp.concatenate([cosine, cosine], axis=1), jnp.concatenate([-sine, sine], axis=1)


Z_COUNT = 4
PART_ROWS = (192, 192)
TIE_FIRST = True
TIE_SECOND = False
TIE_AWAY = True
TIE_SUMS = False


def after(values, *earlier):
    return lax.optimization_barrier((values, *earlier))[0]


def chip_plan(
    token_ids,
    key_value_of_block,
    vocab_table,
    in_gain,
    q_gain,
    k_gain,
    wq_codes,
    wq_scale,
    key_value_codes,
    key_value_scale,
    wo_codes,
    wo_scale,
):
    ranks = lax.axis_size("fsdp")
    chips = ranks // 2
    y_count = chips // Z_COUNT
    my_rank = lax.axis_index("fsdp").astype(jnp.int32)
    core, chip = my_rank % 2, my_rank // 2
    count = token_ids.shape[0]
    vocab_rows = vocab_table.shape[0]
    same_core = [[2 * chip + side for chip in range(chips)] for side in range(2)]

    def swap(values, bits):
        return lax.ppermute(values, "fsdp", [(i, i ^ bits) for i in range(ranks)])

    def swap_groups(values):
        return lax.ppermute(values, "groups", [(0, 1), (1, 0)])

    def to_chips(values):
        return lax.all_to_all(
            values, "fsdp", split_axis=0, concat_axis=0, tiled=True, axis_index_groups=same_core
        )

    def exchange(sent):
        own = to_chips(sent)
        return own, swap(own, 1)

    owners, rows, most = find_slots(token_ids, my_rank, ranks, vocab_rows)
    sent = pick_rows(rows, jnp.int32(0), in_gain, vocab_table, chips)
    most = jnp.maximum(most, swap_groups(after(most, sent)))[0, 0]

    sent_keys = prepare_keys(
        after(my_rank, sent), key_value_of_block, key_value_codes, key_value_scale
    )
    half = sent_keys.shape[1] // 2
    group = lax.axis_index("groups")
    my_half = lax.dynamic_slice_in_dim(sent_keys, group * half, half, 1)
    my_z = chip // y_count

    def keys_for(z):
        return lax.dynamic_slice_in_dim(my_half, z * y_count, y_count, 0)

    by_z = [keys_for(my_z)] + [swap(keys_for(my_z ^ k), 2 * y_count * k) for k in range(1, Z_COUNT)]

    near = jnp.array([1, 3, 0, 2], jnp.int32) * y_count

    def weights_of(flips, order):
        return prepare_weights(
            flips,
            core,
            my_rank,
            order,
            chips,
            wq_codes,
            wq_scale,
            key_value_codes,
            key_value_scale,
        )

    away_own, away_other = weights_of((0, 1), after(chip, sent) ^ 1 ^ near)
    (home_other,) = weights_of((1,), after(chip, sent) ^ near)
    own = to_chips(sent)
    own, away_other, home_other, *by_z = lax.optimization_barrier(
        (own, away_other, home_other, *by_z)
    )
    other = swap(own, 1)
    normed = place_rows(owners, jnp.int32(0), core, own, other)

    def one_more(state):
        base, total = state
        more = exchange(pick_rows(rows, base, in_gain, vocab_table, chips))
        return base + SLOTS, total + place_rows(owners, base, core, *more)

    _, normed = lax.while_loop(
        lambda state: state[0].astype(F32) < most, one_more, (jnp.int32(SLOTS), normed)
    )

    away_other = swap(away_other, 1)
    home_other = swap(home_other, 1)
    away, away_sent, away_kept = project(core, normed, away_own, away_other, BF)
    got = swap(away, 2)
    got_away = swap(away_sent, 2 * y_count)
    (home_own,) = weights_of((0,), after(chip, away) ^ near)
    home, home_sent, home_kept = project(
        after(core, away), normed, home_own, home_other, F32
    )
    got_home = swap(home_sent, 2 * y_count)
    if TIE_AWAY:
        got, got_away = lax.optimization_barrier((got, got_away))

    cosine, sine = rotation_tables(count)
    heads_width = wq_codes.shape[1] // ranks
    by_z = jnp.stack(by_z)
    my_y = chip % y_count
    here = lax.dynamic_index_in_dim(by_z, my_y, 1, keepdims=False)
    there = swap(lax.dynamic_index_in_dim(by_z, 1 - my_y, 1, keepdims=False), 2)
    wo_rows = wo_codes.T
    out_codes = [wo_rows, swap(wo_rows, 1)]
    own_kv, other_kv, held = [], [], []
    share = count // ranks

    def attend_part(start, sums):
        queries, kv = make_heads(core, sums, start, q_gain, k_gain, cosine, sine)
        own_kv.append(kv)
        other_kv.append(swap(kv, 1))
        kept, sent_rows = attend_heads(core, queries, start, own_kv, other_kv, share)
        held.append(jnp.concatenate([kept, swap(sent_rows, 1)], axis=1))

    kept, *sums = join_partials(home, got)
    got_away, got_home = lax.optimization_barrier((got_away, got_home, *sums))[:2]
    pair_sent, pair_kept = join_pair(away_kept, home_kept, got_away, got_home)
    sums = [swap(value, 2 * y_count * (k + 1)) for k, value in enumerate(sums)]
    pair_got = swap(pair_sent, 2)
    if TIE_SUMS:
        pair_got, *sums = lax.optimization_barrier((pair_got, *sums))
    attend_part(0, [kept, *sums])
    kept, last_sent = join_last(pair_kept, pair_got)
    last_got = swap(last_sent, 4 * y_count)
    kept, there = lax.optimization_barrier((kept, there))
    attend_part(PART_ROWS[0], [kept, last_got])

    def add_blocks(total, blocks, numbers, last=False):
        chips_of = chip ^ jnp.array(numbers, jnp.int32)
        return out_project(
            core, my_rank, blocks, chips_of, out_codes, wo_scale, total, last
        )

    own_keys = jnp.stack([here, there], axis=1).reshape(chips, half, HEAD_SIZE)

    def finish_keys(far_keys):
        return collect_keys(
            jnp.stack([core, group, chip]),
            [own_keys, far_keys, swap(own_keys, 1), swap(far_keys, 1)],
        )

    total, synced = gather_project(
        jnp.concatenate(held, axis=0), add_blocks, y_count, swap_groups(own_keys), finish_keys
    )
    columns = to_chips(total.reshape(chips, share, -1))
    attn_out = jnp.transpose(columns, (1, 0, 2)).reshape(share, -1)
    return attn_out, synced


def collect_kernel(info, own, far, other, other_far, out):
    core, group = info[0], info[1]
    out[0, core, group] = own[0]
    out[0, core, 1 - group] = far[0]
    out[0, 1 - core, group] = other[0]
    out[0, 1 - core, 1 - group] = other_far[0]


def collect_keys(info, parts):
    chips, half, width = parts[0].shape
    part = pl.BlockSpec((1, half, width), lambda i, info: (i ^ info[2], 0, 0))
    out = pl.pallas_call(
        collect_kernel,
        grid_spec=pltpu.PrefetchScalarGridSpec(
            num_scalar_prefetch=1,
            grid=(chips,),
            in_specs=[part] * 4,
            out_specs=pl.BlockSpec((1, 2, 2, half, width), lambda i, info: (i, 0, 0, 0, 0)),
        ),
        out_shape=jax.ShapeDtypeStruct((chips, 2, 2, half, width), BF),
        compiler_params=PARAMS,
        cost_estimate=cost(0, 16 * chips * half * width),
        name="collect_keys",
    )(info, *parts)
    return out.reshape(1, -1, width)


def hop(values, pairs, along, ranks):
    moves = [(a * along + rest, b * along + rest) for a, b in pairs for rest in range(along)]
    return lax.ppermute(values, "fsdp", moves)


NEXT = [(0, 1), (1, 0), (2, 3), (3, 2)]
MIDDLE = [(1, 2), (2, 1)]
OUTWARD = [(1, 0), (2, 3)]


def gather_project(block, add_blocks, y_count, beside, finish):
    along = 2 * y_count
    ranks = Z_COUNT * along
    together = lax.optimization_barrier

    def swap_y(values):
        return lax.ppermute(values, "fsdp", [(i, i ^ 2) for i in range(ranks)])

    z_index = lax.axis_index("fsdp") // along
    at_end = (z_index == 0) | (z_index == Z_COUNT - 1)
    across, one, inner = together(
        (swap_y(block), hop(block, NEXT, along, ranks), hop(block, MIDDLE, along, ranks))
    )
    total = add_blocks(None, [block, across, one], (0, 1, 2))
    two_end, two_inner, one_across = (
        hop(inner, OUTWARD, along, ranks),
        hop(one, MIDDLE, along, ranks),
        swap_y(one),
    )
    if TIE_FIRST:
        two_end, two_inner, one_across, total, beside = together(
            (two_end, two_inner, one_across, total, beside)
        )
    else:
        two_end, two_inner, one_across, beside = together(
            (two_end, two_inner, one_across, beside)
        )
    finished = finish(beside)
    two = jnp.where(at_end, two_end, two_inner)
    three_end, two_across = hop(two, OUTWARD, along, ranks), swap_y(two)
    if TIE_SECOND:
        total = add_blocks(total, [one_across, two], (3, 4))
        three_end, two_across, total, finished = together(
            (three_end, two_across, total, finished)
        )
        rest, numbers = [two_across], (5, 6)
    else:
        three_end, two_across, finished = together((three_end, two_across, finished))
        rest, numbers = [one_across, two, two_across], (3, 4, 5, 6)
    three = jnp.where(at_end, three_end, inner)
    three_across = swap_y(three)
    total = add_blocks(total, [*rest, three], numbers)
    return add_blocks(total, [three_across], (7,), True), finished


def solution(mesh):
    sizes = dict(mesh.shape)
    small = sizes["fsdp"] == 2 * KEY_VALUE_HEADS and sizes["groups"] == 2
    return jax.shard_map(
        chip_plan if small else general_plan,
        mesh=mesh,
        in_specs=(
            P("groups"),
            P(),
            P("fsdp", None),
            P(),
            P(),
            P(),
            P("fsdp", None),
            P(),
            P("fsdp", None),
            P(),
            P(None, "fsdp"),
            P(),
        ),
        out_specs=(P(("groups", "fsdp"), None), P(("groups", "fsdp"), None, None)),
        check_vma=False,
    )
```

```python
import functools
import jax
import jax.numpy as jnp
from jax import lax
from jax.experimental import pallas as pl
from jax.experimental.pallas import tpu as pltpu
from jax.sharding import PartitionSpec as P
QUERY_HEADS = 64
KEY_VALUE_HEADS = 8
HEAD_SIZE = 128
TILE_SIDE = 128
LEN = 384


theta_base = 1000000.0
eps_norm = 1e-06


def rms_scale(values, norm_gain):
    mean_square = jnp.mean(values * values, axis=-1, keepdims=True)
    return values * lax.rsqrt(mean_square + eps_norm) * norm_gain


def rotate(values, positions):
    half_width = values.shape[-1] // 2
    frequency = theta_base ** (-jnp.arange(half_width, dtype=jnp.float32) * 2.0 / values.shape[-1])
    angles = positions[:, None] * frequency[None, :]
    cosine = jnp.cos(angles)[:, None, :]
    sine_part = jnp.sin(angles)[:, None, :]
    lower_half = values[..., :half_width]
    upper_half = values[..., half_width:]
    return jnp.concatenate(
        [
            lower_half * cosine - upper_half * sine_part,
            upper_half * cosine + lower_half * sine_part,
        ],
        axis=-1,
    )


def lookup_small(small_table, indices):
    matches = indices[..., None] == jnp.arange(small_table.shape[0], dtype=jnp.int32)
    return jnp.sum(jnp.where(matches, small_table, 0), axis=-1)


def column_scales(tile_scale, first_col, width_cols):
    per_column = jnp.repeat(tile_scale, TILE_SIDE, axis=1)
    picked = lax.dynamic_slice_in_dim(per_column, first_col, width_cols, 1)
    return jnp.repeat(picked, TILE_SIDE, axis=0)


def dequantize(quantized, scales):
    return (quantized.astype(jnp.float32) * scales).astype(jnp.bfloat16)


def attend(queries, key_rows, value_rows, prompt_count):
    token_count, head_count, head_width = queries.shape
    length = token_count // prompt_count
    query_blocks = queries.reshape(prompt_count, length, head_count, head_width)
    key_blocks = key_rows.reshape(prompt_count, length, head_width)
    value_blocks = value_rows.reshape(prompt_count, length, -1)
    scores = jnp.einsum(
        "plhd,pmd->phlm", query_blocks, key_blocks, preferred_element_type=jnp.float32
    ) * head_width ** (-0.5)
    causal = jnp.arange(length)[:, None] >= jnp.arange(length)[None, :]
    weights = jnp.where(causal, jnp.exp(scores), 0.0)
    probabilities = (weights / jnp.sum(weights, axis=-1, keepdims=True)).astype(jnp.bfloat16)
    attended_rows = jnp.einsum(
        "phlm,pmd->plhd", probabilities, value_blocks, preferred_element_type=jnp.float32
    )
    return attended_rows.astype(jnp.bfloat16).reshape(
        token_count, head_count * value_blocks.shape[-1]
    )


def general_plan(
    token_ids,
    key_value_of_block,
    vocab_table,
    in_gain,
    q_gain,
    k_gain,
    wq_codes,
    wq_scale,
    key_value_codes,
    key_value_scale,
    wo_codes,
    wo_scale,
):
    count_of_ranks = lax.axis_size("fsdp")
    my_rank = lax.axis_index("fsdp")
    duplicate_count = count_of_ranks // KEY_VALUE_HEADS
    per_key_value = QUERY_HEADS // KEY_VALUE_HEADS
    split_points = max(1, duplicate_count // per_key_value)
    heads_here = max(1, per_key_value // duplicate_count)
    value_columns = HEAD_SIZE // split_points
    query_width = heads_here * HEAD_SIZE
    local_rows = wq_codes.shape[0]
    token_count = token_ids.shape[0]
    targets = jnp.arange(count_of_ranks, dtype=jnp.int32)
    target_head = lookup_small(key_value_of_block, targets // duplicate_count)
    target_slot = targets % duplicate_count
    target_part = target_slot % split_points
    target_query = target_head * per_key_value + target_slot // split_points * heads_here
    my_head = lookup_small(key_value_of_block, my_rank // duplicate_count)
    my_slot = my_rank % duplicate_count
    my_part = my_slot % split_points
    my_query = my_head * per_key_value + my_slot // split_points * heads_here
    vocab_rows = vocab_table.shape[0]
    local_ids = token_ids - my_rank * vocab_rows
    inside = (local_ids >= 0) & (local_ids < vocab_rows)
    picked = jnp.take(vocab_table, jnp.clip(local_ids, 0, vocab_rows - 1), axis=0)
    terms = jnp.where(inside[:, None], picked, jnp.zeros_like(picked)).astype(jnp.float32)
    embedded = lax.psum(terms, "fsdp").astype(jnp.bfloat16)
    normed = rms_scale(embedded.astype(jnp.float32), in_gain).astype(jnp.bfloat16)
    query_groups = wq_codes.reshape(local_rows, QUERY_HEADS // heads_here, query_width)
    query_send = jnp.take(query_groups, target_query // heads_here, axis=1)
    key_value_heads = key_value_codes.reshape(local_rows, KEY_VALUE_HEADS, 2, HEAD_SIZE)
    key_send = jnp.take(key_value_heads[:, :, 0, :], target_head, axis=1)
    grouped_values = key_value_heads[:, :, 1, :].reshape(
        local_rows, KEY_VALUE_HEADS * split_points, value_columns
    )
    value_send = jnp.take(grouped_values, target_head * split_points + target_part, axis=1)
    both_send = jnp.concatenate([key_send, value_send], axis=2)
    query_got, kv_got = (
        lax.all_to_all(query_send, "fsdp", split_axis=1, concat_axis=0, tiled=True),
        lax.all_to_all(both_send, "fsdp", split_axis=1, concat_axis=0, tiled=True),
    )
    key_quant = kv_got[:, 0, :HEAD_SIZE]
    value_quant = kv_got[:, 0, HEAD_SIZE:]
    query_weight = dequantize(
        query_got[:, 0, :], column_scales(wq_scale, my_query * HEAD_SIZE, query_width)
    )
    key_matrix = dequantize(
        key_quant, column_scales(key_value_scale, my_head * 2 * HEAD_SIZE, HEAD_SIZE)
    )
    value_weight = dequantize(
        value_quant,
        column_scales(
            key_value_scale,
            my_head * 2 * HEAD_SIZE + HEAD_SIZE + my_part * value_columns,
            value_columns,
        ),
    )
    joined_weight = jnp.concatenate([query_weight, key_matrix, value_weight], axis=1)
    projected = jnp.dot(normed, joined_weight, preferred_element_type=jnp.float32)
    positions = (jnp.arange(token_count) % LEN).astype(jnp.float32)
    queries = rotate(
        rms_scale(projected[:, :query_width].reshape(token_count, heads_here, HEAD_SIZE), q_gain),
        positions,
    ).astype(jnp.bfloat16)
    keys_raw = projected[:, query_width : query_width + HEAD_SIZE].reshape(
        token_count, 1, HEAD_SIZE
    )
    key_rows = rotate(rms_scale(keys_raw, k_gain), positions).astype(jnp.bfloat16)[:, 0, :]
    value_rows = projected[:, query_width + HEAD_SIZE :].astype(jnp.bfloat16)
    attended_rows = attend(queries, key_rows, value_rows, token_count // LEN)
    cols_here = wo_codes.shape[1]
    local_weight = dequantize(wo_codes, column_scales(wo_scale, my_rank * cols_here, cols_here))
    ordered = jnp.take(
        local_weight.reshape(KEY_VALUE_HEADS, per_key_value * HEAD_SIZE, cols_here),
        key_value_of_block,
        axis=0,
    ).reshape(QUERY_HEADS * HEAD_SIZE, cols_here)
    columns = jnp.dot(
        lax.all_gather(attended_rows, "fsdp", axis=1, tiled=True),
        ordered,
        preferred_element_type=jnp.float32,
    )
    attn_out = lax.all_to_all(
        columns.astype(jnp.bfloat16), "fsdp", split_axis=0, concat_axis=1, tiled=True
    )
    return (attn_out, key_matrix.reshape(1, key_matrix.shape[0], HEAD_SIZE))


BF = jnp.bfloat16
F32 = jnp.float32
SLOTS = 32
GROUP_ROWS = 64
PARAMS = pltpu.CompilerParams(vmem_limit_bytes=48 << 20)
SMEM = pl.BlockSpec(memory_space=pltpu.SMEM)


COST_SHARE = 1


def cost(flops, bytes_accessed):
    return pl.CostEstimate(
        flops=flops // COST_SHARE, bytes_accessed=bytes_accessed // COST_SHARE, transcendentals=0
    )


def owner_of(ids, vocab_rows, ranks):
    owner = jnp.zeros_like(ids)
    for rank in range(1, ranks):
        owner = owner + jnp.where(ids >= float(rank * vocab_rows), 1.0, 0.0)
    return owner


def iota(shape, axis):
    return lax.broadcasted_iota(jnp.int32, shape, axis).astype(F32)


def slot_kernel(ranks, vocab_rows, info, id_row, col_out, row_out, most_out):
    count = id_row.shape[1]
    ids_r = id_row[...].astype(F32)
    ids_c = jnp.transpose(jnp.broadcast_to(ids_r, (128, count)))[:, 0:1]
    at_r, at_c = iota((count, count), 0), iota((count, count), 1)
    same = ids_c == ids_r
    first_c = jnp.min(jnp.where(same, at_c, float(count)), axis=1, keepdims=True)
    first_r = jnp.min(jnp.where(same, at_r, float(count)), axis=0, keepdims=True)
    is_first_r = first_r == iota((1, count), 1)
    is_first_c = first_c == iota((count, 1), 0)
    owner_c, owner_r = owner_of(ids_c, vocab_rows, ranks), owner_of(ids_r, vocab_rows, ranks)
    peers = owner_c == owner_r
    slot_c = jnp.sum(
        jnp.where(peers & is_first_r & (at_c < first_c), 1.0, 0.0), axis=1, keepdims=True
    )
    slot_r = jnp.sum(
        jnp.where(peers & is_first_c & (at_r < first_r), 1.0, 0.0), axis=0, keepdims=True
    )
    lane = lax.broadcasted_iota(jnp.int32, (count, 128), 1)
    col_out[...] = jnp.where(lane == 0, owner_c, jnp.where(lane == 1, slot_c, 0.0))
    me = info[0].astype(F32)
    mine = is_first_r & (owner_r == me)
    row_out[...] = jnp.zeros_like(row_out)
    row_out[0:1, :] = jnp.where(mine, slot_r, -1.0)
    row_out[1:2, :] = ids_r - me * float(vocab_rows)
    most_out[...] = jnp.broadcast_to(jnp.max(slot_r, axis=1, keepdims=True) + 1.0, (8, 128))


def find_slots(token_ids, my_rank, ranks, vocab_rows):
    count = token_ids.shape[0]
    return pl.pallas_call(
        functools.partial(slot_kernel, ranks, vocab_rows),
        out_shape=(
            jax.ShapeDtypeStruct((count, 128), F32),
            jax.ShapeDtypeStruct((8, count), F32),
            jax.ShapeDtypeStruct((8, 128), F32),
        ),
        in_specs=[SMEM, pl.BlockSpec(memory_space=pltpu.VMEM)],
        compiler_params=PARAMS,
        cost_estimate=cost(1000000, 1000000),
        name="find_slots",
    )(my_rank.reshape(1), token_ids.reshape(1, count))


def pick_kernel(width, info, rows, gain, table, *refs):
    out, picked, total = refs
    step = pl.program_id(0)
    slots = picked.shape[0]
    vocab_rows = table.shape[0]
    wanted = lax.broadcasted_iota(jnp.int32, (slots, 1), 0).astype(F32) + info[0].astype(F32)
    chosen = wanted == rows[0:1, :]
    index = jnp.sum(jnp.where(chosen, rows[1:2, :], 0.0), axis=1, keepdims=True)
    valid = jnp.sum(jnp.where(chosen, 1.0, 0.0), axis=1, keepdims=True)
    hot = (iota((slots, vocab_rows), 1) == index) & (valid > 0.5)
    block = jnp.dot(hot.astype(F32).astype(BF), table[...], preferred_element_type=F32)
    picked[:, pl.ds(pl.multiple_of(step * width, width), width)] = block

    @pl.when(step == 0)
    def _():
        total[...] = jnp.zeros_like(total)

    total[...] += jnp.sum(block * block, axis=1, keepdims=True)

    @pl.when(step == pl.num_programs(0) - 1)
    def _():
        features = picked.shape[1]
        chips, _, chip_width = out.shape
        inverse = lax.rsqrt(total[:, 0:1] * (1.0 / features) + eps_norm)
        for chip in range(chips):
            span = slice(chip * chip_width, (chip + 1) * chip_width)
            out[chip] = (picked[:, span] * inverse * gain[:, span]).astype(BF)


def pick_rows(rows, base, in_gain, vocab_table, chips):
    vocab_rows, features = vocab_table.shape
    steps = 4
    width, chip_width = features // steps, features // chips
    return pl.pallas_call(
        functools.partial(pick_kernel, width),
        grid=(steps,),
        out_shape=jax.ShapeDtypeStruct((chips, SLOTS, chip_width), BF),
        in_specs=[
            SMEM,
            pl.BlockSpec(rows.shape, lambda i: (0, 0)),
            pl.BlockSpec((1, features), lambda i: (0, 0)),
            pl.BlockSpec((vocab_rows, width), lambda i: (0, i)),
        ],
        out_specs=pl.BlockSpec((chips, SLOTS, chip_width), lambda i: (0, 0, 0)),
        scratch_shapes=[pltpu.VMEM((SLOTS, features), F32), pltpu.VMEM((SLOTS, 128), F32)],
        compiler_params=PARAMS,
        cost_estimate=cost(2 * SLOTS * vocab_rows * features, 2 * vocab_rows * features),
        name="pick_rows",
    )(base.reshape(1), rows, in_gain.reshape(1, features), vocab_table)


def place_kernel(chips, info, owners, own, other, out):
    count = owners.shape[0]
    core, base = info[0], info[1].astype(F32)
    owner, slot = owners[:, 0:1].astype(jnp.int32), owners[:, 1:2] - base
    fits = (slot >= 0.0) & (slot < float(SLOTS))
    position = (owner >> 1) * SLOTS + slot.astype(jnp.int32)
    hit = (lax.broadcasted_iota(jnp.int32, (count, chips * SLOTS), 1) == position) & fits
    total = jnp.zeros(out.shape, F32)
    for side, received in enumerate((own, other)):
        hot = jnp.where(hit & ((owner & 1) == (core ^ side)), 1.0, 0.0).astype(BF)
        total = total + jnp.dot(hot, received[...], preferred_element_type=F32)
    out[...] = total.astype(BF)


def place_rows(owners, base, core, own, other):
    count = owners.shape[0]
    chips, _, width = own.shape
    vmem = pl.BlockSpec(memory_space=pltpu.VMEM)
    return pl.pallas_call(
        functools.partial(place_kernel, chips),
        out_shape=jax.ShapeDtypeStruct((count, width), BF),
        in_specs=[SMEM, vmem, vmem, vmem],
        compiler_params=PARAMS,
        cost_estimate=cost(4 * count * chips * SLOTS * width, 6 * chips * SLOTS * width),
        name="place_rows",
    )(
        jnp.stack([core, base]),
        owners,
        own.reshape(chips * SLOTS, width),
        other.reshape(chips * SLOTS, width),
    )


def weight_kernel(info, order, wq_scale, kv_scale, wq, kv, *outs):
    core, rank = info[0], info[1]
    blocks, rows, columns = outs[0].shape
    half = columns - TILE_SIDE
    tiles = half // TILE_SIDE
    tile_row = (rank * pl.num_programs(0) + pl.program_id(0)) // 2
    for number, out in enumerate(outs):
        side = core ^ (number % 2)
        for at in range(blocks):
            column = 2 * order[number // 2 * blocks + at] + side
            for tile in range(tiles):
                scale = wq_scale[tile_row, column * tiles + tile]
                start = pl.multiple_of(column * half + tile * TILE_SIDE, TILE_SIDE)
                codes = wq[:, pl.ds(start, TILE_SIDE)].astype(F32)
                out[at, :, tile * TILE_SIDE : (tile + 1) * TILE_SIDE] = (codes * scale).astype(BF)
            start = pl.multiple_of(column * TILE_SIDE, TILE_SIDE)
            codes = kv[:, pl.ds(start, TILE_SIDE)].astype(F32)
            out[at, :, half:] = (codes * kv_scale[tile_row, column]).astype(BF)


def prepare_weights(core, my_rank, order, wq_codes, wq_scale, kv_codes, kv_scale):
    rows, width = wq_codes.shape
    chips = order.shape[0]
    columns = width // (2 * chips) + TILE_SIDE
    blocks = chips // 2
    return pl.pallas_call(
        weight_kernel,
        grid_spec=pltpu.PrefetchScalarGridSpec(
            num_scalar_prefetch=4,
            grid=(rows // GROUP_ROWS,),
            in_specs=[
                pl.BlockSpec((GROUP_ROWS, width), lambda i, *_: (i, 0)),
                pl.BlockSpec((GROUP_ROWS, kv_codes.shape[1]), lambda i, *_: (i, 0)),
            ],
            out_specs=[pl.BlockSpec((blocks, GROUP_ROWS, columns), lambda i, *_: (0, i, 0))] * 4,
        ),
        out_shape=[jax.ShapeDtypeStruct((blocks, rows, columns), BF)] * 4,
        compiler_params=PARAMS,
        cost_estimate=cost(rows * width * 4, rows * width * 5),
        name="prepare_weights",
    )(jnp.stack([core, my_rank]), order, wq_scale, kv_scale, wq_codes, kv_codes)


def key_kernel(info, head_of, kv_scale, codes, out):
    step = pl.program_id(0)
    rows = codes.shape[0]
    for group in range(rows // GROUP_ROWS):
        tile_row = (info[0] * (rows // GROUP_ROWS) + group) // 2
        span = slice(group * GROUP_ROWS, (group + 1) * GROUP_ROWS)
        scale = kv_scale[tile_row, 2 * head_of[step]]
        out[0, span, :] = (codes[span, :].astype(F32) * scale).astype(BF)


def prepare_keys(my_rank, key_value_of_block, kv_codes, kv_scale):
    rows = kv_codes.shape[0]
    chips = key_value_of_block.shape[0]
    return pl.pallas_call(
        key_kernel,
        grid_spec=pltpu.PrefetchScalarGridSpec(
            num_scalar_prefetch=3,
            grid=(chips,),
            in_specs=[
                pl.BlockSpec((rows, TILE_SIDE), lambda i, info, head_of, *_: (0, 2 * head_of[i]))
            ],
            out_specs=pl.BlockSpec((1, rows, TILE_SIDE), lambda i, *_: (i, 0, 0)),
        ),
        out_shape=jax.ShapeDtypeStruct((chips, rows, TILE_SIDE), BF),
        compiler_params=PARAMS,
        cost_estimate=cost(2 * chips * rows * TILE_SIDE, 4 * chips * rows * TILE_SIDE),
        name="prepare_keys",
    )(my_rank.reshape(1), key_value_of_block, kv_scale, kv_codes)


def project_kernel(info, normed, own, other, first, sent, kept, weight):
    step = pl.program_id(0)
    rows = own.shape[1]
    core = info[0]
    weight[pl.ds(pl.multiple_of(core * rows, GROUP_ROWS), rows), :] = own[0]
    weight[pl.ds(pl.multiple_of((1 - core) * rows, GROUP_ROWS), rows), :] = other[0]
    product = jnp.dot(normed[...], weight[...], preferred_element_type=F32)
    first[0] = product[: first.shape[1]].astype(first.dtype)
    second = product[first.shape[1] :]

    @pl.when(step < 2)
    def _():
        sent[0] = second.astype(BF)

    @pl.when(step >= 2)
    def _():
        kept[0] = second


def project(core, normed, own, other, first_type):
    count, width = normed.shape
    blocks, rows, columns = other.shape
    first, second = PART_ROWS
    return pl.pallas_call(
        project_kernel,
        grid=(blocks,),
        in_specs=[
            SMEM,
            pl.BlockSpec((count, width), lambda k: (0, 0)),
            pl.BlockSpec((1, rows, columns), lambda k: (k, 0, 0)),
            pl.BlockSpec((1, rows, columns), lambda k: (k, 0, 0)),
        ],
        out_specs=[
            pl.BlockSpec((1, first, columns), lambda k: (k, 0, 0)),
            pl.BlockSpec((1, second, columns), lambda k: (jnp.minimum(k, 1), 0, 0)),
            pl.BlockSpec((1, second, columns), lambda k: (jnp.maximum(k - 2, 0), 0, 0)),
        ],
        scratch_shapes=[pltpu.VMEM((width, columns), BF)],
        out_shape=[
            jax.ShapeDtypeStruct((blocks, first, columns), first_type),
            jax.ShapeDtypeStruct((2, second, columns), BF),
            jax.ShapeDtypeStruct((2, second, columns), F32),
        ],
        compiler_params=PARAMS,
        cost_estimate=cost(
            2 * blocks * count * width * columns, 2 * blocks * columns * (width + count)
        ),
        name="project",
    )(core.reshape(1), normed, own, other)


def join_kernel(own, got, kept, near, far, middle):
    for block, out in enumerate((near, far, kept, middle)):
        out[...] = (own[block] + got[block].astype(F32)).astype(out.dtype)


def join_partials(own, got):
    _, rows, columns = got.shape
    vmem = pl.BlockSpec(memory_space=pltpu.VMEM)
    sent = jax.ShapeDtypeStruct((rows, columns), BF)
    kept, near, far, middle = pl.pallas_call(
        join_kernel,
        in_specs=[vmem, vmem],
        out_shape=[jax.ShapeDtypeStruct((rows, columns), F32), sent, sent, sent],
        compiler_params=PARAMS,
        cost_estimate=cost(8 * rows * columns, 32 * rows * columns),
        name="join_partials",
    )(own, got)
    return kept, near, middle, far


def pair_kernel(away, home, got_away, got_home, sent, kept):
    sent[...] = (away[...] + got_away[...].astype(F32)).astype(BF)
    kept[...] = home[...] + got_home[...].astype(F32)


def join_pair(away, home, got_away, got_home):
    vmem = pl.BlockSpec(memory_space=pltpu.VMEM)
    return pl.pallas_call(
        pair_kernel,
        in_specs=[vmem] * 4,
        out_shape=[jax.ShapeDtypeStruct(away.shape, BF), jax.ShapeDtypeStruct(home.shape, F32)],
        compiler_params=PARAMS,
        cost_estimate=cost(2 * home.size, 16 * home.size),
        name="join_pair",
    )(away, home, got_away, got_home)


def last_kernel(kept, got, own, sent):
    own[...] = kept[0] + got[0].astype(F32)
    sent[...] = (kept[1] + got[1].astype(F32)).astype(BF)


def join_last(kept, got):
    _, rows, columns = kept.shape
    vmem = pl.BlockSpec(memory_space=pltpu.VMEM)
    return pl.pallas_call(
        last_kernel,
        in_specs=[vmem, vmem],
        out_shape=[
            jax.ShapeDtypeStruct((rows, columns), F32),
            jax.ShapeDtypeStruct((rows, columns), BF),
        ],
        compiler_params=PARAMS,
        cost_estimate=cost(2 * kept.size, 8 * kept.size),
        name="join_last",
    )(kept, got)


def turn(values, cosine, sine):
    return values * cosine + pltpu.roll(values, HEAD_SIZE // 2, 1) * sine


def normalise(values, gain):
    mean_square = jnp.mean(values * values, axis=-1, keepdims=True)
    return values * lax.rsqrt(mean_square + eps_norm) * gain


def heads_kernel(start, info, *refs):
    *parts, q_gain, k_gain, cosine, sine, q_out, kv_out = refs
    total = parts[0][...]
    for part in parts[1:]:
        total = total + part[...].astype(F32)
    heads, count, _ = q_out.shape
    cos, sin = cosine[start : start + count, :], sine[start : start + count, :]
    last = total[:, heads * HEAD_SIZE :]

    @pl.when(info[0] == 0)
    def _():
        kv_out[...] = turn(normalise(last, k_gain[...]), cos, sin).astype(BF)

    @pl.when(info[0] == 1)
    def _():
        kv_out[...] = last.astype(BF)

    for head in range(heads):
        values = total[:, head * HEAD_SIZE : (head + 1) * HEAD_SIZE]
        q_out[head] = turn(normalise(values, q_gain[...]), cos, sin).astype(BF)


def make_heads(core, parts, start, q_gain, k_gain, cosine, sine):
    count, columns = parts[0].shape
    heads = columns // HEAD_SIZE - 1
    vmem = pl.BlockSpec(memory_space=pltpu.VMEM)
    return pl.pallas_call(
        functools.partial(heads_kernel, start),
        out_shape=(
            jax.ShapeDtypeStruct((heads, count, HEAD_SIZE), BF),
            jax.ShapeDtypeStruct((count, HEAD_SIZE), BF),
        ),
        in_specs=[SMEM] + [vmem] * (len(parts) + 4),
        compiler_params=PARAMS,
        cost_estimate=cost(20 * count * columns, 14 * count * columns),
        name="make_heads",
    )(core.reshape(1), *parts, q_gain.reshape(1, -1), k_gain.reshape(1, -1), cosine, sine)


def attend_kernel(length, start, share, info, queries, *refs):
    *rows, kept, sent = refs
    parts = len(rows) // 2
    own = jnp.concatenate([ref[...] for ref in rows[:parts]], axis=0)
    other = jnp.concatenate([ref[...] for ref in rows[parts:]], axis=0)
    first = info[0] == 0
    keys, values = jnp.where(first, own, other), jnp.where(first, other, own)
    count = queries.shape[1]
    here = lax.broadcasted_iota(jnp.int32, (count, keys.shape[0]), 0) + start
    there = lax.broadcasted_iota(jnp.int32, (count, keys.shape[0]), 1)
    allowed = here >= there
    for prompt in range(1, (start + count + length - 1) // length):
        allowed = allowed & ((here < prompt * length) | (there >= prompt * length))
    for head in range(queries.shape[0]):
        scores = lax.dot_general(
            queries[head], keys, (((1,), (1,)), ((), ())), preferred_element_type=F32
        ) * HEAD_SIZE ** (-0.5)
        weights = jnp.where(allowed, jnp.exp(scores), 0.0)
        probabilities = (weights / jnp.sum(weights, axis=-1, keepdims=True)).astype(BF)
        result = jnp.dot(probabilities, values, preferred_element_type=F32)
        shares = [result[at : at + share] for at in range(0, count, share)]
        even = jnp.concatenate(shares[0::2], axis=0)
        odd = jnp.concatenate(shares[1::2], axis=0)
        span = slice(head * HEAD_SIZE, (head + 1) * HEAD_SIZE)
        kept[:, span] = jnp.where(first, even, odd).astype(BF)
        sent[:, span] = jnp.where(first, odd, even).astype(BF)


def attend_heads(core, queries, start, own, other, share):
    heads, count, width = queries.shape
    vmem = pl.BlockSpec(memory_space=pltpu.VMEM)
    return pl.pallas_call(
        functools.partial(attend_kernel, LEN, start, share),
        out_shape=[jax.ShapeDtypeStruct((count // 2, heads * width), BF)] * 2,
        in_specs=[SMEM] + [vmem] * (1 + len(own) + len(other)),
        compiler_params=PARAMS,
        cost_estimate=cost(4 * heads * count * (start + count) * width, 4 * heads * count * width),
        name="attend",
    )(core.reshape(1), queries, *own, *other)


def out_kernel(blocks, has_start, last, width, info, scales, *refs):
    attended = refs[:blocks]
    codes = refs[blocks : blocks + 2]
    out, held, arrived = refs[-3:]
    core, my_rank = info[0], info[1]
    columns = held.shape[1]
    tiles = width // TILE_SIDE
    pieces = [(block, side) for block in range(blocks) for side in range(2)]
    copies = []
    for number, (block, side) in enumerate(pieces):
        start = pl.multiple_of(info[2 + block] * (2 * width), 2 * width)
        copy = pltpu.make_async_copy(
            codes[side].at[:, pl.ds(start, 2 * width)], held.at[number], arrived.at[number]
        )
        copy.start()
        copies.append(copy)
    totals = [None, None]
    for number, (block, side) in enumerate(pieces):
        copies[number].wait()
        for half in range(2):
            rows = attended[block][:, half * width : (half + 1) * width]
            first_tile = (2 * info[2 + block] + (core ^ half)) * tiles
            weight = []
            for group in range(columns // GROUP_ROWS):
                column = ((my_rank ^ side) * columns + group * GROUP_ROWS) // TILE_SIDE
                span = slice(group * GROUP_ROWS, (group + 1) * GROUP_ROWS)
                parts = []
                for tile in range(tiles):
                    lane = pl.multiple_of((core ^ half) * width + tile * TILE_SIDE, TILE_SIDE)
                    code = held[number, span, pl.ds(lane, TILE_SIDE)].astype(F32)
                    parts.append((code * scales[first_tile + tile, column]).astype(BF))
                weight.append(jnp.concatenate(parts, axis=1))
            term = lax.dot_general(
                jnp.concatenate(weight, axis=0),
                rows,
                (((1,), (1,)), ((), ())),
                preferred_element_type=F32,
            )
            totals[side] = term if totals[side] is None else totals[side] + term
    if has_start:
        start = refs[blocks + 2]
        totals = [total + start[side] for side, total in enumerate(totals)]
    if last:
        first = core == 0
        both = jnp.concatenate(
            [jnp.where(first, totals[0], totals[1]), jnp.where(first, totals[1], totals[0])], axis=0
        )
        out[...] = both.T.astype(out.dtype)
    else:
        for side in range(2):
            out[side] = totals[side]


def out_project(core, my_rank, attended, chips_of, codes, scales, start, last):
    count, both = attended[0].shape
    blocks = len(attended)
    columns = codes[0].shape[0]
    vmem = pl.BlockSpec(memory_space=pltpu.VMEM)
    extra = [] if start is None else [start]
    shape = (count, 2 * columns) if last else (2, columns, count)
    return pl.pallas_call(
        functools.partial(out_kernel, blocks, bool(extra), last, both // 2),
        out_shape=jax.ShapeDtypeStruct(shape, BF if last else F32),
        in_specs=[SMEM, SMEM]
        + [vmem] * blocks
        + [pl.BlockSpec(memory_space=pl.ANY)] * 2
        + [vmem] * len(extra),
        scratch_shapes=[
            pltpu.VMEM((2 * blocks, columns, both), BF),
            pltpu.SemaphoreType.DMA((2 * blocks,)),
        ],
        compiler_params=PARAMS,
        cost_estimate=cost(4 * blocks * count * both * columns, 4 * blocks * both * columns),
        name="out_project",
    )(jnp.concatenate([jnp.stack([core, my_rank]), chips_of]), scales, *attended, *codes, *extra)


def rotation_tables(count):
    half_width = HEAD_SIZE // 2
    positions = (jnp.arange(count) % LEN).astype(F32)
    frequency = theta_base ** (-jnp.arange(half_width, dtype=F32) * 2.0 / HEAD_SIZE)
    angles = positions[:, None] * frequency[None, :]
    cosine, sine = jnp.cos(angles), jnp.sin(angles)
    return jnp.concatenate([cosine, cosine], axis=1), jnp.concatenate([-sine, sine], axis=1)


Z_COUNT = 4
PART_ROWS = (192, 192)
TIE_FIRST = True
TIE_SECOND = False
TIE_AWAY = True
TIE_SUMS = False


def after(values, *earlier):
    return lax.optimization_barrier((values, *earlier))[0]


def chip_plan(
    token_ids,
    key_value_of_block,
    vocab_table,
    in_gain,
    q_gain,
    k_gain,
    wq_codes,
    wq_scale,
    key_value_codes,
    key_value_scale,
    wo_codes,
    wo_scale,
):
    ranks = lax.axis_size("fsdp")
    chips = ranks // 2
    y_count = chips // Z_COUNT
    my_rank = lax.axis_index("fsdp").astype(jnp.int32)
    core, chip = my_rank % 2, my_rank // 2
    count = token_ids.shape[0]
    vocab_rows = vocab_table.shape[0]
    same_core = [[2 * chip + side for chip in range(chips)] for side in range(2)]

    def swap(values, bits):
        return lax.ppermute(values, "fsdp", [(i, i ^ bits) for i in range(ranks)])

    def swap_groups(values):
        return lax.ppermute(values, "groups", [(0, 1), (1, 0)])

    def to_chips(values):
        return lax.all_to_all(
            values, "fsdp", split_axis=0, concat_axis=0, tiled=True, axis_index_groups=same_core
        )

    def exchange(sent):
        own = to_chips(sent)
        return own, swap(own, 1)

    owners, rows, most = find_slots(token_ids, my_rank, ranks, vocab_rows)
    sent = pick_rows(rows, jnp.int32(0), in_gain, vocab_table, chips)
    most = jnp.maximum(most, swap_groups(after(most, sent)))[0, 0]

    sent_keys = prepare_keys(
        after(my_rank, sent), key_value_of_block, key_value_codes, key_value_scale
    )
    half = sent_keys.shape[1] // 2
    group = lax.axis_index("groups")
    my_half = lax.dynamic_slice_in_dim(sent_keys, group * half, half, 1)
    my_z = chip // y_count

    def keys_for(z):
        return lax.dynamic_slice_in_dim(my_half, z * y_count, y_count, 0)

    by_z = [keys_for(my_z)] + [swap(keys_for(my_z ^ k), 2 * y_count * k) for k in range(1, Z_COUNT)]

    near = jnp.array([1, 3, 0, 2], jnp.int32) * y_count

    away_own, away_other, home_own, home_other = prepare_weights(
        core,
        my_rank,
        after(chip, sent) ^ jnp.concatenate([near ^ 1, near]),
        wq_codes,
        wq_scale,
        key_value_codes,
        key_value_scale,
    )
    own = to_chips(sent)
    own, away_other, home_other, *by_z = lax.optimization_barrier(
        (own, away_other, home_other, *by_z)
    )
    other = swap(own, 1)
    normed = place_rows(owners, jnp.int32(0), core, own, other)

    def one_more(state):
        base, total = state
        more = exchange(pick_rows(rows, base, in_gain, vocab_table, chips))
        return base + SLOTS, total + place_rows(owners, base, core, *more)

    _, normed = lax.while_loop(
        lambda state: state[0].astype(F32) < most, one_more, (jnp.int32(SLOTS), normed)
    )

    away_other = swap(away_other, 1)
    home_other = swap(home_other, 1)
    away, away_sent, away_kept = project(core, normed, away_own, away_other, BF)
    got = swap(away, 2)
    got_away = swap(away_sent, 2 * y_count)
    home, home_sent, home_kept = project(
        after(core, away), normed, home_own, home_other, F32
    )
    got_home = swap(home_sent, 2 * y_count)
    if TIE_AWAY:
        got, got_away = lax.optimization_barrier((got, got_away))

    cosine, sine = rotation_tables(count)
    heads_width = wq_codes.shape[1] // ranks
    by_z = jnp.stack(by_z)
    my_y = chip % y_count
    here = lax.dynamic_index_in_dim(by_z, my_y, 1, keepdims=False)
    there = swap(lax.dynamic_index_in_dim(by_z, 1 - my_y, 1, keepdims=False), 2)
    wo_rows = wo_codes.T
    out_codes = [wo_rows, swap(wo_rows, 1)]
    own_kv, other_kv, held = [], [], []
    share = count // ranks

    def attend_part(start, sums):
        queries, kv = make_heads(core, sums, start, q_gain, k_gain, cosine, sine)
        own_kv.append(kv)
        other_kv.append(swap(kv, 1))
        kept, sent_rows = attend_heads(core, queries, start, own_kv, other_kv, share)
        held.append(jnp.concatenate([kept, swap(sent_rows, 1)], axis=1))

    kept, *sums = join_partials(home, got)
    got_away, got_home = lax.optimization_barrier((got_away, got_home, *sums))[:2]
    pair_sent, pair_kept = join_pair(away_kept, home_kept, got_away, got_home)
    sums = [swap(value, 2 * y_count * (k + 1)) for k, value in enumerate(sums)]
    pair_got = swap(pair_sent, 2)
    if TIE_SUMS:
        pair_got, *sums = lax.optimization_barrier((pair_got, *sums))
    attend_part(0, [kept, *sums])
    kept, last_sent = join_last(pair_kept, pair_got)
    last_got = swap(last_sent, 4 * y_count)
    kept, there = lax.optimization_barrier((kept, there))
    attend_part(PART_ROWS[0], [kept, last_got])

    def add_blocks(total, blocks, numbers, last=False):
        chips_of = chip ^ jnp.array(numbers, jnp.int32)
        return out_project(
            core, my_rank, blocks, chips_of, out_codes, wo_scale, total, last
        )

    own_keys = jnp.stack([here, there], axis=1).reshape(chips, half, HEAD_SIZE)

    def finish_keys(far_keys):
        return collect_keys(
            jnp.stack([core, group, chip]),
            [own_keys, far_keys, swap(own_keys, 1), swap(far_keys, 1)],
        )

    total, synced = gather_project(
        jnp.concatenate(held, axis=0), add_blocks, y_count, swap_groups(own_keys), finish_keys
    )
    columns = to_chips(total.reshape(chips, share, -1))
    attn_out = jnp.transpose(columns, (1, 0, 2)).reshape(share, -1)
    return attn_out, synced


def collect_kernel(info, own, far, other, other_far, out):
    core, group = info[0], info[1]
    out[0, core, group] = own[0]
    out[0, core, 1 - group] = far[0]
    out[0, 1 - core, group] = other[0]
    out[0, 1 - core, 1 - group] = other_far[0]


def collect_keys(info, parts):
    chips, half, width = parts[0].shape
    part = pl.BlockSpec((1, half, width), lambda i, info: (i ^ info[2], 0, 0))
    out = pl.pallas_call(
        collect_kernel,
        grid_spec=pltpu.PrefetchScalarGridSpec(
            num_scalar_prefetch=1,
            grid=(chips,),
            in_specs=[part] * 4,
            out_specs=pl.BlockSpec((1, 2, 2, half, width), lambda i, info: (i, 0, 0, 0, 0)),
        ),
        out_shape=jax.ShapeDtypeStruct((chips, 2, 2, half, width), BF),
        compiler_params=PARAMS,
        cost_estimate=cost(0, 16 * chips * half * width),
        name="collect_keys",
    )(info, *parts)
    return out.reshape(1, -1, width)


def hop(values, pairs, along, ranks):
    moves = [(a * along + rest, b * along + rest) for a, b in pairs for rest in range(along)]
    return lax.ppermute(values, "fsdp", moves)


NEXT = [(0, 1), (1, 0), (2, 3), (3, 2)]
MIDDLE = [(1, 2), (2, 1)]
OUTWARD = [(1, 0), (2, 3)]


def gather_project(block, add_blocks, y_count, beside, finish):
    along = 2 * y_count
    ranks = Z_COUNT * along
    together = lax.optimization_barrier

    def swap_y(values):
        return lax.ppermute(values, "fsdp", [(i, i ^ 2) for i in range(ranks)])

    z_index = lax.axis_index("fsdp") // along
    at_end = (z_index == 0) | (z_index == Z_COUNT - 1)
    across, one, inner = together(
        (swap_y(block), hop(block, NEXT, along, ranks), hop(block, MIDDLE, along, ranks))
    )
    total = add_blocks(None, [block, across, one], (0, 1, 2))
    two_end, two_inner, one_across = (
        hop(inner, OUTWARD, along, ranks),
        hop(one, MIDDLE, along, ranks),
        swap_y(one),
    )
    if TIE_FIRST:
        two_end, two_inner, one_across, total, beside = together(
            (two_end, two_inner, one_across, total, beside)
        )
    else:
        two_end, two_inner, one_across, beside = together(
            (two_end, two_inner, one_across, beside)
        )
    finished = finish(beside)
    two = jnp.where(at_end, two_end, two_inner)
    three_end, two_across = hop(two, OUTWARD, along, ranks), swap_y(two)
    if TIE_SECOND:
        total = add_blocks(total, [one_across, two], (3, 4))
        three_end, two_across, total, finished = together(
            (three_end, two_across, total, finished)
        )
        rest, numbers = [two_across], (5, 6)
    else:
        three_end, two_across, finished = together((three_end, two_across, finished))
        rest, numbers = [one_across, two, two_across], (3, 4, 5, 6)
    three = jnp.where(at_end, three_end, inner)
    three_across = swap_y(three)
    total = add_blocks(total, [*rest, three], numbers)
    return add_blocks(total, [three_across], (7,), True), finished


def solution(mesh):
    sizes = dict(mesh.shape)
    small = sizes["fsdp"] == 2 * KEY_VALUE_HEADS and sizes["groups"] == 2
    return jax.shard_map(
        chip_plan if small else general_plan,
        mesh=mesh,
        in_specs=(
            P("groups"),
            P(),
            P("fsdp", None),
            P(),
            P(),
            P(),
            P("fsdp", None),
            P(),
            P("fsdp", None),
            P(),
            P(None, "fsdp"),
            P(),
        ),
        out_specs=(P(("groups", "fsdp"), None), P(("groups", "fsdp"), None, None)),
        check_vma=False,
    )
```

```python
import functools
import jax
import jax.numpy as jnp
from jax import lax
from jax.experimental import pallas as pl
from jax.experimental.pallas import tpu as pltpu
from jax.sharding import PartitionSpec as P
QUERY_HEADS = 64
KEY_VALUE_HEADS = 8
HEAD_SIZE = 128
TILE_SIDE = 128
LEN = 384


theta_base = 1000000.0
eps_norm = 1e-06


def rms_scale(values, norm_gain):
    mean_square = jnp.mean(values * values, axis=-1, keepdims=True)
    return values * lax.rsqrt(mean_square + eps_norm) * norm_gain


def rotate(values, positions):
    half_width = values.shape[-1] // 2
    frequency = theta_base ** (-jnp.arange(half_width, dtype=jnp.float32) * 2.0 / values.shape[-1])
    angles = positions[:, None] * frequency[None, :]
    cosine = jnp.cos(angles)[:, None, :]
    sine_part = jnp.sin(angles)[:, None, :]
    lower_half = values[..., :half_width]
    upper_half = values[..., half_width:]
    return jnp.concatenate(
        [
            lower_half * cosine - upper_half * sine_part,
            upper_half * cosine + lower_half * sine_part,
        ],
        axis=-1,
    )


def lookup_small(small_table, indices):
    matches = indices[..., None] == jnp.arange(small_table.shape[0], dtype=jnp.int32)
    return jnp.sum(jnp.where(matches, small_table, 0), axis=-1)


def column_scales(tile_scale, first_col, width_cols):
    per_column = jnp.repeat(tile_scale, TILE_SIDE, axis=1)
    picked = lax.dynamic_slice_in_dim(per_column, first_col, width_cols, 1)
    return jnp.repeat(picked, TILE_SIDE, axis=0)


def dequantize(quantized, scales):
    return (quantized.astype(jnp.float32) * scales).astype(jnp.bfloat16)


def attend(queries, key_rows, value_rows, prompt_count):
    token_count, head_count, head_width = queries.shape
    length = token_count // prompt_count
    query_blocks = queries.reshape(prompt_count, length, head_count, head_width)
    key_blocks = key_rows.reshape(prompt_count, length, head_width)
    value_blocks = value_rows.reshape(prompt_count, length, -1)
    scores = jnp.einsum(
        "plhd,pmd->phlm", query_blocks, key_blocks, preferred_element_type=jnp.float32
    ) * head_width ** (-0.5)
    causal = jnp.arange(length)[:, None] >= jnp.arange(length)[None, :]
    weights = jnp.where(causal, jnp.exp(scores), 0.0)
    probabilities = (weights / jnp.sum(weights, axis=-1, keepdims=True)).astype(jnp.bfloat16)
    attended_rows = jnp.einsum(
        "phlm,pmd->plhd", probabilities, value_blocks, preferred_element_type=jnp.float32
    )
    return attended_rows.astype(jnp.bfloat16).reshape(
        token_count, head_count * value_blocks.shape[-1]
    )


def general_plan(
    token_ids,
    key_value_of_block,
    vocab_table,
    in_gain,
    q_gain,
    k_gain,
    wq_codes,
    wq_scale,
    key_value_codes,
    key_value_scale,
    wo_codes,
    wo_scale,
):
    count_of_ranks = lax.axis_size("fsdp")
    my_rank = lax.axis_index("fsdp")
    duplicate_count = count_of_ranks // KEY_VALUE_HEADS
    per_key_value = QUERY_HEADS // KEY_VALUE_HEADS
    split_points = max(1, duplicate_count // per_key_value)
    heads_here = max(1, per_key_value // duplicate_count)
    value_columns = HEAD_SIZE // split_points
    query_width = heads_here * HEAD_SIZE
    local_rows = wq_codes.shape[0]
    token_count = token_ids.shape[0]
    targets = jnp.arange(count_of_ranks, dtype=jnp.int32)
    target_head = lookup_small(key_value_of_block, targets // duplicate_count)
    target_slot = targets % duplicate_count
    target_part = target_slot % split_points
    target_query = target_head * per_key_value + target_slot // split_points * heads_here
    my_head = lookup_small(key_value_of_block, my_rank // duplicate_count)
    my_slot = my_rank % duplicate_count
    my_part = my_slot % split_points
    my_query = my_head * per_key_value + my_slot // split_points * heads_here
    vocab_rows = vocab_table.shape[0]
    local_ids = token_ids - my_rank * vocab_rows
    inside = (local_ids >= 0) & (local_ids < vocab_rows)
    picked = jnp.take(vocab_table, jnp.clip(local_ids, 0, vocab_rows - 1), axis=0)
    terms = jnp.where(inside[:, None], picked, jnp.zeros_like(picked)).astype(jnp.float32)
    embedded = lax.psum(terms, "fsdp").astype(jnp.bfloat16)
    normed = rms_scale(embedded.astype(jnp.float32), in_gain).astype(jnp.bfloat16)
    query_groups = wq_codes.reshape(local_rows, QUERY_HEADS // heads_here, query_width)
    query_send = jnp.take(query_groups, target_query // heads_here, axis=1)
    key_value_heads = key_value_codes.reshape(local_rows, KEY_VALUE_HEADS, 2, HEAD_SIZE)
    key_send = jnp.take(key_value_heads[:, :, 0, :], target_head, axis=1)
    grouped_values = key_value_heads[:, :, 1, :].reshape(
        local_rows, KEY_VALUE_HEADS * split_points, value_columns
    )
    value_send = jnp.take(grouped_values, target_head * split_points + target_part, axis=1)
    both_send = jnp.concatenate([key_send, value_send], axis=2)
    query_got, kv_got = (
        lax.all_to_all(query_send, "fsdp", split_axis=1, concat_axis=0, tiled=True),
        lax.all_to_all(both_send, "fsdp", split_axis=1, concat_axis=0, tiled=True),
    )
    key_quant = kv_got[:, 0, :HEAD_SIZE]
    value_quant = kv_got[:, 0, HEAD_SIZE:]
    query_weight = dequantize(
        query_got[:, 0, :], column_scales(wq_scale, my_query * HEAD_SIZE, query_width)
    )
    key_matrix = dequantize(
        key_quant, column_scales(key_value_scale, my_head * 2 * HEAD_SIZE, HEAD_SIZE)
    )
    value_weight = dequantize(
        value_quant,
        column_scales(
            key_value_scale,
            my_head * 2 * HEAD_SIZE + HEAD_SIZE + my_part * value_columns,
            value_columns,
        ),
    )
    joined_weight = jnp.concatenate([query_weight, key_matrix, value_weight], axis=1)
    projected = jnp.dot(normed, joined_weight, preferred_element_type=jnp.float32)
    positions = (jnp.arange(token_count) % LEN).astype(jnp.float32)
    queries = rotate(
        rms_scale(projected[:, :query_width].reshape(token_count, heads_here, HEAD_SIZE), q_gain),
        positions,
    ).astype(jnp.bfloat16)
    keys_raw = projected[:, query_width : query_width + HEAD_SIZE].reshape(
        token_count, 1, HEAD_SIZE
    )
    key_rows = rotate(rms_scale(keys_raw, k_gain), positions).astype(jnp.bfloat16)[:, 0, :]
    value_rows = projected[:, query_width + HEAD_SIZE :].astype(jnp.bfloat16)
    attended_rows = attend(queries, key_rows, value_rows, token_count // LEN)
    cols_here = wo_codes.shape[1]
    local_weight = dequantize(wo_codes, column_scales(wo_scale, my_rank * cols_here, cols_here))
    ordered = jnp.take(
        local_weight.reshape(KEY_VALUE_HEADS, per_key_value * HEAD_SIZE, cols_here),
        key_value_of_block,
        axis=0,
    ).reshape(QUERY_HEADS * HEAD_SIZE, cols_here)
    columns = jnp.dot(
        lax.all_gather(attended_rows, "fsdp", axis=1, tiled=True),
        ordered,
        preferred_element_type=jnp.float32,
    )
    attn_out = lax.all_to_all(
        columns.astype(jnp.bfloat16), "fsdp", split_axis=0, concat_axis=1, tiled=True
    )
    return (attn_out, key_matrix.reshape(1, key_matrix.shape[0], HEAD_SIZE))


BF = jnp.bfloat16
F32 = jnp.float32
SLOTS = 32
GROUP_ROWS = 64
PARAMS = pltpu.CompilerParams(vmem_limit_bytes=48 << 20)
SMEM = pl.BlockSpec(memory_space=pltpu.SMEM)


COST_SHARE = 1


def cost(flops, bytes_accessed):
    return pl.CostEstimate(
        flops=flops // COST_SHARE, bytes_accessed=bytes_accessed // COST_SHARE, transcendentals=0
    )


def owner_of(ids, vocab_rows, ranks):
    owner = jnp.zeros_like(ids)
    for rank in range(1, ranks):
        owner = owner + jnp.where(ids >= float(rank * vocab_rows), 1.0, 0.0)
    return owner


def iota(shape, axis):
    return lax.broadcasted_iota(jnp.int32, shape, axis).astype(F32)


def slot_kernel(ranks, vocab_rows, info, id_row, col_out, row_out, most_out):
    count = id_row.shape[1]
    ids_r = id_row[...].astype(F32)
    ids_c = jnp.transpose(jnp.broadcast_to(ids_r, (128, count)))[:, 0:1]
    at_r, at_c = iota((count, count), 0), iota((count, count), 1)
    same = ids_c == ids_r
    first_c = jnp.min(jnp.where(same, at_c, float(count)), axis=1, keepdims=True)
    first_r = jnp.min(jnp.where(same, at_r, float(count)), axis=0, keepdims=True)
    is_first_r = first_r == iota((1, count), 1)
    is_first_c = first_c == iota((count, 1), 0)
    owner_c, owner_r = owner_of(ids_c, vocab_rows, ranks), owner_of(ids_r, vocab_rows, ranks)
    peers = owner_c == owner_r
    slot_c = jnp.sum(
        jnp.where(peers & is_first_r & (at_c < first_c), 1.0, 0.0), axis=1, keepdims=True
    )
    slot_r = jnp.sum(
        jnp.where(peers & is_first_c & (at_r < first_r), 1.0, 0.0), axis=0, keepdims=True
    )
    lane = lax.broadcasted_iota(jnp.int32, (count, 128), 1)
    col_out[...] = jnp.where(lane == 0, owner_c, jnp.where(lane == 1, slot_c, 0.0))
    me = info[0].astype(F32)
    mine = is_first_r & (owner_r == me)
    row_out[...] = jnp.zeros_like(row_out)
    row_out[0:1, :] = jnp.where(mine, slot_r, -1.0)
    row_out[1:2, :] = ids_r - me * float(vocab_rows)
    most_out[...] = jnp.broadcast_to(jnp.max(slot_r, axis=1, keepdims=True) + 1.0, (8, 128))


def find_slots(token_ids, my_rank, ranks, vocab_rows):
    count = token_ids.shape[0]
    return pl.pallas_call(
        functools.partial(slot_kernel, ranks, vocab_rows),
        out_shape=(
            jax.ShapeDtypeStruct((count, 128), F32),
            jax.ShapeDtypeStruct((8, count), F32),
            jax.ShapeDtypeStruct((8, 128), F32),
        ),
        in_specs=[SMEM, pl.BlockSpec(memory_space=pltpu.VMEM)],
        compiler_params=PARAMS,
        cost_estimate=cost(1000000, 1000000),
        name="find_slots",
    )(my_rank.reshape(1), token_ids.reshape(1, count))


def pick_kernel(width, info, rows, gain, table, *refs):
    out, picked, total = refs
    step = pl.program_id(0)
    slots = picked.shape[0]
    vocab_rows = table.shape[0]
    wanted = lax.broadcasted_iota(jnp.int32, (slots, 1), 0).astype(F32) + info[0].astype(F32)
    chosen = wanted == rows[0:1, :]
    index = jnp.sum(jnp.where(chosen, rows[1:2, :], 0.0), axis=1, keepdims=True)
    valid = jnp.sum(jnp.where(chosen, 1.0, 0.0), axis=1, keepdims=True)
    hot = (iota((slots, vocab_rows), 1) == index) & (valid > 0.5)
    block = jnp.dot(hot.astype(F32).astype(BF), table[...], preferred_element_type=F32)
    picked[:, pl.ds(pl.multiple_of(step * width, width), width)] = block

    @pl.when(step == 0)
    def _():
        total[...] = jnp.zeros_like(total)

    total[...] += jnp.sum(block * block, axis=1, keepdims=True)

    @pl.when(step == pl.num_programs(0) - 1)
    def _():
        features = picked.shape[1]
        chips, _, chip_width = out.shape
        inverse = lax.rsqrt(total[:, 0:1] * (1.0 / features) + eps_norm)
        for chip in range(chips):
            span = slice(chip * chip_width, (chip + 1) * chip_width)
            out[chip] = (picked[:, span] * inverse * gain[:, span]).astype(BF)


def pick_rows(rows, base, in_gain, vocab_table, chips):
    vocab_rows, features = vocab_table.shape
    steps = 4
    width, chip_width = features // steps, features // chips
    return pl.pallas_call(
        functools.partial(pick_kernel, width),
        grid=(steps,),
        out_shape=jax.ShapeDtypeStruct((chips, SLOTS, chip_width), BF),
        in_specs=[
            SMEM,
            pl.BlockSpec(rows.shape, lambda i: (0, 0)),
            pl.BlockSpec((1, features), lambda i: (0, 0)),
            pl.BlockSpec((vocab_rows, width), lambda i: (0, i)),
        ],
        out_specs=pl.BlockSpec((chips, SLOTS, chip_width), lambda i: (0, 0, 0)),
        scratch_shapes=[pltpu.VMEM((SLOTS, features), F32), pltpu.VMEM((SLOTS, 128), F32)],
        compiler_params=PARAMS,
        cost_estimate=cost(2 * SLOTS * vocab_rows * features, 2 * vocab_rows * features),
        name="pick_rows",
    )(base.reshape(1), rows, in_gain.reshape(1, features), vocab_table)


def place_kernel(chips, info, owners, own, other, out):
    count = owners.shape[0]
    core, base = info[0], info[1].astype(F32)
    owner, slot = owners[:, 0:1].astype(jnp.int32), owners[:, 1:2] - base
    fits = (slot >= 0.0) & (slot < float(SLOTS))
    position = (owner >> 1) * SLOTS + slot.astype(jnp.int32)
    hit = (lax.broadcasted_iota(jnp.int32, (count, chips * SLOTS), 1) == position) & fits
    total = jnp.zeros(out.shape, F32)
    for side, received in enumerate((own, other)):
        hot = jnp.where(hit & ((owner & 1) == (core ^ side)), 1.0, 0.0).astype(BF)
        total = total + jnp.dot(hot, received[...], preferred_element_type=F32)
    out[...] = total.astype(BF)


def place_rows(owners, base, core, own, other):
    count = owners.shape[0]
    chips, _, width = own.shape
    vmem = pl.BlockSpec(memory_space=pltpu.VMEM)
    return pl.pallas_call(
        functools.partial(place_kernel, chips),
        out_shape=jax.ShapeDtypeStruct((count, width), BF),
        in_specs=[SMEM, vmem, vmem, vmem],
        compiler_params=PARAMS,
        cost_estimate=cost(4 * count * chips * SLOTS * width, 6 * chips * SLOTS * width),
        name="place_rows",
    )(
        jnp.stack([core, base]),
        owners,
        own.reshape(chips * SLOTS, width),
        other.reshape(chips * SLOTS, width),
    )


def weight_kernel(info, order, wq_scale, kv_scale, wq, kv, *outs):
    core, rank = info[0], info[1]
    blocks, rows, columns = outs[0].shape
    half = columns - TILE_SIDE
    tiles = half // TILE_SIDE
    tile_row = (rank * pl.num_programs(0) + pl.program_id(0)) // 2
    for number, out in enumerate(outs):
        side = core ^ (number % 2)
        for at in range(blocks):
            column = 2 * order[number // 2 * blocks + at] + side
            for tile in range(tiles):
                scale = wq_scale[tile_row, column * tiles + tile]
                start = pl.multiple_of(column * half + tile * TILE_SIDE, TILE_SIDE)
                codes = wq[:, pl.ds(start, TILE_SIDE)].astype(F32)
                out[at, :, tile * TILE_SIDE : (tile + 1) * TILE_SIDE] = (codes * scale).astype(BF)
            start = pl.multiple_of(column * TILE_SIDE, TILE_SIDE)
            codes = kv[:, pl.ds(start, TILE_SIDE)].astype(F32)
            out[at, :, half:] = (codes * kv_scale[tile_row, column]).astype(BF)


def prepare_weights(core, my_rank, order, wq_codes, wq_scale, kv_codes, kv_scale):
    rows, width = wq_codes.shape
    chips = order.shape[0]
    columns = width // (2 * chips) + TILE_SIDE
    blocks = chips // 2
    return pl.pallas_call(
        weight_kernel,
        grid_spec=pltpu.PrefetchScalarGridSpec(
            num_scalar_prefetch=4,
            grid=(rows // GROUP_ROWS,),
            in_specs=[
                pl.BlockSpec((GROUP_ROWS, width), lambda i, *_: (i, 0)),
                pl.BlockSpec((GROUP_ROWS, kv_codes.shape[1]), lambda i, *_: (i, 0)),
            ],
            out_specs=[pl.BlockSpec((blocks, GROUP_ROWS, columns), lambda i, *_: (0, i, 0))] * 4,
        ),
        out_shape=[jax.ShapeDtypeStruct((blocks, rows, columns), BF)] * 4,
        compiler_params=PARAMS,
        cost_estimate=cost(rows * width * 4, rows * width * 5),
        name="prepare_weights",
    )(jnp.stack([core, my_rank]), order, wq_scale, kv_scale, wq_codes, kv_codes)


def key_kernel(info, head_of, kv_scale, codes, out):
    step = pl.program_id(0)
    rows = codes.shape[0]
    for group in range(rows // GROUP_ROWS):
        tile_row = (info[0] * (rows // GROUP_ROWS) + group) // 2
        span = slice(group * GROUP_ROWS, (group + 1) * GROUP_ROWS)
        scale = kv_scale[tile_row, 2 * head_of[step]]
        out[0, span, :] = (codes[span, :].astype(F32) * scale).astype(BF)


def prepare_keys(my_rank, key_value_of_block, kv_codes, kv_scale):
    rows = kv_codes.shape[0]
    chips = key_value_of_block.shape[0]
    return pl.pallas_call(
        key_kernel,
        grid_spec=pltpu.PrefetchScalarGridSpec(
            num_scalar_prefetch=3,
            grid=(chips,),
            in_specs=[
                pl.BlockSpec((rows, TILE_SIDE), lambda i, info, head_of, *_: (0, 2 * head_of[i]))
            ],
            out_specs=pl.BlockSpec((1, rows, TILE_SIDE), lambda i, *_: (i, 0, 0)),
        ),
        out_shape=jax.ShapeDtypeStruct((chips, rows, TILE_SIDE), BF),
        compiler_params=PARAMS,
        cost_estimate=cost(2 * chips * rows * TILE_SIDE, 4 * chips * rows * TILE_SIDE),
        name="prepare_keys",
    )(my_rank.reshape(1), key_value_of_block, kv_scale, kv_codes)


def project_kernel(info, normed, own, other, first, sent, kept, weight):
    step = pl.program_id(0)
    rows = own.shape[1]
    core = info[0]
    weight[pl.ds(pl.multiple_of(core * rows, GROUP_ROWS), rows), :] = own[0]
    weight[pl.ds(pl.multiple_of((1 - core) * rows, GROUP_ROWS), rows), :] = other[0]
    product = jnp.dot(normed[...], weight[...], preferred_element_type=F32)
    first[0] = product[: first.shape[1]].astype(first.dtype)
    second = product[first.shape[1] :]

    @pl.when(step < 2)
    def _():
        sent[0] = second.astype(BF)

    @pl.when(step >= 2)
    def _():
        kept[0] = second


def project(core, normed, own, other, first_type):
    count, width = normed.shape
    blocks, rows, columns = other.shape
    first, second = PART_ROWS
    return pl.pallas_call(
        project_kernel,
        grid=(blocks,),
        in_specs=[
            SMEM,
            pl.BlockSpec((count, width), lambda k: (0, 0)),
            pl.BlockSpec((1, rows, columns), lambda k: (k, 0, 0)),
            pl.BlockSpec((1, rows, columns), lambda k: (k, 0, 0)),
        ],
        out_specs=[
            pl.BlockSpec((1, first, columns), lambda k: (k, 0, 0)),
            pl.BlockSpec((1, second, columns), lambda k: (jnp.minimum(k, 1), 0, 0)),
            pl.BlockSpec((1, second, columns), lambda k: (jnp.maximum(k - 2, 0), 0, 0)),
        ],
        scratch_shapes=[pltpu.VMEM((width, columns), BF)],
        out_shape=[
            jax.ShapeDtypeStruct((blocks, first, columns), first_type),
            jax.ShapeDtypeStruct((2, second, columns), BF),
            jax.ShapeDtypeStruct((2, second, columns), F32),
        ],
        compiler_params=PARAMS,
        cost_estimate=cost(
            2 * blocks * count * width * columns, 2 * blocks * columns * (width + count)
        ),
        name="project",
    )(core.reshape(1), normed, own, other)


def project_first_kernel(info, normed, own, other, out, weight):
    rows = own.shape[1]
    core = info[0]
    weight[pl.ds(pl.multiple_of(core * rows, GROUP_ROWS), rows), :] = own[0]
    weight[pl.ds(pl.multiple_of((1 - core) * rows, GROUP_ROWS), rows), :] = other[0]
    product = jnp.dot(normed[...], weight[...], preferred_element_type=F32)
    out[0] = product.astype(out.dtype)


def project_part(core, normed, part, own, other, first_block, blocks, out_type):
    width = normed.shape[1]
    _, rows, columns = other.shape
    count = PART_ROWS[part]
    weight = pl.BlockSpec((1, rows, columns), lambda k: (first_block + k, 0, 0))
    return pl.pallas_call(
        project_first_kernel,
        grid=(blocks,),
        in_specs=[SMEM, pl.BlockSpec((count, width), lambda k: (part, 0)), weight, weight],
        out_specs=pl.BlockSpec((1, count, columns), lambda k: (k, 0, 0)),
        scratch_shapes=[pltpu.VMEM((width, columns), BF)],
        out_shape=jax.ShapeDtypeStruct((blocks, count, columns), out_type),
        compiler_params=PARAMS,
        cost_estimate=cost(
            2 * blocks * count * width * columns, 2 * blocks * columns * (width + count)
        ),
        name="project_part",
    )(core.reshape(1), normed, own, other)


def join_kernel(own, got, kept, near, far, middle):
    for block, out in enumerate((near, far, kept, middle)):
        out[...] = (own[block] + got[block].astype(F32)).astype(out.dtype)


def join_partials(own, got):
    _, rows, columns = got.shape
    vmem = pl.BlockSpec(memory_space=pltpu.VMEM)
    sent = jax.ShapeDtypeStruct((rows, columns), BF)
    kept, near, far, middle = pl.pallas_call(
        join_kernel,
        in_specs=[vmem, vmem],
        out_shape=[jax.ShapeDtypeStruct((rows, columns), F32), sent, sent, sent],
        compiler_params=PARAMS,
        cost_estimate=cost(8 * rows * columns, 32 * rows * columns),
        name="join_partials",
    )(own, got)
    return kept, near, middle, far


def pair_kernel(away, home, got_away, got_home, sent, kept):
    sent[...] = (away[...] + got_away[...].astype(F32)).astype(BF)
    kept[...] = home[...] + got_home[...].astype(F32)


def join_pair(away, home, got_away, got_home):
    vmem = pl.BlockSpec(memory_space=pltpu.VMEM)
    return pl.pallas_call(
        pair_kernel,
        in_specs=[vmem] * 4,
        out_shape=[jax.ShapeDtypeStruct(away.shape, BF), jax.ShapeDtypeStruct(home.shape, F32)],
        compiler_params=PARAMS,
        cost_estimate=cost(2 * home.size, 16 * home.size),
        name="join_pair",
    )(away, home, got_away, got_home)


def last_kernel(kept, got, own, sent):
    own[...] = kept[0] + got[0].astype(F32)
    sent[...] = (kept[1] + got[1].astype(F32)).astype(BF)


def join_last(kept, got):
    _, rows, columns = kept.shape
    vmem = pl.BlockSpec(memory_space=pltpu.VMEM)
    return pl.pallas_call(
        last_kernel,
        in_specs=[vmem, vmem],
        out_shape=[
            jax.ShapeDtypeStruct((rows, columns), F32),
            jax.ShapeDtypeStruct((rows, columns), BF),
        ],
        compiler_params=PARAMS,
        cost_estimate=cost(2 * kept.size, 8 * kept.size),
        name="join_last",
    )(kept, got)


def turn(values, cosine, sine):
    return values * cosine + pltpu.roll(values, HEAD_SIZE // 2, 1) * sine


def normalise(values, gain):
    mean_square = jnp.mean(values * values, axis=-1, keepdims=True)
    return values * lax.rsqrt(mean_square + eps_norm) * gain


def heads_kernel(start, info, *refs):
    *parts, q_gain, k_gain, cosine, sine, q_out, kv_out = refs
    total = parts[0][...]
    for part in parts[1:]:
        total = total + part[...].astype(F32)
    heads, count, _ = q_out.shape
    cos, sin = cosine[start : start + count, :], sine[start : start + count, :]
    last = total[:, heads * HEAD_SIZE :]

    @pl.when(info[0] == 0)
    def _():
        kv_out[...] = turn(normalise(last, k_gain[...]), cos, sin).astype(BF)

    @pl.when(info[0] == 1)
    def _():
        kv_out[...] = last.astype(BF)

    for head in range(heads):
        values = total[:, head * HEAD_SIZE : (head + 1) * HEAD_SIZE]
        q_out[head] = turn(normalise(values, q_gain[...]), cos, sin).astype(BF)


def make_heads(core, parts, start, q_gain, k_gain, cosine, sine):
    count, columns = parts[0].shape
    heads = columns // HEAD_SIZE - 1
    vmem = pl.BlockSpec(memory_space=pltpu.VMEM)
    return pl.pallas_call(
        functools.partial(heads_kernel, start),
        out_shape=(
            jax.ShapeDtypeStruct((heads, count, HEAD_SIZE), BF),
            jax.ShapeDtypeStruct((count, HEAD_SIZE), BF),
        ),
        in_specs=[SMEM] + [vmem] * (len(parts) + 4),
        compiler_params=PARAMS,
        cost_estimate=cost(20 * count * columns, 14 * count * columns),
        name="make_heads",
    )(core.reshape(1), *parts, q_gain.reshape(1, -1), k_gain.reshape(1, -1), cosine, sine)


def attend_kernel(length, start, share, info, queries, *refs):
    *rows, kept, sent = refs
    parts = len(rows) // 2
    own = jnp.concatenate([ref[...] for ref in rows[:parts]], axis=0)
    other = jnp.concatenate([ref[...] for ref in rows[parts:]], axis=0)
    first = info[0] == 0
    keys, values = jnp.where(first, own, other), jnp.where(first, other, own)
    count = queries.shape[1]
    here = lax.broadcasted_iota(jnp.int32, (count, keys.shape[0]), 0) + start
    there = lax.broadcasted_iota(jnp.int32, (count, keys.shape[0]), 1)
    allowed = here >= there
    for prompt in range(1, (start + count + length - 1) // length):
        allowed = allowed & ((here < prompt * length) | (there >= prompt * length))
    for head in range(queries.shape[0]):
        scores = lax.dot_general(
            queries[head], keys, (((1,), (1,)), ((), ())), preferred_element_type=F32
        ) * HEAD_SIZE ** (-0.5)
        weights = jnp.where(allowed, jnp.exp(scores), 0.0)
        probabilities = (weights / jnp.sum(weights, axis=-1, keepdims=True)).astype(BF)
        result = jnp.dot(probabilities, values, preferred_element_type=F32)
        shares = [result[at : at + share] for at in range(0, count, share)]
        even = jnp.concatenate(shares[0::2], axis=0)
        odd = jnp.concatenate(shares[1::2], axis=0)
        span = slice(head * HEAD_SIZE, (head + 1) * HEAD_SIZE)
        kept[:, span] = jnp.where(first, even, odd).astype(BF)
        sent[:, span] = jnp.where(first, odd, even).astype(BF)


def attend_heads(core, queries, start, own, other, share):
    heads, count, width = queries.shape
    vmem = pl.BlockSpec(memory_space=pltpu.VMEM)
    return pl.pallas_call(
        functools.partial(attend_kernel, LEN, start, share),
        out_shape=[jax.ShapeDtypeStruct((count // 2, heads * width), BF)] * 2,
        in_specs=[SMEM] + [vmem] * (1 + len(own) + len(other)),
        compiler_params=PARAMS,
        cost_estimate=cost(4 * heads * count * (start + count) * width, 4 * heads * count * width),
        name="attend",
    )(core.reshape(1), queries, *own, *other)


def out_kernel(blocks, has_start, last, width, info, scales, *refs):
    attended = refs[:blocks]
    codes = refs[blocks : blocks + 2]
    out, held, arrived = refs[-3:]
    core, my_rank = info[0], info[1]
    columns = held.shape[1]
    tiles = width // TILE_SIDE
    pieces = [(block, side) for block in range(blocks) for side in range(2)]
    copies = []
    for number, (block, side) in enumerate(pieces):
        start = pl.multiple_of(info[2 + block] * (2 * width), 2 * width)
        copy = pltpu.make_async_copy(
            codes[side].at[:, pl.ds(start, 2 * width)], held.at[number], arrived.at[number]
        )
        copy.start()
        copies.append(copy)
    totals = [None, None]
    for number, (block, side) in enumerate(pieces):
        copies[number].wait()
        for half in range(2):
            rows = attended[block][:, half * width : (half + 1) * width]
            first_tile = (2 * info[2 + block] + (core ^ half)) * tiles
            weight = []
            for group in range(columns // GROUP_ROWS):
                column = ((my_rank ^ side) * columns + group * GROUP_ROWS) // TILE_SIDE
                span = slice(group * GROUP_ROWS, (group + 1) * GROUP_ROWS)
                parts = []
                for tile in range(tiles):
                    lane = pl.multiple_of((core ^ half) * width + tile * TILE_SIDE, TILE_SIDE)
                    code = held[number, span, pl.ds(lane, TILE_SIDE)].astype(F32)
                    parts.append((code * scales[first_tile + tile, column]).astype(BF))
                weight.append(jnp.concatenate(parts, axis=1))
            term = lax.dot_general(
                jnp.concatenate(weight, axis=0),
                rows,
                (((1,), (1,)), ((), ())),
                preferred_element_type=F32,
            )
            totals[side] = term if totals[side] is None else totals[side] + term
    if has_start:
        start = refs[blocks + 2]
        totals = [total + start[side] for side, total in enumerate(totals)]
    if last:
        first = core == 0
        both = jnp.concatenate(
            [jnp.where(first, totals[0], totals[1]), jnp.where(first, totals[1], totals[0])], axis=0
        )
        out[...] = both.T.astype(out.dtype)
    else:
        for side in range(2):
            out[side] = totals[side]


def out_project(core, my_rank, attended, chips_of, codes, scales, start, last):
    count, both = attended[0].shape
    blocks = len(attended)
    columns = codes[0].shape[0]
    vmem = pl.BlockSpec(memory_space=pltpu.VMEM)
    extra = [] if start is None else [start]
    shape = (count, 2 * columns) if last else (2, columns, count)
    return pl.pallas_call(
        functools.partial(out_kernel, blocks, bool(extra), last, both // 2),
        out_shape=jax.ShapeDtypeStruct(shape, BF if last else F32),
        in_specs=[SMEM, SMEM]
        + [vmem] * blocks
        + [pl.BlockSpec(memory_space=pl.ANY)] * 2
        + [vmem] * len(extra),
        scratch_shapes=[
            pltpu.VMEM((2 * blocks, columns, both), BF),
            pltpu.SemaphoreType.DMA((2 * blocks,)),
        ],
        compiler_params=PARAMS,
        cost_estimate=cost(4 * blocks * count * both * columns, 4 * blocks * both * columns),
        name="out_project",
    )(jnp.concatenate([jnp.stack([core, my_rank]), chips_of]), scales, *attended, *codes, *extra)


def rotation_tables(count):
    half_width = HEAD_SIZE // 2
    positions = (jnp.arange(count) % LEN).astype(F32)
    frequency = theta_base ** (-jnp.arange(half_width, dtype=F32) * 2.0 / HEAD_SIZE)
    angles = positions[:, None] * frequency[None, :]
    cosine, sine = jnp.cos(angles), jnp.sin(angles)
    return jnp.concatenate([cosine, cosine], axis=1), jnp.concatenate([-sine, sine], axis=1)


Z_COUNT = 4
PART_ROWS = (192, 192)
TIE_FIRST = True
TIE_SECOND = False
TIE_AWAY = True


def after(values, *earlier):
    return lax.optimization_barrier((values, *earlier))[0]


def chip_plan(
    token_ids,
    key_value_of_block,
    vocab_table,
    in_gain,
    q_gain,
    k_gain,
    wq_codes,
    wq_scale,
    key_value_codes,
    key_value_scale,
    wo_codes,
    wo_scale,
):
    ranks = lax.axis_size("fsdp")
    chips = ranks // 2
    y_count = chips // Z_COUNT
    my_rank = lax.axis_index("fsdp").astype(jnp.int32)
    core, chip = my_rank % 2, my_rank // 2
    count = token_ids.shape[0]
    vocab_rows = vocab_table.shape[0]
    same_core = [[2 * chip + side for chip in range(chips)] for side in range(2)]

    def swap(values, bits):
        return lax.ppermute(values, "fsdp", [(i, i ^ bits) for i in range(ranks)])

    def swap_groups(values):
        return lax.ppermute(values, "groups", [(0, 1), (1, 0)])

    def to_chips(values):
        return lax.all_to_all(
            values, "fsdp", split_axis=0, concat_axis=0, tiled=True, axis_index_groups=same_core
        )

    def exchange(sent):
        own = to_chips(sent)
        return own, swap(own, 1)

    owners, rows, most = find_slots(token_ids, my_rank, ranks, vocab_rows)
    sent = pick_rows(rows, jnp.int32(0), in_gain, vocab_table, chips)
    most = jnp.maximum(most, swap_groups(after(most, sent)))[0, 0]

    sent_keys = prepare_keys(
        after(my_rank, sent), key_value_of_block, key_value_codes, key_value_scale
    )
    half = sent_keys.shape[1] // 2
    group = lax.axis_index("groups")
    my_half = lax.dynamic_slice_in_dim(sent_keys, group * half, half, 1)
    my_z = chip // y_count

    def keys_for(z):
        return lax.dynamic_slice_in_dim(my_half, z * y_count, y_count, 0)

    by_z = [keys_for(my_z)] + [swap(keys_for(my_z ^ k), 2 * y_count * k) for k in range(1, Z_COUNT)]

    near = jnp.array([1, 3, 0, 2], jnp.int32) * y_count

    away_own, away_other, home_own, home_other = prepare_weights(
        core,
        my_rank,
        after(chip, sent) ^ jnp.concatenate([near ^ 1, near]),
        wq_codes,
        wq_scale,
        key_value_codes,
        key_value_scale,
    )
    own = to_chips(sent)
    own, away_other, home_other, *by_z = lax.optimization_barrier(
        (own, away_other, home_other, *by_z)
    )
    other = swap(own, 1)
    normed = place_rows(owners, jnp.int32(0), core, own, other)

    def one_more(state):
        base, total = state
        more = exchange(pick_rows(rows, base, in_gain, vocab_table, chips))
        return base + SLOTS, total + place_rows(owners, base, core, *more)

    _, normed = lax.while_loop(
        lambda state: state[0].astype(F32) < most, one_more, (jnp.int32(SLOTS), normed)
    )

    away_other = swap(away_other, 1)
    home_other = swap(home_other, 1)
    away = project_part(core, normed, 0, away_own, away_other, 0, Z_COUNT, BF)
    got = swap(away, 2)
    away_sent = project_part(after(core, away), normed, 1, away_own, away_other, 0, 2, BF)
    got_away = swap(away_sent, 2 * y_count)
    away_kept = project_part(after(core, away_sent), normed, 1, away_own, away_other, 2, 2, F32)
    home, home_sent, home_kept = project(
        after(core, away_sent), normed, home_own, home_other, F32
    )
    got_home = swap(home_sent, 2 * y_count)
    if TIE_AWAY:
        got, got_away = lax.optimization_barrier((got, got_away))

    cosine, sine = rotation_tables(count)
    heads_width = wq_codes.shape[1] // ranks
    by_z = jnp.stack(by_z)
    my_y = chip % y_count
    here = lax.dynamic_index_in_dim(by_z, my_y, 1, keepdims=False)
    there = swap(lax.dynamic_index_in_dim(by_z, 1 - my_y, 1, keepdims=False), 2)
    wo_rows = wo_codes.T
    out_codes = [wo_rows, swap(wo_rows, 1)]
    own_kv, other_kv, held = [], [], []
    share = count // ranks

    def attend_part(start, sums):
        queries, kv = make_heads(core, sums, start, q_gain, k_gain, cosine, sine)
        own_kv.append(kv)
        other_kv.append(swap(kv, 1))
        kept, sent_rows = attend_heads(core, queries, start, own_kv, other_kv, share)
        held.append(jnp.concatenate([kept, swap(sent_rows, 1)], axis=1))

    kept, *sums = join_partials(home, got)
    got_away, got_home = lax.optimization_barrier((got_away, got_home, *sums))[:2]
    pair_sent, pair_kept = join_pair(away_kept, home_kept, got_away, got_home)
    sums = [swap(value, 2 * y_count * (k + 1)) for k, value in enumerate(sums)]
    pair_got = swap(pair_sent, 2)
    pair_got, sums[0], sums[1] = lax.optimization_barrier((pair_got, sums[0], sums[1]))
    attend_part(0, [kept, *sums])
    kept, last_sent = join_last(pair_kept, pair_got)
    last_got = swap(last_sent, 4 * y_count)
    kept, there = lax.optimization_barrier((kept, there))
    attend_part(PART_ROWS[0], [kept, last_got])

    def add_blocks(total, blocks, numbers, last=False):
        chips_of = chip ^ jnp.array(numbers, jnp.int32)
        return out_project(
            core, my_rank, blocks, chips_of, out_codes, wo_scale, total, last
        )

    own_keys = jnp.stack([here, there], axis=1).reshape(chips, half, HEAD_SIZE)

    def finish_keys(far_keys):
        return collect_keys(
            jnp.stack([core, group, chip]),
            [own_keys, far_keys, swap(own_keys, 1), swap(far_keys, 1)],
        )

    total, synced = gather_project(
        jnp.concatenate(held, axis=0), add_blocks, y_count, swap_groups(own_keys), finish_keys
    )
    columns = to_chips(total.reshape(chips, share, -1))
    attn_out = jnp.transpose(columns, (1, 0, 2)).reshape(share, -1)
    return attn_out, synced


def collect_kernel(info, own, far, other, other_far, out):
    core, group = info[0], info[1]
    out[0, core, group] = own[0]
    out[0, core, 1 - group] = far[0]
    out[0, 1 - core, group] = other[0]
    out[0, 1 - core, 1 - group] = other_far[0]


def collect_keys(info, parts):
    chips, half, width = parts[0].shape
    part = pl.BlockSpec((1, half, width), lambda i, info: (i ^ info[2], 0, 0))
    out = pl.pallas_call(
        collect_kernel,
        grid_spec=pltpu.PrefetchScalarGridSpec(
            num_scalar_prefetch=1,
            grid=(chips,),
            in_specs=[part] * 4,
            out_specs=pl.BlockSpec((1, 2, 2, half, width), lambda i, info: (i, 0, 0, 0, 0)),
        ),
        out_shape=jax.ShapeDtypeStruct((chips, 2, 2, half, width), BF),
        compiler_params=PARAMS,
        cost_estimate=cost(0, 16 * chips * half * width),
        name="collect_keys",
    )(info, *parts)
    return out.reshape(1, -1, width)


def hop(values, pairs, along, ranks):
    moves = [(a * along + rest, b * along + rest) for a, b in pairs for rest in range(along)]
    return lax.ppermute(values, "fsdp", moves)


NEXT = [(0, 1), (1, 0), (2, 3), (3, 2)]
MIDDLE = [(1, 2), (2, 1)]
OUTWARD = [(1, 0), (2, 3)]


def gather_project(block, add_blocks, y_count, beside, finish):
    along = 2 * y_count
    ranks = Z_COUNT * along
    together = lax.optimization_barrier

    def swap_y(values):
        return lax.ppermute(values, "fsdp", [(i, i ^ 2) for i in range(ranks)])

    z_index = lax.axis_index("fsdp") // along
    at_end = (z_index == 0) | (z_index == Z_COUNT - 1)
    across, one, inner = together(
        (swap_y(block), hop(block, NEXT, along, ranks), hop(block, MIDDLE, along, ranks))
    )
    total = add_blocks(None, [block, across, one], (0, 1, 2))
    two_end, two_inner, one_across = (
        hop(inner, OUTWARD, along, ranks),
        hop(one, MIDDLE, along, ranks),
        swap_y(one),
    )
    if TIE_FIRST:
        two_end, two_inner, one_across, total, beside = together(
            (two_end, two_inner, one_across, total, beside)
        )
    else:
        two_end, two_inner, one_across, beside = together(
            (two_end, two_inner, one_across, beside)
        )
    finished = finish(beside)
    two = jnp.where(at_end, two_end, two_inner)
    three_end, two_across = hop(two, OUTWARD, along, ranks), swap_y(two)
    if TIE_SECOND:
        total = add_blocks(total, [one_across, two], (3, 4))
        three_end, two_across, total, finished = together(
            (three_end, two_across, total, finished)
        )
        rest, numbers = [two_across], (5, 6)
    else:
        three_end, two_across, finished = together((three_end, two_across, finished))
        rest, numbers = [one_across, two, two_across], (3, 4, 5, 6)
    three = jnp.where(at_end, three_end, inner)
    three_across = swap_y(three)
    total = add_blocks(total, [*rest, three], numbers)
    return add_blocks(total, [three_across], (7,), True), finished


def solution(mesh):
    sizes = dict(mesh.shape)
    small = sizes["fsdp"] == 2 * KEY_VALUE_HEADS and sizes["groups"] == 2
    return jax.shard_map(
        chip_plan if small else general_plan,
        mesh=mesh,
        in_specs=(
            P("groups"),
            P(),
            P("fsdp", None),
            P(),
            P(),
            P(),
            P("fsdp", None),
            P(),
            P("fsdp", None),
            P(),
            P(None, "fsdp"),
            P(),
        ),
        out_specs=(P(("groups", "fsdp"), None), P(("groups", "fsdp"), None, None)),
        check_vma=False,
    )
```

```python
import functools
import jax
import jax.numpy as jnp
from jax import lax
from jax.experimental import pallas as pl
from jax.experimental.pallas import tpu as pltpu
from jax.sharding import PartitionSpec as P
QUERY_HEADS = 64
KEY_VALUE_HEADS = 8
HEAD_SIZE = 128
TILE_SIDE = 128
LEN = 384


theta_base = 1000000.0
eps_norm = 1e-06


def rms_scale(values, norm_gain):
    mean_square = jnp.mean(values * values, axis=-1, keepdims=True)
    return values * lax.rsqrt(mean_square + eps_norm) * norm_gain


def rotate(values, positions):
    half_width = values.shape[-1] // 2
    frequency = theta_base ** (-jnp.arange(half_width, dtype=jnp.float32) * 2.0 / values.shape[-1])
    angles = positions[:, None] * frequency[None, :]
    cosine = jnp.cos(angles)[:, None, :]
    sine_part = jnp.sin(angles)[:, None, :]
    lower_half = values[..., :half_width]
    upper_half = values[..., half_width:]
    return jnp.concatenate(
        [
            lower_half * cosine - upper_half * sine_part,
            upper_half * cosine + lower_half * sine_part,
        ],
        axis=-1,
    )


def lookup_small(small_table, indices):
    matches = indices[..., None] == jnp.arange(small_table.shape[0], dtype=jnp.int32)
    return jnp.sum(jnp.where(matches, small_table, 0), axis=-1)


def column_scales(tile_scale, first_col, width_cols):
    per_column = jnp.repeat(tile_scale, TILE_SIDE, axis=1)
    picked = lax.dynamic_slice_in_dim(per_column, first_col, width_cols, 1)
    return jnp.repeat(picked, TILE_SIDE, axis=0)


def dequantize(quantized, scales):
    return (quantized.astype(jnp.float32) * scales).astype(jnp.bfloat16)


def attend(queries, key_rows, value_rows, prompt_count):
    token_count, head_count, head_width = queries.shape
    length = token_count // prompt_count
    query_blocks = queries.reshape(prompt_count, length, head_count, head_width)
    key_blocks = key_rows.reshape(prompt_count, length, head_width)
    value_blocks = value_rows.reshape(prompt_count, length, -1)
    scores = jnp.einsum(
        "plhd,pmd->phlm", query_blocks, key_blocks, preferred_element_type=jnp.float32
    ) * head_width ** (-0.5)
    causal = jnp.arange(length)[:, None] >= jnp.arange(length)[None, :]
    weights = jnp.where(causal, jnp.exp(scores), 0.0)
    probabilities = (weights / jnp.sum(weights, axis=-1, keepdims=True)).astype(jnp.bfloat16)
    attended_rows = jnp.einsum(
        "phlm,pmd->plhd", probabilities, value_blocks, preferred_element_type=jnp.float32
    )
    return attended_rows.astype(jnp.bfloat16).reshape(
        token_count, head_count * value_blocks.shape[-1]
    )


def general_plan(
    token_ids,
    key_value_of_block,
    vocab_table,
    in_gain,
    q_gain,
    k_gain,
    wq_codes,
    wq_scale,
    key_value_codes,
    key_value_scale,
    wo_codes,
    wo_scale,
):
    count_of_ranks = lax.axis_size("fsdp")
    my_rank = lax.axis_index("fsdp")
    duplicate_count = count_of_ranks // KEY_VALUE_HEADS
    per_key_value = QUERY_HEADS // KEY_VALUE_HEADS
    split_points = max(1, duplicate_count // per_key_value)
    heads_here = max(1, per_key_value // duplicate_count)
    value_columns = HEAD_SIZE // split_points
    query_width = heads_here * HEAD_SIZE
    local_rows = wq_codes.shape[0]
    token_count = token_ids.shape[0]
    targets = jnp.arange(count_of_ranks, dtype=jnp.int32)
    target_head = lookup_small(key_value_of_block, targets // duplicate_count)
    target_slot = targets % duplicate_count
    target_part = target_slot % split_points
    target_query = target_head * per_key_value + target_slot // split_points * heads_here
    my_head = lookup_small(key_value_of_block, my_rank // duplicate_count)
    my_slot = my_rank % duplicate_count
    my_part = my_slot % split_points
    my_query = my_head * per_key_value + my_slot // split_points * heads_here
    vocab_rows = vocab_table.shape[0]
    local_ids = token_ids - my_rank * vocab_rows
    inside = (local_ids >= 0) & (local_ids < vocab_rows)
    picked = jnp.take(vocab_table, jnp.clip(local_ids, 0, vocab_rows - 1), axis=0)
    terms = jnp.where(inside[:, None], picked, jnp.zeros_like(picked)).astype(jnp.float32)
    embedded = lax.psum(terms, "fsdp").astype(jnp.bfloat16)
    normed = rms_scale(embedded.astype(jnp.float32), in_gain).astype(jnp.bfloat16)
    query_groups = wq_codes.reshape(local_rows, QUERY_HEADS // heads_here, query_width)
    query_send = jnp.take(query_groups, target_query // heads_here, axis=1)
    key_value_heads = key_value_codes.reshape(local_rows, KEY_VALUE_HEADS, 2, HEAD_SIZE)
    key_send = jnp.take(key_value_heads[:, :, 0, :], target_head, axis=1)
    grouped_values = key_value_heads[:, :, 1, :].reshape(
        local_rows, KEY_VALUE_HEADS * split_points, value_columns
    )
    value_send = jnp.take(grouped_values, target_head * split_points + target_part, axis=1)
    both_send = jnp.concatenate([key_send, value_send], axis=2)
    query_got, kv_got = (
        lax.all_to_all(query_send, "fsdp", split_axis=1, concat_axis=0, tiled=True),
        lax.all_to_all(both_send, "fsdp", split_axis=1, concat_axis=0, tiled=True),
    )
    key_quant = kv_got[:, 0, :HEAD_SIZE]
    value_quant = kv_got[:, 0, HEAD_SIZE:]
    query_weight = dequantize(
        query_got[:, 0, :], column_scales(wq_scale, my_query * HEAD_SIZE, query_width)
    )
    key_matrix = dequantize(
        key_quant, column_scales(key_value_scale, my_head * 2 * HEAD_SIZE, HEAD_SIZE)
    )
    value_weight = dequantize(
        value_quant,
        column_scales(
            key_value_scale,
            my_head * 2 * HEAD_SIZE + HEAD_SIZE + my_part * value_columns,
            value_columns,
        ),
    )
    joined_weight = jnp.concatenate([query_weight, key_matrix, value_weight], axis=1)
    projected = jnp.dot(normed, joined_weight, preferred_element_type=jnp.float32)
    positions = (jnp.arange(token_count) % LEN).astype(jnp.float32)
    queries = rotate(
        rms_scale(projected[:, :query_width].reshape(token_count, heads_here, HEAD_SIZE), q_gain),
        positions,
    ).astype(jnp.bfloat16)
    keys_raw = projected[:, query_width : query_width + HEAD_SIZE].reshape(
        token_count, 1, HEAD_SIZE
    )
    key_rows = rotate(rms_scale(keys_raw, k_gain), positions).astype(jnp.bfloat16)[:, 0, :]
    value_rows = projected[:, query_width + HEAD_SIZE :].astype(jnp.bfloat16)
    attended_rows = attend(queries, key_rows, value_rows, token_count // LEN)
    cols_here = wo_codes.shape[1]
    local_weight = dequantize(wo_codes, column_scales(wo_scale, my_rank * cols_here, cols_here))
    ordered = jnp.take(
        local_weight.reshape(KEY_VALUE_HEADS, per_key_value * HEAD_SIZE, cols_here),
        key_value_of_block,
        axis=0,
    ).reshape(QUERY_HEADS * HEAD_SIZE, cols_here)
    columns = jnp.dot(
        lax.all_gather(attended_rows, "fsdp", axis=1, tiled=True),
        ordered,
        preferred_element_type=jnp.float32,
    )
    attn_out = lax.all_to_all(
        columns.astype(jnp.bfloat16), "fsdp", split_axis=0, concat_axis=1, tiled=True
    )
    return (attn_out, key_matrix.reshape(1, key_matrix.shape[0], HEAD_SIZE))


BF = jnp.bfloat16
F32 = jnp.float32
SLOTS = 32
GROUP_ROWS = 64
PARAMS = pltpu.CompilerParams(vmem_limit_bytes=48 << 20)
SMEM = pl.BlockSpec(memory_space=pltpu.SMEM)


COST_SHARE = 1


def cost(flops, bytes_accessed):
    return pl.CostEstimate(
        flops=flops // COST_SHARE, bytes_accessed=bytes_accessed // COST_SHARE, transcendentals=0
    )


def owner_of(ids, vocab_rows, ranks):
    owner = jnp.zeros_like(ids)
    for rank in range(1, ranks):
        owner = owner + jnp.where(ids >= float(rank * vocab_rows), 1.0, 0.0)
    return owner


def iota(shape, axis):
    return lax.broadcasted_iota(jnp.int32, shape, axis).astype(F32)


def slot_kernel(ranks, vocab_rows, info, id_row, col_out, row_out, most_out):
    count = id_row.shape[1]
    ids_r = id_row[...].astype(F32)
    ids_c = jnp.transpose(jnp.broadcast_to(ids_r, (128, count)))[:, 0:1]
    at_r, at_c = iota((count, count), 0), iota((count, count), 1)
    same = ids_c == ids_r
    first_c = jnp.min(jnp.where(same, at_c, float(count)), axis=1, keepdims=True)
    first_r = jnp.min(jnp.where(same, at_r, float(count)), axis=0, keepdims=True)
    is_first_r = first_r == iota((1, count), 1)
    is_first_c = first_c == iota((count, 1), 0)
    owner_c, owner_r = owner_of(ids_c, vocab_rows, ranks), owner_of(ids_r, vocab_rows, ranks)
    peers = owner_c == owner_r
    slot_c = jnp.sum(
        jnp.where(peers & is_first_r & (at_c < first_c), 1.0, 0.0), axis=1, keepdims=True
    )
    slot_r = jnp.sum(
        jnp.where(peers & is_first_c & (at_r < first_r), 1.0, 0.0), axis=0, keepdims=True
    )
    lane = lax.broadcasted_iota(jnp.int32, (count, 128), 1)
    col_out[...] = jnp.where(lane == 0, owner_c, jnp.where(lane == 1, slot_c, 0.0))
    me = info[0].astype(F32)
    mine = is_first_r & (owner_r == me)
    row_out[...] = jnp.zeros_like(row_out)
    row_out[0:1, :] = jnp.where(mine, slot_r, -1.0)
    row_out[1:2, :] = ids_r - me * float(vocab_rows)
    most_out[...] = jnp.broadcast_to(jnp.max(slot_r, axis=1, keepdims=True) + 1.0, (8, 128))


def find_slots(token_ids, my_rank, ranks, vocab_rows):
    count = token_ids.shape[0]
    return pl.pallas_call(
        functools.partial(slot_kernel, ranks, vocab_rows),
        out_shape=(
            jax.ShapeDtypeStruct((count, 128), F32),
            jax.ShapeDtypeStruct((8, count), F32),
            jax.ShapeDtypeStruct((8, 128), F32),
        ),
        in_specs=[SMEM, pl.BlockSpec(memory_space=pltpu.VMEM)],
        compiler_params=PARAMS,
        cost_estimate=cost(1000000, 1000000),
        name="find_slots",
    )(my_rank.reshape(1), token_ids.reshape(1, count))


def pick_kernel(width, info, rows, gain, table, *refs):
    out, picked, total = refs
    step = pl.program_id(0)
    slots = picked.shape[0]
    vocab_rows = table.shape[0]
    wanted = lax.broadcasted_iota(jnp.int32, (slots, 1), 0).astype(F32) + info[0].astype(F32)
    chosen = wanted == rows[0:1, :]
    index = jnp.sum(jnp.where(chosen, rows[1:2, :], 0.0), axis=1, keepdims=True)
    valid = jnp.sum(jnp.where(chosen, 1.0, 0.0), axis=1, keepdims=True)
    hot = (iota((slots, vocab_rows), 1) == index) & (valid > 0.5)
    block = jnp.dot(hot.astype(F32).astype(BF), table[...], preferred_element_type=F32)
    picked[:, pl.ds(pl.multiple_of(step * width, width), width)] = block

    @pl.when(step == 0)
    def _():
        total[...] = jnp.zeros_like(total)

    total[...] += jnp.sum(block * block, axis=1, keepdims=True)

    @pl.when(step == pl.num_programs(0) - 1)
    def _():
        features = picked.shape[1]
        chips, _, chip_width = out.shape
        inverse = lax.rsqrt(total[:, 0:1] * (1.0 / features) + eps_norm)
        for chip in range(chips):
            span = slice(chip * chip_width, (chip + 1) * chip_width)
            out[chip] = (picked[:, span] * inverse * gain[:, span]).astype(BF)


def pick_rows(rows, base, in_gain, vocab_table, chips):
    vocab_rows, features = vocab_table.shape
    steps = 4
    width, chip_width = features // steps, features // chips
    return pl.pallas_call(
        functools.partial(pick_kernel, width),
        grid=(steps,),
        out_shape=jax.ShapeDtypeStruct((chips, SLOTS, chip_width), BF),
        in_specs=[
            SMEM,
            pl.BlockSpec(rows.shape, lambda i: (0, 0)),
            pl.BlockSpec((1, features), lambda i: (0, 0)),
            pl.BlockSpec((vocab_rows, width), lambda i: (0, i)),
        ],
        out_specs=pl.BlockSpec((chips, SLOTS, chip_width), lambda i: (0, 0, 0)),
        scratch_shapes=[pltpu.VMEM((SLOTS, features), F32), pltpu.VMEM((SLOTS, 128), F32)],
        compiler_params=PARAMS,
        cost_estimate=cost(2 * SLOTS * vocab_rows * features, 2 * vocab_rows * features),
        name="pick_rows",
    )(base.reshape(1), rows, in_gain.reshape(1, features), vocab_table)


def place_kernel(chips, info, owners, own, other, out):
    count = owners.shape[0]
    core, base = info[0], info[1].astype(F32)
    owner, slot = owners[:, 0:1].astype(jnp.int32), owners[:, 1:2] - base
    fits = (slot >= 0.0) & (slot < float(SLOTS))
    position = (owner >> 1) * SLOTS + slot.astype(jnp.int32)
    hit = (lax.broadcasted_iota(jnp.int32, (count, chips * SLOTS), 1) == position) & fits
    total = jnp.zeros(out.shape, F32)
    for side, received in enumerate((own, other)):
        hot = jnp.where(hit & ((owner & 1) == (core ^ side)), 1.0, 0.0).astype(BF)
        total = total + jnp.dot(hot, received[...], preferred_element_type=F32)
    out[...] = total.astype(BF)


def place_rows(owners, base, core, own, other):
    count = owners.shape[0]
    chips, _, width = own.shape
    vmem = pl.BlockSpec(memory_space=pltpu.VMEM)
    return pl.pallas_call(
        functools.partial(place_kernel, chips),
        out_shape=jax.ShapeDtypeStruct((count, width), BF),
        in_specs=[SMEM, vmem, vmem, vmem],
        compiler_params=PARAMS,
        cost_estimate=cost(4 * count * chips * SLOTS * width, 6 * chips * SLOTS * width),
        name="place_rows",
    )(
        jnp.stack([core, base]),
        owners,
        own.reshape(chips * SLOTS, width),
        other.reshape(chips * SLOTS, width),
    )


def weight_kernel(info, order, wq_scale, kv_scale, wq, kv, *outs):
    core, rank = info[0], info[1]
    blocks, rows, columns = outs[0].shape
    half = columns - TILE_SIDE
    tiles = half // TILE_SIDE
    tile_row = (rank * pl.num_programs(0) + pl.program_id(0)) // 2
    for number, out in enumerate(outs):
        side = core ^ (number % 2)
        for at in range(blocks):
            column = 2 * order[number // 2 * blocks + at] + side
            for tile in range(tiles):
                scale = wq_scale[tile_row, column * tiles + tile]
                start = pl.multiple_of(column * half + tile * TILE_SIDE, TILE_SIDE)
                codes = wq[:, pl.ds(start, TILE_SIDE)].astype(F32)
                out[at, :, tile * TILE_SIDE : (tile + 1) * TILE_SIDE] = (codes * scale).astype(BF)
            start = pl.multiple_of(column * TILE_SIDE, TILE_SIDE)
            codes = kv[:, pl.ds(start, TILE_SIDE)].astype(F32)
            out[at, :, half:] = (codes * kv_scale[tile_row, column]).astype(BF)


def prepare_weights(core, my_rank, order, wq_codes, wq_scale, kv_codes, kv_scale):
    rows, width = wq_codes.shape
    chips = order.shape[0]
    columns = width // (2 * chips) + TILE_SIDE
    blocks = chips // 2
    return pl.pallas_call(
        weight_kernel,
        grid_spec=pltpu.PrefetchScalarGridSpec(
            num_scalar_prefetch=4,
            grid=(rows // GROUP_ROWS,),
            in_specs=[
                pl.BlockSpec((GROUP_ROWS, width), lambda i, *_: (i, 0)),
                pl.BlockSpec((GROUP_ROWS, kv_codes.shape[1]), lambda i, *_: (i, 0)),
            ],
            out_specs=[pl.BlockSpec((blocks, GROUP_ROWS, columns), lambda i, *_: (0, i, 0))] * 4,
        ),
        out_shape=[jax.ShapeDtypeStruct((blocks, rows, columns), BF)] * 4,
        compiler_params=PARAMS,
        cost_estimate=cost(rows * width * 4, rows * width * 5),
        name="prepare_weights",
    )(jnp.stack([core, my_rank]), order, wq_scale, kv_scale, wq_codes, kv_codes)


def key_kernel(info, head_of, kv_scale, codes, out):
    step = pl.program_id(0)
    rows = codes.shape[0]
    for group in range(rows // GROUP_ROWS):
        tile_row = (info[0] * (rows // GROUP_ROWS) + group) // 2
        span = slice(group * GROUP_ROWS, (group + 1) * GROUP_ROWS)
        scale = kv_scale[tile_row, 2 * head_of[step]]
        out[0, span, :] = (codes[span, :].astype(F32) * scale).astype(BF)


def prepare_keys(my_rank, key_value_of_block, kv_codes, kv_scale):
    rows = kv_codes.shape[0]
    chips = key_value_of_block.shape[0]
    return pl.pallas_call(
        key_kernel,
        grid_spec=pltpu.PrefetchScalarGridSpec(
            num_scalar_prefetch=3,
            grid=(chips,),
            in_specs=[
                pl.BlockSpec((rows, TILE_SIDE), lambda i, info, head_of, *_: (0, 2 * head_of[i]))
            ],
            out_specs=pl.BlockSpec((1, rows, TILE_SIDE), lambda i, *_: (i, 0, 0)),
        ),
        out_shape=jax.ShapeDtypeStruct((chips, rows, TILE_SIDE), BF),
        compiler_params=PARAMS,
        cost_estimate=cost(2 * chips * rows * TILE_SIDE, 4 * chips * rows * TILE_SIDE),
        name="prepare_keys",
    )(my_rank.reshape(1), key_value_of_block, kv_scale, kv_codes)


def project_kernel(info, normed, own, other, first, sent, kept, weight):
    step = pl.program_id(0)
    rows = own.shape[1]
    core = info[0]
    weight[pl.ds(pl.multiple_of(core * rows, GROUP_ROWS), rows), :] = own[0]
    weight[pl.ds(pl.multiple_of((1 - core) * rows, GROUP_ROWS), rows), :] = other[0]
    product = jnp.dot(normed[...], weight[...], preferred_element_type=F32)
    first[0] = product[: first.shape[1]].astype(first.dtype)
    second = product[first.shape[1] :]

    @pl.when(step < 2)
    def _():
        sent[0] = second.astype(BF)

    @pl.when(step >= 2)
    def _():
        kept[0] = second


def project(core, normed, own, other, first_type):
    count, width = normed.shape
    blocks, rows, columns = other.shape
    first, second = PART_ROWS
    return pl.pallas_call(
        project_kernel,
        grid=(blocks,),
        in_specs=[
            SMEM,
            pl.BlockSpec((count, width), lambda k: (0, 0)),
            pl.BlockSpec((1, rows, columns), lambda k: (k, 0, 0)),
            pl.BlockSpec((1, rows, columns), lambda k: (k, 0, 0)),
        ],
        out_specs=[
            pl.BlockSpec((1, first, columns), lambda k: (k, 0, 0)),
            pl.BlockSpec((1, second, columns), lambda k: (jnp.minimum(k, 1), 0, 0)),
            pl.BlockSpec((1, second, columns), lambda k: (jnp.maximum(k - 2, 0), 0, 0)),
        ],
        scratch_shapes=[pltpu.VMEM((width, columns), BF)],
        out_shape=[
            jax.ShapeDtypeStruct((blocks, first, columns), first_type),
            jax.ShapeDtypeStruct((2, second, columns), BF),
            jax.ShapeDtypeStruct((2, second, columns), F32),
        ],
        compiler_params=PARAMS,
        cost_estimate=cost(
            2 * blocks * count * width * columns, 2 * blocks * columns * (width + count)
        ),
        name="project",
    )(core.reshape(1), normed, own, other)


def project_first_kernel(info, normed, own, other, out, weight):
    rows = own.shape[1]
    core = info[0]
    weight[pl.ds(pl.multiple_of(core * rows, GROUP_ROWS), rows), :] = own[0]
    weight[pl.ds(pl.multiple_of((1 - core) * rows, GROUP_ROWS), rows), :] = other[0]
    product = jnp.dot(normed[...], weight[...], preferred_element_type=F32)
    out[0] = product.astype(out.dtype)


def project_part(core, normed, part, own, other, first_block, blocks, out_type):
    width = normed.shape[1]
    _, rows, columns = other.shape
    count = PART_ROWS[part]
    weight = pl.BlockSpec((1, rows, columns), lambda k: (first_block + k, 0, 0))
    return pl.pallas_call(
        project_first_kernel,
        grid=(blocks,),
        in_specs=[SMEM, pl.BlockSpec((count, width), lambda k: (part, 0)), weight, weight],
        out_specs=pl.BlockSpec((1, count, columns), lambda k: (k, 0, 0)),
        scratch_shapes=[pltpu.VMEM((width, columns), BF)],
        out_shape=jax.ShapeDtypeStruct((blocks, count, columns), out_type),
        compiler_params=PARAMS,
        cost_estimate=cost(
            2 * blocks * count * width * columns, 2 * blocks * columns * (width + count)
        ),
        name="project_part",
    )(core.reshape(1), normed, own, other)


def join_kernel(own, got, kept, near, far, middle):
    for block, out in enumerate((near, far, kept, middle)):
        out[...] = (own[block] + got[block].astype(F32)).astype(out.dtype)


def join_partials(own, got):
    _, rows, columns = got.shape
    vmem = pl.BlockSpec(memory_space=pltpu.VMEM)
    sent = jax.ShapeDtypeStruct((rows, columns), BF)
    kept, near, far, middle = pl.pallas_call(
        join_kernel,
        in_specs=[vmem, vmem],
        out_shape=[jax.ShapeDtypeStruct((rows, columns), F32), sent, sent, sent],
        compiler_params=PARAMS,
        cost_estimate=cost(8 * rows * columns, 32 * rows * columns),
        name="join_partials",
    )(own, got)
    return kept, near, middle, far


def pair_kernel(away, home, got_away, got_home, sent, kept):
    sent[...] = (away[...] + got_away[...].astype(F32)).astype(BF)
    kept[...] = home[...] + got_home[...].astype(F32)


def join_pair(away, home, got_away, got_home):
    vmem = pl.BlockSpec(memory_space=pltpu.VMEM)
    return pl.pallas_call(
        pair_kernel,
        in_specs=[vmem] * 4,
        out_shape=[jax.ShapeDtypeStruct(away.shape, BF), jax.ShapeDtypeStruct(home.shape, F32)],
        compiler_params=PARAMS,
        cost_estimate=cost(2 * home.size, 16 * home.size),
        name="join_pair",
    )(away, home, got_away, got_home)


def last_kernel(kept, got, own, sent):
    own[...] = kept[0] + got[0].astype(F32)
    sent[...] = (kept[1] + got[1].astype(F32)).astype(BF)


def join_last(kept, got):
    _, rows, columns = kept.shape
    vmem = pl.BlockSpec(memory_space=pltpu.VMEM)
    return pl.pallas_call(
        last_kernel,
        in_specs=[vmem, vmem],
        out_shape=[
            jax.ShapeDtypeStruct((rows, columns), F32),
            jax.ShapeDtypeStruct((rows, columns), BF),
        ],
        compiler_params=PARAMS,
        cost_estimate=cost(2 * kept.size, 8 * kept.size),
        name="join_last",
    )(kept, got)


def turn(values, cosine, sine):
    return values * cosine + pltpu.roll(values, HEAD_SIZE // 2, 1) * sine


def normalise(values, gain):
    mean_square = jnp.mean(values * values, axis=-1, keepdims=True)
    return values * lax.rsqrt(mean_square + eps_norm) * gain


def heads_kernel(start, info, *refs):
    *parts, q_gain, k_gain, cosine, sine, q_out, kv_out = refs
    total = parts[0][...]
    for part in parts[1:]:
        total = total + part[...].astype(F32)
    heads, count, _ = q_out.shape
    cos, sin = cosine[start : start + count, :], sine[start : start + count, :]
    last = total[:, heads * HEAD_SIZE :]

    @pl.when(info[0] == 0)
    def _():
        kv_out[...] = turn(normalise(last, k_gain[...]), cos, sin).astype(BF)

    @pl.when(info[0] == 1)
    def _():
        kv_out[...] = last.astype(BF)

    for head in range(heads):
        values = total[:, head * HEAD_SIZE : (head + 1) * HEAD_SIZE]
        q_out[head] = turn(normalise(values, q_gain[...]), cos, sin).astype(BF)


def make_heads(core, parts, start, q_gain, k_gain, cosine, sine):
    count, columns = parts[0].shape
    heads = columns // HEAD_SIZE - 1
    vmem = pl.BlockSpec(memory_space=pltpu.VMEM)
    return pl.pallas_call(
        functools.partial(heads_kernel, start),
        out_shape=(
            jax.ShapeDtypeStruct((heads, count, HEAD_SIZE), BF),
            jax.ShapeDtypeStruct((count, HEAD_SIZE), BF),
        ),
        in_specs=[SMEM] + [vmem] * (len(parts) + 4),
        compiler_params=PARAMS,
        cost_estimate=cost(20 * count * columns, 14 * count * columns),
        name="make_heads",
    )(core.reshape(1), *parts, q_gain.reshape(1, -1), k_gain.reshape(1, -1), cosine, sine)


def attend_kernel(length, start, share, info, queries, *refs):
    *rows, kept, sent = refs
    parts = len(rows) // 2
    own = jnp.concatenate([ref[...] for ref in rows[:parts]], axis=0)
    other = jnp.concatenate([ref[...] for ref in rows[parts:]], axis=0)
    first = info[0] == 0
    keys, values = jnp.where(first, own, other), jnp.where(first, other, own)
    count = queries.shape[1]
    here = lax.broadcasted_iota(jnp.int32, (count, keys.shape[0]), 0) + start
    there = lax.broadcasted_iota(jnp.int32, (count, keys.shape[0]), 1)
    allowed = here >= there
    for prompt in range(1, (start + count + length - 1) // length):
        allowed = allowed & ((here < prompt * length) | (there >= prompt * length))
    for head in range(queries.shape[0]):
        scores = lax.dot_general(
            queries[head], keys, (((1,), (1,)), ((), ())), preferred_element_type=F32
        ) * HEAD_SIZE ** (-0.5)
        weights = jnp.where(allowed, jnp.exp(scores), 0.0)
        probabilities = (weights / jnp.sum(weights, axis=-1, keepdims=True)).astype(BF)
        result = jnp.dot(probabilities, values, preferred_element_type=F32)
        shares = [result[at : at + share] for at in range(0, count, share)]
        even = jnp.concatenate(shares[0::2], axis=0)
        odd = jnp.concatenate(shares[1::2], axis=0)
        span = slice(head * HEAD_SIZE, (head + 1) * HEAD_SIZE)
        kept[:, span] = jnp.where(first, even, odd).astype(BF)
        sent[:, span] = jnp.where(first, odd, even).astype(BF)


def attend_heads(core, queries, start, own, other, share):
    heads, count, width = queries.shape
    vmem = pl.BlockSpec(memory_space=pltpu.VMEM)
    return pl.pallas_call(
        functools.partial(attend_kernel, LEN, start, share),
        out_shape=[jax.ShapeDtypeStruct((count // 2, heads * width), BF)] * 2,
        in_specs=[SMEM] + [vmem] * (1 + len(own) + len(other)),
        compiler_params=PARAMS,
        cost_estimate=cost(4 * heads * count * (start + count) * width, 4 * heads * count * width),
        name="attend",
    )(core.reshape(1), queries, *own, *other)


def out_kernel(blocks, has_start, last, width, info, scales, *refs):
    attended = refs[:blocks]
    codes = refs[blocks : blocks + 2]
    out, held, arrived = refs[-3:]
    core, my_rank = info[0], info[1]
    columns = held.shape[1]
    tiles = width // TILE_SIDE
    pieces = [(block, side) for block in range(blocks) for side in range(2)]
    copies = []
    for number, (block, side) in enumerate(pieces):
        start = pl.multiple_of(info[2 + block] * (2 * width), 2 * width)
        copy = pltpu.make_async_copy(
            codes[side].at[:, pl.ds(start, 2 * width)], held.at[number], arrived.at[number]
        )
        copy.start()
        copies.append(copy)
    totals = [None, None]
    for number, (block, side) in enumerate(pieces):
        copies[number].wait()
        for half in range(2):
            rows = attended[block][:, half * width : (half + 1) * width]
            first_tile = (2 * info[2 + block] + (core ^ half)) * tiles
            weight = []
            for group in range(columns // GROUP_ROWS):
                column = ((my_rank ^ side) * columns + group * GROUP_ROWS) // TILE_SIDE
                span = slice(group * GROUP_ROWS, (group + 1) * GROUP_ROWS)
                parts = []
                for tile in range(tiles):
                    lane = pl.multiple_of((core ^ half) * width + tile * TILE_SIDE, TILE_SIDE)
                    code = held[number, span, pl.ds(lane, TILE_SIDE)].astype(F32)
                    parts.append((code * scales[first_tile + tile, column]).astype(BF))
                weight.append(jnp.concatenate(parts, axis=1))
            term = lax.dot_general(
                jnp.concatenate(weight, axis=0),
                rows,
                (((1,), (1,)), ((), ())),
                preferred_element_type=F32,
            )
            totals[side] = term if totals[side] is None else totals[side] + term
    if has_start:
        start = refs[blocks + 2]
        totals = [total + start[side] for side, total in enumerate(totals)]
    if last:
        first = core == 0
        both = jnp.concatenate(
            [jnp.where(first, totals[0], totals[1]), jnp.where(first, totals[1], totals[0])], axis=0
        )
        out[...] = both.T.astype(out.dtype)
    else:
        for side in range(2):
            out[side] = totals[side]


def out_project(core, my_rank, attended, chips_of, codes, scales, start, last):
    count, both = attended[0].shape
    blocks = len(attended)
    columns = codes[0].shape[0]
    vmem = pl.BlockSpec(memory_space=pltpu.VMEM)
    extra = [] if start is None else [start]
    shape = (count, 2 * columns) if last else (2, columns, count)
    return pl.pallas_call(
        functools.partial(out_kernel, blocks, bool(extra), last, both // 2),
        out_shape=jax.ShapeDtypeStruct(shape, BF if last else F32),
        in_specs=[SMEM, SMEM]
        + [vmem] * blocks
        + [pl.BlockSpec(memory_space=pl.ANY)] * 2
        + [vmem] * len(extra),
        scratch_shapes=[
            pltpu.VMEM((2 * blocks, columns, both), BF),
            pltpu.SemaphoreType.DMA((2 * blocks,)),
        ],
        compiler_params=PARAMS,
        cost_estimate=cost(4 * blocks * count * both * columns, 4 * blocks * both * columns),
        name="out_project",
    )(jnp.concatenate([jnp.stack([core, my_rank]), chips_of]), scales, *attended, *codes, *extra)


def rotation_tables(count):
    half_width = HEAD_SIZE // 2
    positions = (jnp.arange(count) % LEN).astype(F32)
    frequency = theta_base ** (-jnp.arange(half_width, dtype=F32) * 2.0 / HEAD_SIZE)
    angles = positions[:, None] * frequency[None, :]
    cosine, sine = jnp.cos(angles), jnp.sin(angles)
    return jnp.concatenate([cosine, cosine], axis=1), jnp.concatenate([-sine, sine], axis=1)


Z_COUNT = 4
PART_ROWS = (192, 192)
TIE_FIRST = True
TIE_SECOND = False
TIE_AWAY = True


def after(values, *earlier):
    return lax.optimization_barrier((values, *earlier))[0]


def chip_plan(
    token_ids,
    key_value_of_block,
    vocab_table,
    in_gain,
    q_gain,
    k_gain,
    wq_codes,
    wq_scale,
    key_value_codes,
    key_value_scale,
    wo_codes,
    wo_scale,
):
    ranks = lax.axis_size("fsdp")
    chips = ranks // 2
    y_count = chips // Z_COUNT
    my_rank = lax.axis_index("fsdp").astype(jnp.int32)
    core, chip = my_rank % 2, my_rank // 2
    count = token_ids.shape[0]
    vocab_rows = vocab_table.shape[0]
    same_core = [[2 * chip + side for chip in range(chips)] for side in range(2)]

    def swap(values, bits):
        return lax.ppermute(values, "fsdp", [(i, i ^ bits) for i in range(ranks)])

    def swap_groups(values):
        return lax.ppermute(values, "groups", [(0, 1), (1, 0)])

    def to_chips(values):
        return lax.all_to_all(
            values, "fsdp", split_axis=0, concat_axis=0, tiled=True, axis_index_groups=same_core
        )

    def exchange(sent):
        own = to_chips(sent)
        return own, swap(own, 1)

    owners, rows, most = find_slots(token_ids, my_rank, ranks, vocab_rows)
    sent = pick_rows(rows, jnp.int32(0), in_gain, vocab_table, chips)
    most = jnp.maximum(most, swap_groups(after(most, sent)))[0, 0]

    sent_keys = prepare_keys(
        after(my_rank, sent), key_value_of_block, key_value_codes, key_value_scale
    )
    half = sent_keys.shape[1] // 2
    group = lax.axis_index("groups")
    my_half = lax.dynamic_slice_in_dim(sent_keys, group * half, half, 1)
    my_z = chip // y_count

    def keys_for(z):
        return lax.dynamic_slice_in_dim(my_half, z * y_count, y_count, 0)

    by_z = [keys_for(my_z)] + [swap(keys_for(my_z ^ k), 2 * y_count * k) for k in range(1, Z_COUNT)]

    near = jnp.array([1, 3, 0, 2], jnp.int32) * y_count

    away_own, away_other, home_own, home_other = prepare_weights(
        core,
        my_rank,
        after(chip, sent) ^ jnp.concatenate([near ^ 1, near]),
        wq_codes,
        wq_scale,
        key_value_codes,
        key_value_scale,
    )
    own = to_chips(sent)
    own, away_other, home_other, *by_z = lax.optimization_barrier(
        (own, away_other, home_other, *by_z)
    )
    other = swap(own, 1)
    normed = place_rows(owners, jnp.int32(0), core, own, other)

    def one_more(state):
        base, total = state
        more = exchange(pick_rows(rows, base, in_gain, vocab_table, chips))
        return base + SLOTS, total + place_rows(owners, base, core, *more)

    _, normed = lax.while_loop(
        lambda state: state[0].astype(F32) < most, one_more, (jnp.int32(SLOTS), normed)
    )

    away_other = swap(away_other, 1)
    home_other = swap(home_other, 1)
    away = project_part(core, normed, 0, away_own, away_other, 0, Z_COUNT, BF)
    got = swap(away, 2)
    away_sent = project_part(after(core, away), normed, 1, away_own, away_other, 0, 2, BF)
    got_away = swap(away_sent, 2 * y_count)
    away_kept = project_part(after(core, away_sent), normed, 1, away_own, away_other, 2, 2, F32)
    home, home_sent, home_kept = project(
        after(core, away_sent), normed, home_own, home_other, F32
    )
    got_home = swap(home_sent, 2 * y_count)
    if TIE_AWAY:
        got, got_away = lax.optimization_barrier((got, got_away))

    cosine, sine = rotation_tables(count)
    heads_width = wq_codes.shape[1] // ranks
    by_z = jnp.stack(by_z)
    my_y = chip % y_count
    here = lax.dynamic_index_in_dim(by_z, my_y, 1, keepdims=False)
    there = swap(lax.dynamic_index_in_dim(by_z, 1 - my_y, 1, keepdims=False), 2)
    wo_rows = wo_codes.T
    out_codes = [wo_rows, swap(wo_rows, 1)]
    own_kv, other_kv, held = [], [], []
    share = count // ranks

    def attend_part(start, sums):
        queries, kv = make_heads(core, sums, start, q_gain, k_gain, cosine, sine)
        own_kv.append(kv)
        other_kv.append(swap(kv, 1))
        kept, sent_rows = attend_heads(core, queries, start, own_kv, other_kv, share)
        held.append(jnp.concatenate([kept, swap(sent_rows, 1)], axis=1))

    kept, *sums = join_partials(home, got)
    got_away, got_home = lax.optimization_barrier((got_away, got_home, *sums))[:2]
    pair_sent, pair_kept = join_pair(away_kept, home_kept, got_away, got_home)
    sums = [swap(value, 2 * y_count * (k + 1)) for k, value in enumerate(sums)]
    pair_got = swap(pair_sent, 2)
    pair_got, sums[0], sums[2] = lax.optimization_barrier((pair_got, sums[0], sums[2]))
    attend_part(0, [kept, *sums])
    kept, last_sent = join_last(pair_kept, pair_got)
    last_got = swap(last_sent, 4 * y_count)
    kept, there = lax.optimization_barrier((kept, there))
    attend_part(PART_ROWS[0], [kept, last_got])

    def add_blocks(total, blocks, numbers, last=False):
        chips_of = chip ^ jnp.array(numbers, jnp.int32)
        return out_project(
            core, my_rank, blocks, chips_of, out_codes, wo_scale, total, last
        )

    own_keys = jnp.stack([here, there], axis=1).reshape(chips, half, HEAD_SIZE)

    def finish_keys(far_keys):
        return collect_keys(
            jnp.stack([core, group, chip]),
            [own_keys, far_keys, swap(own_keys, 1), swap(far_keys, 1)],
        )

    total, synced = gather_project(
        jnp.concatenate(held, axis=0), add_blocks, y_count, swap_groups(own_keys), finish_keys
    )
    columns = to_chips(total.reshape(chips, share, -1))
    attn_out = jnp.transpose(columns, (1, 0, 2)).reshape(share, -1)
    return attn_out, synced


def collect_kernel(info, own, far, other, other_far, out):
    core, group = info[0], info[1]
    out[0, core, group] = own[0]
    out[0, core, 1 - group] = far[0]
    out[0, 1 - core, group] = other[0]
    out[0, 1 - core, 1 - group] = other_far[0]


def collect_keys(info, parts):
    chips, half, width = parts[0].shape
    part = pl.BlockSpec((1, half, width), lambda i, info: (i ^ info[2], 0, 0))
    out = pl.pallas_call(
        collect_kernel,
        grid_spec=pltpu.PrefetchScalarGridSpec(
            num_scalar_prefetch=1,
            grid=(chips,),
            in_specs=[part] * 4,
            out_specs=pl.BlockSpec((1, 2, 2, half, width), lambda i, info: (i, 0, 0, 0, 0)),
        ),
        out_shape=jax.ShapeDtypeStruct((chips, 2, 2, half, width), BF),
        compiler_params=PARAMS,
        cost_estimate=cost(0, 16 * chips * half * width),
        name="collect_keys",
    )(info, *parts)
    return out.reshape(1, -1, width)


def hop(values, pairs, along, ranks):
    moves = [(a * along + rest, b * along + rest) for a, b in pairs for rest in range(along)]
    return lax.ppermute(values, "fsdp", moves)


NEXT = [(0, 1), (1, 0), (2, 3), (3, 2)]
MIDDLE = [(1, 2), (2, 1)]
OUTWARD = [(1, 0), (2, 3)]


def gather_project(block, add_blocks, y_count, beside, finish):
    along = 2 * y_count
    ranks = Z_COUNT * along
    together = lax.optimization_barrier

    def swap_y(values):
        return lax.ppermute(values, "fsdp", [(i, i ^ 2) for i in range(ranks)])

    z_index = lax.axis_index("fsdp") // along
    at_end = (z_index == 0) | (z_index == Z_COUNT - 1)
    across, one, inner = together(
        (swap_y(block), hop(block, NEXT, along, ranks), hop(block, MIDDLE, along, ranks))
    )
    total = add_blocks(None, [block, across, one], (0, 1, 2))
    two_end, two_inner, one_across = (
        hop(inner, OUTWARD, along, ranks),
        hop(one, MIDDLE, along, ranks),
        swap_y(one),
    )
    if TIE_FIRST:
        two_end, two_inner, one_across, total, beside = together(
            (two_end, two_inner, one_across, total, beside)
        )
    else:
        two_end, two_inner, one_across, beside = together(
            (two_end, two_inner, one_across, beside)
        )
    finished = finish(beside)
    two = jnp.where(at_end, two_end, two_inner)
    three_end, two_across = hop(two, OUTWARD, along, ranks), swap_y(two)
    if TIE_SECOND:
        total = add_blocks(total, [one_across, two], (3, 4))
        three_end, two_across, total, finished = together(
            (three_end, two_across, total, finished)
        )
        rest, numbers = [two_across], (5, 6)
    else:
        three_end, two_across, finished = together((three_end, two_across, finished))
        rest, numbers = [one_across, two, two_across], (3, 4, 5, 6)
    three = jnp.where(at_end, three_end, inner)
    three_across = swap_y(three)
    total = add_blocks(total, [*rest, three], numbers)
    return add_blocks(total, [three_across], (7,), True), finished


def solution(mesh):
    sizes = dict(mesh.shape)
    small = sizes["fsdp"] == 2 * KEY_VALUE_HEADS and sizes["groups"] == 2
    return jax.shard_map(
        chip_plan if small else general_plan,
        mesh=mesh,
        in_specs=(
            P("groups"),
            P(),
            P("fsdp", None),
            P(),
            P(),
            P(),
            P("fsdp", None),
            P(),
            P("fsdp", None),
            P(),
            P(None, "fsdp"),
            P(),
        ),
        out_specs=(P(("groups", "fsdp"), None), P(("groups", "fsdp"), None, None)),
        check_vma=False,
    )
```
